32 devices in a mesh: tm: 4 (over z), height: 2 (over x), width: 4 (over y, core).
Axes of the slice: x: 2, y: 2, z: 4, core: 2. Of those that a mesh axis runs over, the one named last changes fastest.
Arguments:
- video_in: bfloat16 [16, 16, 6144], P('tm', 'height', 'width'), may hold values from -24 to 24
- gain_first: float32 [96], replicated, may hold values from 0.5 to 2
- gain_second: float32 [192], replicated, may hold values from 0.5 to 2
- conv_first: bfloat16 [3, 3, 3, 96, 192], replicated, may hold values from -0.125 to 0.125
- conv_second: bfloat16 [3, 3, 3, 192, 192], replicated, may hold values from -0.078125 to 0.078125
- shortcut: bfloat16 [96, 192], replicated, may hold values from -0.625 to 0.625
- downscale_weight: bfloat16 [3, 3, 192, 192], replicated, may hold values from -0.15625 to 0.15625
Outputs:
- encoded: bfloat16 [16, 8, 6144], P('tm', 'height', 'width')
The draws below stay inside these ranges and needn't reach their ends.
All inputs are finite; a program needn't handle non-finite values.
Results may differ from the reference program's by a relative error of at most 0.0054.
Values may be sent and summed in bfloat16 or wider, within the bound.
No kernel may reach another device: no remote copies, remote signals or barrier semaphores. Data moves between devices by JAX's collectives and lax.ppermute only.
A program may use at most 64 MiB of HBM per device.

```python
import math
import jax
import jax.numpy as jnp
from jax import lax

C1 = 96
C2 = 192
FRAMES = 16
IMG_ROWS = 16
IMG_COLS = 64


def draw_video_in(key, part):
    key_base, key_chan, key_pos = jax.random.split(key, 3)
    chan_scale = jnp.exp(jax.random.uniform(key_chan, (C1,), jnp.float32, jnp.log(0.3), jnp.log(3.0)))
    pos_scale = jnp.exp(jax.random.uniform(key_pos, (FRAMES, IMG_ROWS, IMG_COLS, 1), jnp.float32, jnp.log(0.5), jnp.log(2.0)))
    base = jnp.clip(jax.random.normal(key_base, (FRAMES, IMG_ROWS, IMG_COLS, C1), jnp.float32), -4.0, 4.0)
    feature_values = base * chan_scale * pos_scale
    return feature_values.reshape(FRAMES, IMG_ROWS, IMG_COLS * C1).astype(jnp.bfloat16)


def scatter_about(own_key, shape, deviation, limit, kind=jnp.bfloat16):
    drawn = jax.random.normal(own_key, shape, jnp.float32) * deviation
    return jnp.minimum(jnp.maximum(drawn, -limit), limit).astype(kind)


def setup_inputs(seed: int = 0) -> dict:
    splits = jax.random.split(jax.random.key(seed), 8)
    video_in = draw_video_in(jax.random.fold_in(splits[7], 71), 0)
    gain_first = jnp.clip(jnp.exp(jax.random.uniform(splits[1], (C1,), jnp.float32, math.log(0.5), math.log(2.0))), 0.5, 2.0)
    gain_second = jnp.clip(jnp.exp(jax.random.uniform(splits[2], (C2,), jnp.float32, math.log(0.5), math.log(2.0))), 0.5, 2.0)
    conv_first = scatter_about(splits[3], (3, 3, 3, C1, C2), (27 * C1) ** -0.5, 0.125)
    conv_second = scatter_about(splits[4], (3, 3, 3, C2, C2), (27 * C2) ** -0.5, 0.078125)
    shortcut = scatter_about(splits[5], (C1, C2), C1 ** -0.5, 0.625)
    downscale_weight = scatter_about(splits[6], (3, 3, C2, C2), (9 * C2) ** -0.5, 0.15625)
    return dict(video_in=video_in, gain_first=gain_first, gain_second=gain_second, conv_first=conv_first, conv_second=conv_second, shortcut=shortcut, downscale_weight=downscale_weight)


epsilon = 1e-06

def activate(feature_values, gain):
    feature_values = feature_values.astype(jnp.float32)
    meansq = lax.optimization_barrier(jnp.mean(feature_values * feature_values, axis=-1, keepdims=True))
    normed = feature_values * lax.rsqrt(meansq + epsilon) * gain
    return jax.nn.silu(normed).astype(jnp.bfloat16)

def convolve(border_filled, filter_weight):
    frames = border_filled.shape[0] - 2
    rows = border_filled.shape[1] - 2
    cols = border_filled.shape[2] - 2
    c_in = border_filled.shape[3]
    c_out = filter_weight.shape[4]
    total = jnp.zeros((frames * rows * cols, c_out), jnp.float32)
    for depth_tap in range(3):
        for row_tap in range(3):
            window_slab = border_filled[depth_tap:depth_tap + frames, row_tap:row_tap + rows]
            stacked = jnp.concatenate([window_slab[:, :, col_tap:col_tap + cols] for col_tap in range(3)], axis=-1)
            total = total + jnp.dot(stacked.reshape(-1, 3 * c_in), filter_weight[depth_tap, row_tap].reshape(3 * c_in, c_out), preferred_element_type=jnp.float32)
    return total.reshape(frames, rows, cols, c_out)

def halve_spatial(border_filled, filter_weight):
    frames = border_filled.shape[0]
    out_rows = (border_filled.shape[1] - 1) // 2
    out_cols = (border_filled.shape[2] - 1) // 2
    chans = border_filled.shape[3]
    total = jnp.zeros((frames * out_rows * out_cols, filter_weight.shape[3]), jnp.float32)
    for row_tap in range(3):
        stacked = jnp.concatenate([border_filled[:, row_tap:row_tap + 2 * out_rows:2, col_tap:col_tap + 2 * out_cols:2] for col_tap in range(3)], axis=-1)
        total = total + jnp.dot(stacked.reshape(-1, 3 * chans), filter_weight[row_tap].reshape(3 * chans, filter_weight.shape[3]), preferred_element_type=jnp.float32)
    return total.reshape(frames, out_rows, out_cols, filter_weight.shape[3])

def reference(video_in, gain_first, gain_second, conv_first, conv_second, shortcut, downscale_weight):
    field = video_in.reshape(FRAMES, IMG_ROWS, IMG_COLS, C1)
    pads = ((2, 0), (1, 1), (1, 1), (0, 0))
    first = jnp.pad(activate(field, gain_first), pads)
    hidden = convolve(first, conv_first)
    second = jnp.pad(activate(hidden, gain_second), pads)
    branch = convolve(second, conv_second)
    skip_term = jnp.dot(field.reshape(-1, C1), shortcut, preferred_element_type=jnp.float32).reshape(FRAMES, IMG_ROWS, IMG_COLS, C2)
    merged = (branch + skip_term).astype(jnp.bfloat16)
    border_filled = jnp.pad(merged, ((0, 0), (0, 1), (0, 1), (0, 0)))
    block_output = halve_spatial(border_filled, downscale_weight)
    return block_output.astype(jnp.bfloat16).reshape(FRAMES, IMG_ROWS // 2, IMG_COLS // 2 * C2)
```

```python
import functools
import jax
import jax.numpy as jnp
from jax import lax
from jax.experimental import pallas as pl
from jax.experimental.pallas import tpu as pltpu
from jax.sharding import PartitionSpec as P

epsilon = 1e-06
AXES = ("tm", "height", "width")
LANES = 128
LOW, HIGH = 2, 3
EDGE = 4


def swap_pairs(axis, parity):
    sizes = [lax.axis_size(name) for name in AXES]
    place = AXES.index(axis)
    count = sizes[place]
    pairs = []
    for t in range(sizes[0]):
        for h in range(sizes[1]):
            for w in range(sizes[2]):
                source = [t, h, w]
                target = [t, h, w]
                other = source[place] + (1 if source[place] % 2 == parity else -1)
                if 0 <= other < count:
                    target[place] = other
                elif axis == "width":
                    target[place] = other % count
                else:
                    target[2] = w ^ 1
                pairs.append(
                    tuple((p[0] * sizes[1] + p[1]) * sizes[2] + p[2] for p in (source, target))
                )
    return pairs


def exchange(axis, to_next, to_prev):
    count = lax.axis_size(axis)
    index = lax.axis_index(axis)
    even = index % 2 == 0
    zero = jnp.zeros_like(to_next)
    with_pair = lax.ppermute(jnp.where(even, to_next, to_prev), AXES, swap_pairs(axis, 0))
    if count > 2:
        across = lax.ppermute(jnp.where(even, to_prev, to_next), AXES, swap_pairs(axis, 1))
    else:
        across = zero
    from_prev = jnp.where(even, jnp.where(index > 0, across, zero), with_pair)
    from_next = jnp.where(even, with_pair, jnp.where(index < count - 1, across, zero))
    return from_prev, from_next


def kernel(
    dims, mid_ref, left_ref, right_ref, gain1, gain2, shortcut, conv1, conv2, down,
    out_ref, first, raw, stack1, sec_a, sec_b, stack2, mer_a, mer_b, stack3, result,
    w1, w2m, w2r, wdm, wdr, wsc, g1, g2, sems,
):
    frames, rows, cols, c1, c2 = dims
    R = rows + LOW + HIGH
    in_cols, hid_cols, mer_cols = cols + LOW + HIGH, cols + 3, cols + 1
    M1, M2 = stack1.shape[1], stack2.shape[1]
    rest = c2 - LANES
    bf, f32 = jnp.bfloat16, jnp.float32

    copies1, copies2, copies3 = [], [], []
    copies0 = [
        pltpu.make_async_copy(gain1, g1, sems.at[15]),
        pltpu.make_async_copy(gain2, g2, sems.at[16]),
        pltpu.make_async_copy(shortcut, wsc.at[pl.ds(0, c1)], sems.at[17]),
    ]
    for dc in range(3):
        copies1.append(pltpu.make_async_copy(conv1.at[:, :, dc], w1.at[dc, :, :, pl.ds(0, c1)], sems.at[dc]))
        copies2.append(
            pltpu.make_async_copy(conv2.at[:, :, dc, pl.ds(0, LANES)], w2m.at[dc], sems.at[3 + dc])
        )
        copies2.append(
            pltpu.make_async_copy(
                conv2.at[:, :, dc, pl.ds(LANES, rest)], w2r.at[dc, :, pl.ds(0, 3)], sems.at[6 + dc]
            )
        )
        copies3.append(
            pltpu.make_async_copy(down.at[:, dc, pl.ds(0, LANES)], wdm.at[dc], sems.at[9 + dc])
        )
        copies3.append(
            pltpu.make_async_copy(
                down.at[:, dc, pl.ds(LANES, rest)], wdr.at[dc, pl.ds(0, 3)], sems.at[12 + dc]
            )
        )
    for copy in copies0 + copies1 + copies2 + copies3:
        copy.start()
    w1[:, :, :, c1:, :] = jnp.zeros((3, 3, 3, LANES - c1, c2), bf)
    w2r[:, :, 3] = jnp.zeros((3, 3, rest, c2), bf)
    wdr[:, 3] = jnp.zeros((3, rest, c2), bf)
    wsc[c1:] = jnp.zeros((LANES - c1, c2), bf)
    sec_b[...] = jnp.zeros_like(sec_b)
    mer_a[...] = jnp.zeros_like(mer_a)
    mer_b[...] = jnp.zeros_like(mer_b)

    slots = EDGE * LANES
    source = lax.broadcasted_iota(jnp.int32, (EDGE * c1, slots), 0)
    target = lax.broadcasted_iota(jnp.int32, (EDGE * c1, slots), 1)
    slot, lane = target // LANES, target % LANES
    spread = jnp.where((source == slot * c1 + lane) & (lane < c1), 1.0, 0.0).astype(bf)
    for copy in copies0:
        copy.wait()
    gain1 = jnp.concatenate([g1[...], jnp.zeros((1, LANES - c1), f32)], axis=-1)
    pieces = [(left_ref, 0, EDGE - LOW, EDGE, 0)]
    for group in range(cols // EDGE):
        pieces.append((mid_ref, group * EDGE * c1, 0, EDGE, LOW + group * EDGE))
    pieces.append((right_ref, 0, 0, HIGH, LOW + cols))
    P16 = mid_ref.shape[1]
    for ref, lane, lo, hi, c in pieces:
        x = ref[:, :, lane : lane + EDGE * c1].reshape(2 * frames * P16, EDGE * c1)
        xu = jnp.dot(x, spread, preferred_element_type=f32)
        for k in range(lo, hi):
            v = xu[:, k * LANES : (k + 1) * LANES]
            ms = jnp.sum(v * v, axis=-1, keepdims=True) * (1.0 / c1)
            u = v * lax.rsqrt(ms + epsilon) * gain1
            u = u / (1.0 + jnp.exp(-u))
            for f in range(2 * frames):
                first[c, f * R : f * R + P16, :] = u[f * P16 : (f + 1) * P16]
                if f >= frames and LOW <= c < LOW + mer_cols:
                    g = f - frames
                    raw[c - LOW, g * R : g * R + P16, :] = v[f * P16 : (f + 1) * P16]
            c += 1

    def build1(c, carry):
        for k in range(9):
            off = (k // 3) * R + k % 3
            stack1[c, :, k * LANES : (k + 1) * LANES] = first[c, off : off + M1, :].astype(bf)
        return carry

    lax.fori_loop(0, in_cols, build1, 0)

    t, h, w = [lax.axis_index(name) for name in AXES]
    first_t, top, leftmost = [jnp.where(i == 0, 1, 0) for i in (t, h, w)]
    bottom = jnp.where(h == lax.axis_size("height") - 1, 1, 0)
    rightmost = jnp.where(w == lax.axis_size("width") - 1, 1, 0)
    p = lax.broadcasted_iota(jnp.int32, (M1, 1), 0)
    dead = (p < 2 * R) & (first_t == 1)
    for f in range(frames + 2):
        dead |= (p == f * R) & (top == 1)
        dead |= ((p == f * R + rows + 1) | (p == f * R + rows + 2)) & (bottom == 1)
    live1 = jnp.where(dead, 0.0, 1.0).astype(f32)
    q = lax.broadcasted_iota(jnp.int32, (M2, 1), 0)
    dead = q < 0
    for f in range(frames):
        dead |= (q == f * R + rows) & (bottom == 1)
    live2 = jnp.where(dead, 0.0, 1.0).astype(f32)
    keep_left = jnp.where(leftmost == 1, 0.0, 1.0).astype(f32)
    keep_right = jnp.where(rightmost == 1, 0.0, 1.0).astype(f32)

    for copy in copies1:
        copy.wait()
    gain2 = g2[...]
    step1 = 5
    for start in range(0, hid_cols, step1):
        n = min(step1, hid_cols - start)
        acc = None
        for dc in range(3):
            part = jnp.dot(
                stack1[start + dc : start + dc + n].reshape(n * M1, 9 * LANES),
                w1[dc].reshape(9 * LANES, c2),
                preferred_element_type=f32,
            )
            acc = part if acc is None else acc + part
        for i in range(n):
            c = start + i
            hid = acc[i * M1 : (i + 1) * M1]
            ms = jnp.sum(hid * hid, axis=-1, keepdims=True) * (1.0 / c2)
            u = hid * lax.rsqrt(ms + epsilon) * gain2
            u = u / (1.0 + jnp.exp(-u)) * live1
            if c == 0:
                u = u * keep_left
            if c > cols:
                u = u * keep_right
            sec_a[c, :, :] = u[:, :LANES]
            sec_b[c, 0:M1, 0:rest] = u[:, LANES:]
            sec_b[c, 0 : M1 - 1, rest : 2 * rest] = u[1:, LANES:]

    def build2(c, carry):
        for k in range(9):
            off = (k // 3) * R + k % 3
            stack2[c, :, k * LANES : (k + 1) * LANES] = sec_a[c, off : off + M2, :].astype(bf)
        for dt in range(3):
            for half in range(2):
                k = 9 + 2 * dt + half
                off = dt * R + 2 * half
                stack2[c, :, k * LANES : (k + 1) * LANES] = sec_b[c, off : off + M2, :].astype(bf)
        return carry

    lax.fori_loop(0, hid_cols, build2, 0)
    for copy in copies2:
        copy.wait()
    step2 = 9
    for start in range(0, mer_cols, step2):
        n = min(step2, mer_cols - start)
        acc = jnp.dot(
            raw[start : start + n, LOW : LOW + M2, :].reshape(n * M2, LANES).astype(bf),
            wsc[...],
            preferred_element_type=f32,
        )
        for dc in range(3):
            acc += jnp.dot(
                stack2[start + dc : start + dc + n, :, : 9 * LANES].reshape(n * M2, 9 * LANES),
                w2m[dc].reshape(9 * LANES, c2),
                preferred_element_type=f32,
            )
            acc += jnp.dot(
                stack2[start + dc : start + dc + n, :, 9 * LANES :].reshape(n * M2, 6 * LANES),
                w2r[dc].reshape(6 * LANES, c2),
                preferred_element_type=f32,
            )
        for i in range(n):
            c = start + i
            mer = acc[i * M2 : (i + 1) * M2] * live2
            if c == cols:
                mer = mer * keep_right
            mer_a[c, 0:M2, :] = mer[:, :LANES]
            mer_b[c, 0:M2, 0:rest] = mer[:, LANES:]
            mer_b[c, 0 : M2 - 1, rest : 2 * rest] = mer[1:, LANES:]

    out_cols = cols // 2
    for j in range(out_cols):
        for dc in range(3):
            for dr in range(3):
                k = dc * 3 + dr
                stack3[j, :, k * LANES : (k + 1) * LANES] = mer_a[2 * j + dc, dr : dr + M2, :].astype(bf)
            for half in range(2):
                k = 9 + 2 * dc + half
                stack3[j, :, k * LANES : (k + 1) * LANES] = mer_b[
                    2 * j + dc, 2 * half : 2 * half + M2, :
                ].astype(bf)
    for copy in copies3:
        copy.wait()
    acc = jnp.dot(
        stack3[:, :, : 9 * LANES].reshape(out_cols * M2, 9 * LANES),
        wdm[...].reshape(9 * LANES, c2),
        preferred_element_type=f32,
    )
    acc += jnp.dot(
        stack3[:, :, 9 * LANES :].reshape(out_cols * M2, 6 * LANES),
        wdr[...].reshape(6 * LANES, c2),
        preferred_element_type=f32,
    )
    acc = acc.reshape(out_cols, M2, c2)
    result[0] = acc[:, :, :LANES]
    result[1, :, :, 0:rest] = acc[:, :, LANES:]
    for f in range(frames):
        for j in range(out_cols):
            a = result[0, j, pl.ds(f * R, rows // 2, stride=2), :]
            b = result[1, j, pl.ds(f * R, rows // 2, stride=2), :][:, :rest]
            out_ref[f, :, j * c2 : (j + 1) * c2] = jnp.concatenate([a, b], axis=-1).astype(bf)


def up(n, k):
    return -(-n // k) * k


def local(video_in, gain_first, gain_second, conv_first, conv_second, shortcut, downscale_weight):
    frames, rows, merged_cols = video_in.shape
    c1, c2 = shortcut.shape
    cols = merged_cols // c1

    prev, _ = exchange("tm", video_in, video_in)
    both = jnp.concatenate([prev, video_in], axis=0)
    above, below = exchange("height", both[:, rows - HIGH :], both[:, :HIGH])
    spare = jnp.zeros((2 * frames, 16 - (rows + LOW + HIGH), merged_cols), jnp.bfloat16)
    mid = jnp.concatenate([above[:, HIGH - LOW :], both, below, spare], axis=1)
    left, right = exchange("width", mid[:, :, merged_cols - EDGE * c1 :], mid[:, :, : EDGE * c1])

    R = rows + LOW + HIGH
    in_cols, hid_cols, mer_cols = cols + LOW + HIGH, cols + 3, cols + 1
    M1 = up((frames + 1) * R + rows + 3, 16)
    M2 = up((frames - 1) * R + rows + 1, 16)
    bf, f32 = jnp.bfloat16, jnp.float32
    vmem = pl.BlockSpec(memory_space=pltpu.VMEM)
    hbm = pl.BlockSpec(memory_space=pltpu.HBM)
    out_cols = cols // 2
    rows_up = mid.shape[1]
    return pl.pallas_call(
        functools.partial(kernel, (frames, rows, cols, c1, c2)),
        out_shape=jax.ShapeDtypeStruct((frames, rows // 2, out_cols * c2), bf),
        in_specs=[vmem] * 3 + [hbm] * 6,
        out_specs=vmem,
        scratch_shapes=[
            pltpu.VMEM((in_cols, up(max(M1 + 2 * R + 2, (2 * frames - 1) * R + rows_up), 8), LANES), f32),
            pltpu.VMEM((mer_cols, up((frames - 1) * R + rows_up, 8), LANES), f32),
            pltpu.VMEM((in_cols, M1, 9 * LANES), bf),
            pltpu.VMEM((hid_cols, M1, LANES), f32),
            pltpu.VMEM((hid_cols, M1, LANES), f32),
            pltpu.VMEM((hid_cols, M2, 15 * LANES), bf),
            pltpu.VMEM((mer_cols, M2 + 8, LANES), f32),
            pltpu.VMEM((mer_cols, M2 + 8, LANES), f32),
            pltpu.VMEM((out_cols, M2, 15 * LANES), bf),
            pltpu.VMEM((2, out_cols, M2, LANES), f32),
            pltpu.VMEM((3, 3, 3, LANES, c2), bf),
            pltpu.VMEM((3, 3, 3, LANES, c2), bf),
            pltpu.VMEM((3, 3, 4, c2 - LANES, c2), bf),
            pltpu.VMEM((3, 3, LANES, c2), bf),
            pltpu.VMEM((3, 4, c2 - LANES, c2), bf),
            pltpu.VMEM((LANES, c2), bf),
            pltpu.VMEM((1, c1), f32),
            pltpu.VMEM((1, c2), f32),
            pltpu.SemaphoreType.DMA((18,)),
        ],
        compiler_params=pltpu.CompilerParams(vmem_limit_bytes=60 * 1024 * 1024),
        cost_estimate=pl.CostEstimate(flops=4 * 10**9, bytes_accessed=5 * 10**6, transcendentals=10**6),
    )(
        mid, left, right, gain_first.reshape(1, c1), gain_second.reshape(1, c2), shortcut,
        conv_first, conv_second, downscale_weight,
    )


def solution(mesh):
    placed = (P("tm", "height", "width"), P(), P(), P(), P(), P(), P())
    return jax.shard_map(
        local, mesh=mesh, in_specs=placed, out_specs=P("tm", "height", "width"), check_vma=False
    )
```

```python
import functools
import jax
import jax.numpy as jnp
from jax import lax
from jax.experimental import pallas as pl
from jax.experimental.pallas import tpu as pltpu
from jax.sharding import PartitionSpec as P

epsilon = 1e-06
AXES = ("tm", "height", "width")
LANES = 128
LOW, HIGH = 2, 3
EDGE = 4
SLAB = 4


def swap_pairs(axis, parity):
    sizes = [lax.axis_size(name) for name in AXES]
    place = AXES.index(axis)
    count = sizes[place]
    pairs = []
    for t in range(sizes[0]):
        for h in range(sizes[1]):
            for w in range(sizes[2]):
                source = [t, h, w]
                target = [t, h, w]
                other = source[place] + (1 if source[place] % 2 == parity else -1)
                if 0 <= other < count:
                    target[place] = other
                elif axis == "width":
                    target[place] = other % count
                else:
                    target[2] = w ^ 1
                pairs.append(
                    tuple((p[0] * sizes[1] + p[1]) * sizes[2] + p[2] for p in (source, target))
                )
    return pairs


def swap(axis, outgoing):
    return [lax.ppermute(value, AXES, swap_pairs(axis, i)) for i, value in enumerate(outgoing)]


def rounds(axis):
    return 1 if lax.axis_size(axis) == 2 else 2


def choose(condition, target, first, second):
    @pl.when(condition)
    def _():
        target[...] = first()

    @pl.when(jnp.logical_not(condition))
    def _():
        target[...] = second()


def outgoing(axis, refs, to_next, to_prev):
    even = lax.axis_index(axis) % 2 == 0
    choose(even, refs[0], to_next, to_prev)
    if len(refs) > 1:
        choose(even, refs[1], to_prev, to_next)


def incoming(axis, refs, from_prev, from_next):
    index, count = lax.axis_index(axis), lax.axis_size(axis)
    even = index % 2 == 0
    for target, at_even, absent in ((from_prev, 1, 0), (from_next, 0, count - 1)):
        if target is None:
            continue
        for mine, which in ((even, at_even), (jnp.logical_not(even), 1 - at_even)):
            if which >= len(refs):
                continue

            @pl.when(mine & (index != absent))
            def _(target=target, which=which):
                target[...] = refs[which][...]

        @pl.when(index == absent)
        def _(target=target):
            target[...] = jnp.zeros(target.shape, target.dtype)


def rows_out(own, *refs):
    got, slabs = refs[: rounds("tm")], refs[rounds("tm") : -1]
    prev = refs[-1]
    incoming("tm", got, prev, None)
    rows = own.shape[1]

    def part(lo):
        return lambda: jnp.concatenate([prev[:, lo : lo + SLAB], own[:, lo : lo + SLAB]], axis=0)

    outgoing("height", slabs, part(rows - SLAB), part(0))


def cols_out(width, own, prev, *refs):
    got, mid, slabs = refs[: rounds("height")], refs[rounds("height")], refs[rounds("height") + 1 :]
    frames, rows = own.shape[0], own.shape[1]
    mid[0:frames, 0:rows, :] = prev[...]
    mid[frames:, 0:rows, :] = own[...]
    incoming("height", got, mid.at[:, rows : rows + SLAB, :], mid.at[:, rows + SLAB :, :])
    last = mid.shape[2] - width
    outgoing("width", slabs, lambda: mid[:, :, last:], lambda: mid[:, :, 0:width])


def arrange(c1, x, gain1, gain2, shortcut, conv1, conv2, down, xv, g1, g2, wsc, w1, w2m, w2r, wdm, wdr, sems):
    c2 = g2.shape[1]
    rest = c2 - LANES
    copies = [
        pltpu.make_async_copy(x, xv, sems.at[0]),
        pltpu.make_async_copy(gain1, g1, sems.at[1]),
        pltpu.make_async_copy(gain2, g2, sems.at[2]),
        pltpu.make_async_copy(shortcut, wsc.at[pl.ds(0, c1)], sems.at[3]),
    ]
    for dc in range(3):
        moves = [
            (conv1.at[:, :, dc], w1.at[dc, :, :, pl.ds(0, c1)]),
            (conv2.at[:, :, dc, pl.ds(0, LANES)], w2m.at[dc]),
            (conv2.at[:, :, dc, pl.ds(LANES, rest)], w2r.at[dc, :, pl.ds(0, 3)]),
            (down.at[:, dc, pl.ds(0, LANES)], wdm.at[dc]),
            (down.at[:, dc, pl.ds(LANES, rest)], wdr.at[dc, pl.ds(0, 3)]),
        ]
        for i, (source, target) in enumerate(moves):
            copies.append(pltpu.make_async_copy(source, target, sems.at[4 + 5 * dc + i]))
    for copy in copies:
        copy.start()
    bf = jnp.bfloat16
    wsc[c1:] = jnp.zeros((LANES - c1, c2), bf)
    w1[:, :, :, c1:, :] = jnp.zeros((3, 3, 3, LANES - c1, c2), bf)
    w2r[:, :, 3] = jnp.zeros((3, 3, rest, c2), bf)
    wdr[:, 3] = jnp.zeros((3, rest, c2), bf)
    for copy in copies:
        copy.wait()


class Steps:
    def __init__(self, frames, rows, cols, c1, c2, w1, w2m, w2r, wsc, g1, g2):
        self.frames, self.rows, self.cols, self.c1, self.c2 = frames, rows, cols, c1, c2
        self.rest = c2 - LANES
        self.R = rows + LOW + HIGH
        self.M1 = up((frames + 1) * self.R + rows + 3, 16)
        self.M2 = up((frames - 1) * self.R + rows + 1, 16)
        self.w1, self.w2m, self.w2r, self.wsc = w1, w2m, w2r, wsc
        gap = jnp.zeros((1, LANES - c1), jnp.float32)
        self.gain1, self.gain2 = jnp.concatenate([g1[...], gap], axis=-1), g2[...]
        t, h, w = [lax.axis_index(name) for name in AXES]
        starts, top, left = [i == 0 for i in (t, h, w)]
        bottom, right = [i == lax.axis_size(name) - 1 for i, name in ((h, "height"), (w, "width"))]
        p = lax.broadcasted_iota(jnp.int32, (self.M1, 1), 0)
        dead = (p < 2 * self.R) & starts
        for f in range(frames + 2):
            q = p - f * self.R
            dead |= ((q == 0) & top) | (((q == rows + 1) | (q == rows + 2)) & bottom)
        self.live1 = jnp.where(dead, 0.0, 1.0).astype(jnp.float32)
        p = lax.broadcasted_iota(jnp.int32, (self.M2, 1), 0)
        dead = p < 0
        for f in range(frames):
            dead |= (p == f * self.R + rows) & bottom
        self.live2 = jnp.where(dead, 0.0, 1.0).astype(jnp.float32)
        self.keep_left = jnp.where(left, 0.0, 1.0).astype(jnp.float32)
        self.keep_right = jnp.where(right, 0.0, 1.0).astype(jnp.float32)

    def spread(self):
        shape = (EDGE * self.c1, EDGE * LANES)
        source = lax.broadcasted_iota(jnp.int32, shape, 0)
        target = lax.broadcasted_iota(jnp.int32, shape, 1)
        slot, lane = target // LANES, target % LANES
        return jnp.where((source == slot * self.c1 + lane) & (lane < self.c1), 1.0, 0.0).astype(jnp.bfloat16)

    def unpack(self, ref, lane, spread, lo, hi, first, raw, place):
        tall = ref.shape[1]
        count = 2 * self.frames
        x = ref[:, :, lane : lane + EDGE * self.c1].reshape(count * tall, EDGE * self.c1)
        wide = jnp.dot(x, spread, preferred_element_type=jnp.float32)
        for k in range(lo, hi):
            v = wide[:, k * LANES : (k + 1) * LANES]
            ms = jnp.sum(v * v, axis=-1, keepdims=True) * (1.0 / self.c1)
            u = v * lax.rsqrt(ms + epsilon) * self.gain1
            u = u / (1.0 + jnp.exp(-u))
            c = place + k - lo
            for f in range(count):
                at = f * self.R
                for at_row, n, to in (
                    (0, self.rows, LOW),
                    (self.rows + SLAB - LOW, LOW, 0),
                    (self.rows + SLAB, HIGH, LOW + self.rows),
                ):
                    chunk = slice(f * tall + at_row, f * tall + at_row + n)
                    first[c, at + to : at + to + n, :] = u[chunk]
                    if f >= self.frames and (to == LOW or n == HIGH):
                        to += (f - self.frames) * self.R
                        raw[c, to : to + n, :] = v[chunk]

    def stack_first(self, c, first, stack):
        for k in range(9):
            off = (k // 3) * self.R + k % 3
            stack[c, :, k * LANES : (k + 1) * LANES] = first[c, off : off + self.M1, :].astype(jnp.bfloat16)

    def conv_first(self, get, wanted):
        acc = None
        for dc in range(3):
            part = jnp.dot(
                jnp.concatenate([get(c + dc) for c in wanted], axis=0),
                self.w1[dc].reshape(9 * LANES, self.c2),
                preferred_element_type=jnp.float32,
            )
            acc = part if acc is None else acc + part
        return acc

    def act_second(self, hid, keep):
        ms = jnp.sum(hid * hid, axis=-1, keepdims=True) * (1.0 / self.c2)
        u = hid * lax.rsqrt(ms + epsilon) * self.gain2
        u = u / (1.0 + jnp.exp(-u)) * self.live1
        return u if keep is None else u * keep

    def halves(self, c, value, low, high):
        count = value.shape[0]
        low[c, 0:count, :] = value[:, :LANES]
        high[c, 0:count, 0 : self.rest] = value[:, LANES:]
        high[c, 0 : count - 1, self.rest : 2 * self.rest] = value[1:, LANES:]

    def stack_second(self, c, low, high, stack):
        for k in range(9):
            off = (k // 3) * self.R + k % 3
            stack[c, :, k * LANES : (k + 1) * LANES] = low[c, off : off + self.M2, :].astype(jnp.bfloat16)
        for k in range(9, 15):
            off = (k - 9) // 2 * self.R + (k - 9) % 2 * 2
            stack[c, :, k * LANES : (k + 1) * LANES] = high[c, off : off + self.M2, :].astype(jnp.bfloat16)

    def conv_second(self, get, get_raw, wanted):
        acc = jnp.dot(
            jnp.concatenate([get_raw(m + LOW) for m in wanted], axis=0).astype(jnp.bfloat16),
            self.wsc[...],
            preferred_element_type=jnp.float32,
        )
        for dc in range(3):
            lhs = jnp.concatenate([get(m + dc) for m in wanted], axis=0)
            acc += jnp.dot(
                lhs[:, : 9 * LANES],
                self.w2m[dc].reshape(9 * LANES, self.c2),
                preferred_element_type=jnp.float32,
            )
            acc += jnp.dot(
                lhs[:, 9 * LANES :],
                self.w2r[dc].reshape(6 * LANES, self.c2),
                preferred_element_type=jnp.float32,
            )
        return acc

    def merged(self, c, value, keep, low, high):
        value = value * self.live2
        self.halves(c, value if keep is None else value * keep, low, high)


def inner(dims, mid, w1, w2m, w2r, wsc, g1, g2, stack1, stack2, raw, mer_a, mer_b, first, sec_a, sec_b):
    s = Steps(*dims, w1, w2m, w2r, wsc, g1, g2)
    sec_b[...] = jnp.zeros_like(sec_b)
    mer_a[...] = jnp.zeros_like(mer_a)
    mer_b[...] = jnp.zeros_like(mer_b)
    spread = s.spread()
    tail = 2 * s.frames * s.R
    first[:, tail:, :] = jnp.zeros((first.shape[0], first.shape[1] - tail, LANES), jnp.float32)
    for group in range(s.cols // EDGE):
        s.unpack(mid, group * EDGE * s.c1, spread, 0, EDGE, first, raw, group * EDGE)
    for c in range(s.cols):
        s.stack_first(c, first, stack1)
    hidden = list(range(LOW, s.cols))
    step = 7
    for start in range(0, len(hidden), step):
        wanted = hidden[start : start + step]
        acc = s.conv_first(lambda c: stack1[c - LOW], wanted)
        for i, c in enumerate(wanted):
            s.halves(c - LOW, s.act_second(acc[i * s.M1 : (i + 1) * s.M1], None), sec_a, sec_b)
    for c in range(len(hidden)):
        s.stack_second(c, sec_a, sec_b, stack2)
    wanted = list(range(LOW, s.cols - 2))
    acc = s.conv_second(
        lambda c: stack2[c - LOW], lambda c: raw[c - LOW, LOW : LOW + s.M2, :], wanted
    )
    for i in range(len(wanted)):
        s.merged(i, acc[i * s.M2 : (i + 1) * s.M2], None, mer_a, mer_b)


def outer(
    dims, got_a, got_b, w1, w2m, w2r, wsc, g1, g2, wdm, wdr, in_stack1, in_stack2, in_raw, in_mer_a, in_mer_b,
    out, left, right, first, raw, stack1, sec_a, sec_b, stack2, mer_a, mer_b, stack3, result,
):
    incoming("width", (got_a, got_b), left, right)
    s = Steps(*dims, w1, w2m, w2r, wsc, g1, g2)
    bf, f32 = jnp.bfloat16, jnp.float32
    cols, rest, R, M2 = s.cols, s.rest, s.R, s.M2
    sec_b[...] = jnp.zeros_like(sec_b)
    mer_a[...] = jnp.zeros_like(mer_a)
    mer_b[...] = jnp.zeros_like(mer_b)
    spread = s.spread()
    tail = 2 * s.frames * s.R
    first[:, tail:, :] = jnp.zeros((first.shape[0], first.shape[1] - tail, LANES), jnp.float32)
    s.unpack(left, 0, spread, EDGE - LOW, EDGE, first, raw, 0)
    s.unpack(right, 0, spread, 0, HIGH, first, raw, LOW)
    for c in range(LOW + HIGH):
        s.stack_first(c, first, stack1)

    def new_or(own, given, lo, hi):
        return lambda c: given(c - lo) if lo <= c < hi else own(c if c < lo else c - hi + lo)

    wanted = [0, 1, cols, cols + 1, cols + 2]
    acc = s.conv_first(new_or(lambda i: stack1[i], lambda i: in_stack1[i], LOW, LOW + cols), wanted)
    keeps = [s.keep_left, None, None, s.keep_right, s.keep_right]
    for i, keep in enumerate(keeps):
        s.halves(i, s.act_second(acc[i * s.M1 : (i + 1) * s.M1], keep), sec_a, sec_b)
    for c in range(len(wanted)):
        s.stack_second(c, sec_a, sec_b, stack2)
    wanted = [0, 1, cols - 2, cols - 1, cols]
    acc = s.conv_second(
        new_or(lambda i: stack2[i], lambda i: in_stack2[i], LOW, cols),
        new_or(
            lambda i: raw[i, LOW : LOW + M2, :], lambda i: in_raw[i, LOW : LOW + M2, :], LOW, LOW + cols
        ),
        wanted,
    )
    keeps = [None, None, None, None, s.keep_right]
    for i, keep in enumerate(keeps):
        s.merged(i, acc[i * M2 : (i + 1) * M2], keep, mer_a, mer_b)

    lows = new_or(lambda i: (mer_a, i), lambda i: (in_mer_a, i), LOW, cols - 2)
    highs = new_or(lambda i: (mer_b, i), lambda i: (in_mer_b, i), LOW, cols - 2)
    out_cols = cols // 2
    for j in range(out_cols):
        for dc in range(3):
            ref, c = lows(2 * j + dc)
            for dr in range(3):
                k = dc * 3 + dr
                stack3[j, :, k * LANES : (k + 1) * LANES] = ref[c, dr : dr + M2, :].astype(bf)
            ref, c = highs(2 * j + dc)
            for half in range(2):
                k = 9 + 2 * dc + half
                stack3[j, :, k * LANES : (k + 1) * LANES] = ref[c, 2 * half : 2 * half + M2, :].astype(bf)
    acc = jnp.dot(
        stack3[:, :, : 9 * LANES].reshape(out_cols * M2, 9 * LANES),
        wdm[...].reshape(9 * LANES, s.c2),
        preferred_element_type=f32,
    )
    acc += jnp.dot(
        stack3[:, :, 9 * LANES :].reshape(out_cols * M2, 6 * LANES),
        wdr[...].reshape(6 * LANES, s.c2),
        preferred_element_type=f32,
    )
    acc = acc.reshape(out_cols, M2, s.c2)
    result[0] = acc[:, :, :LANES]
    result[1, :, :, 0:rest] = acc[:, :, LANES:]
    for f in range(s.frames):
        for j in range(out_cols):
            a = result[0, j, pl.ds(f * R, s.rows // 2, stride=2), :]
            b = result[1, j, pl.ds(f * R, s.rows // 2, stride=2), :][:, :rest]
            out[f, :, j * s.c2 : (j + 1) * s.c2] = jnp.concatenate([a, b], axis=-1).astype(bf)


def up(n, k):
    return -(-n // k) * k


def cost(flops):
    return pl.CostEstimate(flops=flops, bytes_accessed=5 * 10**6, transcendentals=10**5)


def local(video_in, gain_first, gain_second, conv_first, conv_second, shortcut, downscale_weight):
    frames, rows, merged_cols = video_in.shape
    c1, c2 = shortcut.shape
    cols = merged_cols // c1
    rest = c2 - LANES
    dims = (frames, rows, cols, c1, c2)
    bf, f32 = jnp.bfloat16, jnp.float32
    vmem = pl.BlockSpec(memory_space=pltpu.VMEM)
    hbm = pl.BlockSpec(memory_space=pltpu.HBM)
    params = pltpu.CompilerParams(vmem_limit_bytes=14 * 1024 * 1024)
    small = pltpu.CompilerParams(vmem_limit_bytes=4 * 1024 * 1024)
    out_cols = cols // 2
    R = rows + LOW + HIGH
    M1 = up((frames + 1) * R + rows + 3, 16)
    M2 = up((frames - 1) * R + rows + 1, 16)
    first_rows = up(M1 + 2 * R + 2, 8)
    raw_rows = up(M2 + LOW, 8)
    held = M2 + 8

    source = [gain_first.reshape(1, c1), gain_second.reshape(1, c2), shortcut]
    source += [conv_first, conv_second, downscale_weight]
    own, g1, g2, wsc, w1, w2m, w2r, wdm, wdr = pl.pallas_call(
        functools.partial(arrange, c1),
        out_shape=[
            pltpu.VMEM(video_in.shape, bf),
            pltpu.VMEM((1, c1), f32),
            pltpu.VMEM((1, c2), f32),
            pltpu.VMEM((LANES, c2), bf),
            pltpu.VMEM((3, 3, 3, LANES, c2), bf),
            pltpu.VMEM((3, 3, 3, LANES, c2), bf),
            pltpu.VMEM((3, 3, 4, rest, c2), bf),
            pltpu.VMEM((3, 3, LANES, c2), bf),
            pltpu.VMEM((3, 4, rest, c2), bf),
        ],
        in_specs=[hbm] * 7,
        out_specs=[vmem] * 9,
        scratch_shapes=[pltpu.SemaphoreType.DMA((19,))],
        compiler_params=small,
        cost_estimate=cost(0),
        name="arrange",
    )(*[pltpu.with_memory_space_constraint(a, pltpu.HBM) for a in [video_in] + source])

    tall = rows + 2 * SLAB
    got = swap("tm", [video_in] * rounds("tm"))
    *slabs, prev = pl.pallas_call(
        rows_out,
        out_shape=[pltpu.VMEM((2 * frames, SLAB, merged_cols), bf)] * rounds("height")
        + [pltpu.VMEM(video_in.shape, bf)],
        in_specs=[vmem] * (1 + len(got)),
        out_specs=[vmem] * (1 + rounds("height")),
        compiler_params=small,
        cost_estimate=cost(0),
        name="rows_out",
    )(own, *got)
    got = swap("height", slabs)
    mid, *slabs = pl.pallas_call(
        functools.partial(cols_out, EDGE * c1),
        out_shape=[pltpu.VMEM((2 * frames, tall, merged_cols), bf)]
        + [pltpu.VMEM((2 * frames, tall, EDGE * c1), bf)] * 2,
        in_specs=[vmem] * (2 + len(got)),
        out_specs=[vmem] * 3,
        compiler_params=small,
        cost_estimate=cost(0),
        name="cols_out",
    )(own, prev, *got)
    got_a, got_b = swap("width", slabs)

    hid_in, mer_in = cols - 2, cols - 4
    passed = pl.pallas_call(
        functools.partial(inner, dims),
        out_shape=[
            pltpu.VMEM((cols, M1, 9 * LANES), bf),
            pltpu.VMEM((hid_in, M2, 15 * LANES), bf),
            pltpu.VMEM((cols, raw_rows, LANES), f32),
            pltpu.VMEM((mer_in, held, LANES), f32),
            pltpu.VMEM((mer_in, held, LANES), f32),
        ],
        in_specs=[vmem] * 7,
        out_specs=[vmem] * 5,
        scratch_shapes=[
            pltpu.VMEM((cols, first_rows, LANES), f32),
            pltpu.VMEM((hid_in, M1, LANES), f32),
            pltpu.VMEM((hid_in, M1, LANES), f32),
        ],
        compiler_params=params,
        cost_estimate=cost(4 * 10**9),
        name="inner",
    )(mid, w1, w2m, w2r, wsc, g1, g2)
    edge = LOW + HIGH
    return pl.pallas_call(
        functools.partial(outer, dims),
        out_shape=jax.ShapeDtypeStruct((frames, rows // 2, out_cols * c2), bf),
        in_specs=[vmem] * 15,
        out_specs=vmem,
        scratch_shapes=[
            pltpu.VMEM((2 * frames, tall, EDGE * c1), bf),
            pltpu.VMEM((2 * frames, tall, EDGE * c1), bf),
            pltpu.VMEM((edge, first_rows, LANES), f32),
            pltpu.VMEM((edge, raw_rows, LANES), f32),
            pltpu.VMEM((edge, M1, 9 * LANES), bf),
            pltpu.VMEM((edge, M1, LANES), f32),
            pltpu.VMEM((edge, M1, LANES), f32),
            pltpu.VMEM((edge, M2, 15 * LANES), bf),
            pltpu.VMEM((edge, held, LANES), f32),
            pltpu.VMEM((edge, held, LANES), f32),
            pltpu.VMEM((out_cols, M2, 15 * LANES), bf),
            pltpu.VMEM((2, out_cols, M2, LANES), f32),
        ],
        compiler_params=params,
        cost_estimate=cost(2 * 10**9),
        name="outer",
    )(got_a, got_b, w1, w2m, w2r, wsc, g1, g2, wdm, wdr, *passed)


def solution(mesh):
    placed = (P("tm", "height", "width"), P(), P(), P(), P(), P(), P())
    return jax.shard_map(
        local, mesh=mesh, in_specs=placed, out_specs=P("tm", "height", "width"), check_vma=False
    )
```

```python
import functools
import jax
import jax.numpy as jnp
from jax import lax
from jax.experimental import pallas as pl
from jax.experimental.pallas import tpu as pltpu
from jax.sharding import PartitionSpec as P

epsilon = 1e-06
AXES = ("tm", "height", "width")
LANES = 128
LOW, HIGH = 2, 3
EDGE = 4


def swap_pairs(axis, parity):
    sizes = [lax.axis_size(name) for name in AXES]
    place = AXES.index(axis)
    count = sizes[place]
    pairs = []
    for t in range(sizes[0]):
        for h in range(sizes[1]):
            for w in range(sizes[2]):
                source = [t, h, w]
                target = [t, h, w]
                other = source[place] + (1 if source[place] % 2 == parity else -1)
                if 0 <= other < count:
                    target[place] = other
                elif axis == "width":
                    target[place] = other % count
                else:
                    target[2] = w ^ 1
                pairs.append(
                    tuple((p[0] * sizes[1] + p[1]) * sizes[2] + p[2] for p in (source, target))
                )
    return pairs


def swap(axis, outgoing):
    return [lax.ppermute(value, AXES, swap_pairs(axis, i)) for i, value in enumerate(outgoing)]


def rounds(axis):
    return 1 if lax.axis_size(axis) == 2 else 2


def outgoing(axis, count, to_next, to_prev):
    even = lax.axis_index(axis) % 2 == 0
    return [jnp.where(even, *pair) for pair in ((to_next, to_prev), (to_prev, to_next))[:count]]


def incoming(axis, values):
    index, count = lax.axis_index(axis), lax.axis_size(axis)
    even = index % 2 == 0
    at_even, at_odd = values[0], values[-1]
    zero = jnp.zeros_like(at_even)
    if len(values) == 1:
        return jnp.where(even, zero, at_even), jnp.where(even, at_even, zero)
    return (
        jnp.where(index == 0, zero, jnp.where(even, at_odd, at_even)),
        jnp.where(index == count - 1, zero, jnp.where(even, at_even, at_odd)),
    )


def rows_out(own, *refs):
    got, slabs, prev, wide = refs[: rounds("tm")], refs[rounds("tm") : -2], refs[-2], refs[-1]
    prev[...] = incoming("tm", [ref[...] for ref in got])[0]
    frames, rows = own.shape[0], own.shape[1]
    for i, slab in enumerate(slabs):
        for f in range(2 * frames):
            block = (prev if f < frames else own)[f % frames].astype(jnp.float32)
            part = outgoing("height", len(slabs), block[rows - HIGH :], block[:HIGH])[i]
            wide[f * HIGH : (f + 1) * HIGH, :] = part
        slab[...] = wide[...].astype(jnp.bfloat16)


def cols_out(width, own, prev, *refs):
    got, rim, slabs, wide = refs[: rounds("height")], refs[rounds("height")], refs[-3:-1], refs[-1]
    frames, rows = own.shape[0], own.shape[1]
    above, below = incoming("height", [ref[...].astype(jnp.float32) for ref in got])
    for f in range(2 * frames):
        wide[f, 0:1, :] = jnp.zeros((1, wide.shape[2]), jnp.float32)
        wide[f, 1 : 1 + HIGH, :] = above[f * HIGH : (f + 1) * HIGH]
        wide[f, 1 + HIGH : 1 + 2 * HIGH, :] = below[f * HIGH : (f + 1) * HIGH]
        wide[f, 1 + 2 * HIGH :, :] = jnp.zeros((1, wide.shape[2]), jnp.float32)
    rim[...] = wide[...].astype(jnp.bfloat16)
    last = own.shape[2] - width
    for lo, hi, source in ((0, frames, prev), (frames, 2 * frames, own)):
        for slab, part in zip(slabs, outgoing("width", 2, source[:, :, last:], source[:, :, :width])):
            slab[lo:hi, 0:rows, :] = part
    for slab, part in zip(slabs, outgoing("width", 2, rim[:, :, last:], rim[:, :, :width])):
        slab[:, rows:, :] = part


def arrange(c1, x, gain1, gain2, shortcut, conv1, conv2, down, xv, g1, g2, wsc, w1, w2m, w2r, wdm, wdr, sems):
    c2 = g2.shape[1]
    rest = c2 - LANES
    copies = [
        pltpu.make_async_copy(x, xv, sems.at[0]),
        pltpu.make_async_copy(gain1, g1, sems.at[1]),
        pltpu.make_async_copy(gain2, g2, sems.at[2]),
        pltpu.make_async_copy(shortcut, wsc.at[pl.ds(0, c1)], sems.at[3]),
    ]
    for dc in range(3):
        moves = [
            (conv1.at[:, :, dc], w1.at[dc, :, :, pl.ds(0, c1)]),
            (conv2.at[:, :, dc, pl.ds(0, LANES)], w2m.at[dc]),
            (conv2.at[:, :, dc, pl.ds(LANES, rest)], w2r.at[dc, :, pl.ds(0, 3)]),
            (down.at[:, dc, pl.ds(0, LANES)], wdm.at[dc]),
            (down.at[:, dc, pl.ds(LANES, rest)], wdr.at[dc, pl.ds(0, 3)]),
        ]
        for i, (source, target) in enumerate(moves):
            copies.append(pltpu.make_async_copy(source, target, sems.at[4 + 5 * dc + i]))
    for copy in copies:
        copy.start()
    bf = jnp.bfloat16
    wsc[c1:] = jnp.zeros((LANES - c1, c2), bf)
    w1[:, :, :, c1:, :] = jnp.zeros((3, 3, 3, LANES - c1, c2), bf)
    w2r[:, :, 3] = jnp.zeros((3, 3, rest, c2), bf)
    wdr[:, 3] = jnp.zeros((3, rest, c2), bf)
    for copy in copies:
        copy.wait()


class Steps:
    def __init__(self, frames, rows, cols, c1, c2, w1, w2m, w2r, wsc, g1, g2):
        self.frames, self.rows, self.cols, self.c1, self.c2 = frames, rows, cols, c1, c2
        self.rest = c2 - LANES
        self.R = rows + LOW + HIGH
        self.M1 = up((frames + 1) * self.R + rows + 3, 16)
        self.M2 = up((frames - 1) * self.R + rows + 1, 16)
        self.pitch = rows + 2
        self.w1, self.w2m, self.w2r, self.wsc = w1, w2m, w2r, wsc
        gap = jnp.zeros((1, LANES - c1), jnp.float32)
        self.gain1 = jnp.concatenate([g1[...], gap], axis=-1)
        self.gain2 = None if g2 is None else g2[...]
        t, h, w = [lax.axis_index(name) for name in AXES]
        starts, top, left = [i == 0 for i in (t, h, w)]
        bottom, right = [i == lax.axis_size(name) - 1 for i, name in ((h, "height"), (w, "width"))]
        p = lax.broadcasted_iota(jnp.int32, (self.M1, 1), 0)
        dead = (p < 2 * self.R) & starts
        for f in range(frames + 2):
            q = p - f * self.R
            dead |= ((q == 0) & top) | (((q == rows + 1) | (q == rows + 2)) & bottom)
        self.live1 = jnp.where(dead, 0.0, 1.0).astype(jnp.float32)
        p = lax.broadcasted_iota(jnp.int32, (self.M2, 1), 0)
        dead = p < 0
        for f in range(frames):
            dead |= (p == f * self.R + rows) & bottom
        self.live2 = jnp.where(dead, 0.0, 1.0).astype(jnp.float32)
        self.keep_left = jnp.where(left, 0.0, 1.0).astype(jnp.float32)
        self.keep_right = jnp.where(right, 0.0, 1.0).astype(jnp.float32)

    def spread(self):
        shape = (EDGE * self.c1, EDGE * LANES)
        source = lax.broadcasted_iota(jnp.int32, shape, 0)
        target = lax.broadcasted_iota(jnp.int32, shape, 1)
        slot, lane = target // LANES, target % LANES
        return jnp.where((source == slot * self.c1 + lane) & (lane < self.c1), 1.0, 0.0).astype(jnp.bfloat16)

    def unpack(self, x, spread, lo, hi, first, raw, place, pieces):
        count, tall = x.shape[0], x.shape[1]
        wide = jnp.dot(
            x.reshape(count * tall, EDGE * self.c1), spread, preferred_element_type=jnp.float32
        )
        for k in range(lo, hi):
            v = wide[:, k * LANES : (k + 1) * LANES]
            ms = jnp.sum(v * v, axis=-1, keepdims=True) * (1.0 / self.c1)
            u = v * (0.5 * lax.rsqrt(ms + epsilon)) * self.gain1
            u = u + u * jnp.tanh(u)
            c = place + k - lo
            for f in range(count):
                at = f * self.R
                for source, n, to in pieces:
                    chunk = slice(f * tall + source, f * tall + source + n)
                    first[c, at + to : at + to + n, :] = u[chunk]
                    if f >= self.frames and to >= LOW:
                        to += (f - self.frames) * self.R
                        raw[c, to : to + n, :] = v[chunk]

    def own_pieces(self):
        return [(0, self.rows, LOW)]

    def rim_pieces(self, start):
        return [(start + 1 + HIGH - LOW, LOW, 0), (start + 1 + HIGH, HIGH, LOW + self.rows)]

    def stack_first(self, c, first, stack):
        for k in range(9):
            off = (k // 3) * self.R + k % 3
            stack[c, :, k * LANES : (k + 1) * LANES] = first[c, off : off + self.M1, :].astype(jnp.bfloat16)

    def conv_first(self, get, wanted):
        lhs = [jnp.concatenate([get(c + dc) for dc in range(3)], axis=-1) for c in wanted]
        return jnp.dot(
            jnp.concatenate(lhs, axis=0),
            self.w1[...].reshape(27 * LANES, self.c2),
            preferred_element_type=jnp.float32,
        )

    def act_second(self, hid, keep):
        ms = jnp.sum(hid * hid, axis=-1, keepdims=True) * (1.0 / self.c2)
        scale = 0.5 * lax.rsqrt(ms + epsilon) * self.live1
        u = hid * (scale if keep is None else scale * keep) * self.gain2
        return u + u * jnp.tanh(u)

    def halves(self, c, value, low, high):
        count = value.shape[0]
        low[c, 0:count, :] = value[:, :LANES]
        high[c, 0:count, 0 : self.rest] = value[:, LANES:]
        high[c, 0 : count - 1, self.rest : 2 * self.rest] = value[1:, LANES:]

    def stack_second(self, c, low, high, stack):
        for k in range(9):
            off = (k // 3) * self.R + k % 3
            stack[c, :, k * LANES : (k + 1) * LANES] = low[c, off : off + self.M2, :].astype(jnp.bfloat16)
        for k in range(9, 15):
            off = (k - 9) // 2 * self.R + (k - 9) % 2 * 2
            stack[c, :, k * LANES : (k + 1) * LANES] = high[c, off : off + self.M2, :].astype(jnp.bfloat16)

    def conv_second(self, get, get_raw, wanted):
        mains = [[get(m + dc)[:, : 9 * LANES] for dc in range(3)] for m in wanted]
        rests = [[get(m + dc)[:, 9 * LANES :] for dc in range(3)] for m in wanted]
        lhs = [
            jnp.concatenate(main + rest + [get_raw(m + LOW).astype(jnp.bfloat16)], axis=-1)
            for m, main, rest in zip(wanted, mains, rests)
        ]
        rhs = [self.w2m[...].reshape(27 * LANES, self.c2), self.w2r[...].reshape(18 * LANES, self.c2)]
        return jnp.dot(
            jnp.concatenate(lhs, axis=0),
            jnp.concatenate(rhs + [self.wsc[...]], axis=0),
            preferred_element_type=jnp.float32,
        )

    def merged(self, c, value, keep, low, high):
        value = value * (self.live2 if keep is None else self.live2 * keep)
        n = self.rows + 1
        for f in range(self.frames):
            at = f * self.pitch
            chunk = value[f * self.R : f * self.R + n]
            low[c, at : at + n, :] = chunk[:, :LANES]
            high[c, at : at + n, 0 : self.rest] = chunk[:, LANES:]
            high[c, at : at + n - 1, self.rest : 2 * self.rest] = chunk[1:, LANES:]

    def down(self, lows, highs, wanted, stack, wdm, wdr, result):
        bf = jnp.bfloat16
        count = stack.shape[1]
        for j in wanted:
            for dc in range(3):
                ref, c = lows(2 * j + dc)
                for dr in range(3):
                    k = dc * 3 + dr
                    stack[j, :, k * LANES : (k + 1) * LANES] = ref[c, pl.ds(dr, count, stride=2), :].astype(bf)
                ref, c = highs(2 * j + dc)
                for half in range(2):
                    k = 9 + 2 * dc + half
                    part = ref[c, pl.ds(2 * half, count, stride=2), :]
                    stack[j, :, k * LANES : (k + 1) * LANES] = part.astype(bf)
        acc = jnp.dot(
            jnp.concatenate([stack[j] for j in wanted], axis=0),
            jnp.concatenate([wdm[...].reshape(9 * LANES, self.c2), wdr[...].reshape(6 * LANES, self.c2)], axis=0),
            preferred_element_type=jnp.float32,
        )
        for i, j in enumerate(wanted):
            result(j, acc[i * count : (i + 1) * count])


def early(dims, own, prev, g1, first, raw):
    s = Steps(*dims, None, None, None, None, g1, None)
    tail = 2 * s.frames * s.R
    first[:, tail:, :] = jnp.zeros((first.shape[0], first.shape[1] - tail, LANES), jnp.float32)
    spread = s.spread()
    for group in range(s.cols // EDGE):
        lanes = slice(group * EDGE * s.c1, (group + 1) * EDGE * s.c1)
        x = jnp.concatenate([prev[:, :, lanes], own[:, :, lanes]], axis=0)
        s.unpack(x, spread, 0, EDGE, first, raw, group * EDGE, s.own_pieces())


def inner(
    dims, rim, w1, w2m, w2r, wsc, g1, g2, _first, _raw, first, raw, stack1, stack2, mer_a, mer_b, sec_a, sec_b
):
    s = Steps(*dims, w1, w2m, w2r, wsc, g1, g2)
    sec_b[...] = jnp.zeros_like(sec_b)
    mer_a[...] = jnp.zeros_like(mer_a)
    mer_b[...] = jnp.zeros_like(mer_b)
    spread = s.spread()
    for group in range(s.cols // EDGE):
        x = rim[:, :, group * EDGE * s.c1 : (group + 1) * EDGE * s.c1]
        s.unpack(x, spread, 0, EDGE, first, raw, group * EDGE, s.rim_pieces(0))
    for c in range(s.cols):
        s.stack_first(c, first, stack1)
    hidden = list(range(LOW, s.cols))
    step = 7
    for start in range(0, len(hidden), step):
        wanted = hidden[start : start + step]
        acc = s.conv_first(lambda c: stack1[c - LOW], wanted)
        for i, c in enumerate(wanted):
            s.halves(c - LOW, s.act_second(acc[i * s.M1 : (i + 1) * s.M1], None), sec_a, sec_b)
            s.stack_second(c - LOW, sec_a, sec_b, stack2)
    merged = list(range(LOW, s.cols - 2))
    step = 6
    for start in range(0, len(merged), step):
        wanted = merged[start : start + step]
        acc = s.conv_second(
            lambda c: stack2[c - LOW], lambda c: raw[c - LOW, LOW : LOW + s.M2, :], wanted
        )
        for i, c in enumerate(wanted):
            s.merged(c - LOW, acc[i * s.M2 : (i + 1) * s.M2], None, mer_a, mer_b)


def outer(
    dims, got_a, got_b, w1, w2m, w2r, wsc, g1, g2, wdm, wdr, in_raw, in_stack1, in_stack2, in_mer_a, in_mer_b,
    out, first, raw, stack1, sec_a, sec_b, stack2, mer_a, mer_b, stack3,
):
    s = Steps(*dims, w1, w2m, w2r, wsc, g1, g2)
    cols, M1, M2 = s.cols, s.M1, s.M2
    sec_b[...] = jnp.zeros_like(sec_b)
    mer_a[...] = jnp.zeros_like(mer_a)
    mer_b[...] = jnp.zeros_like(mer_b)
    tail = 2 * s.frames * s.R
    first[:, tail:, :] = jnp.zeros((first.shape[0], first.shape[1] - tail, LANES), jnp.float32)
    spread = s.spread()
    left, right = incoming("width", [got_a[...], got_b[...]])
    pieces = s.own_pieces() + s.rim_pieces(s.rows)
    s.unpack(left, spread, EDGE - LOW, EDGE, first, raw, 0, pieces)
    s.unpack(right, spread, 0, HIGH, first, raw, LOW, pieces)
    for c in range(LOW + HIGH):
        s.stack_first(c, first, stack1)

    def new_or(own, given, lo, hi):
        return lambda c: given(c - lo) if lo <= c < hi else own(c if c < lo else c - hi + lo)

    def store(j, value):
        n = s.rows // 2
        for f in range(s.frames):
            at = f * s.pitch // 2
            out[f, :, j * s.c2 : (j + 1) * s.c2] = value[at : at + n].astype(jnp.bfloat16)

    lows = new_or(lambda i: (mer_a, i), lambda i: (in_mer_a, i), LOW, cols - 2)
    highs = new_or(lambda i: (mer_b, i), lambda i: (in_mer_b, i), LOW, cols - 2)
    out_cols = cols // 2
    get1 = new_or(lambda i: stack1[i], lambda i: in_stack1[i], LOW, LOW + cols)
    get2 = new_or(lambda i: stack2[i], lambda i: in_stack2[i], LOW, cols)
    get_raw = new_or(
        lambda i: raw[i, LOW : LOW + M2, :], lambda i: in_raw[i, LOW : LOW + M2, :], LOW, LOW + cols
    )
    sides = [
        ([0, 1], [s.keep_left, None], [0, 1], [None, None], 0),
        ([cols, cols + 1, cols + 2], [None] + [s.keep_right] * 2, [cols - 2, cols - 1, cols], [None, None, s.keep_right], 2),
    ]
    for wanted, keeps, _, _, at in sides:
        acc = s.conv_first(get1, wanted)
        for i, keep in enumerate(keeps):
            s.halves(at + i, s.act_second(acc[i * M1 : (i + 1) * M1], keep), sec_a, sec_b)
            s.stack_second(at + i, sec_a, sec_b, stack2)
    s.down(lows, highs, list(range(1, out_cols - 2)), stack3, wdm, wdr, store)
    for _, _, wanted, keeps, at in sides:
        acc = s.conv_second(get2, get_raw, wanted)
        for i, keep in enumerate(keeps):
            s.merged(at + i, acc[i * M2 : (i + 1) * M2], keep, mer_a, mer_b)
    s.down(lows, highs, [0, out_cols - 2, out_cols - 1], stack3, wdm, wdr, store)


def up(n, k):
    return -(-n // k) * k


def cost(flops):
    return pl.CostEstimate(flops=flops, bytes_accessed=5 * 10**6, transcendentals=10**5)


def local(video_in, gain_first, gain_second, conv_first, conv_second, shortcut, downscale_weight):
    frames, rows, merged_cols = video_in.shape
    c1, c2 = shortcut.shape
    cols = merged_cols // c1
    rest = c2 - LANES
    dims = (frames, rows, cols, c1, c2)
    bf, f32 = jnp.bfloat16, jnp.float32
    vmem = pl.BlockSpec(memory_space=pltpu.VMEM)
    hbm = pl.BlockSpec(memory_space=pltpu.HBM)
    params = pltpu.CompilerParams(vmem_limit_bytes=14 * 1024 * 1024)
    small = pltpu.CompilerParams(vmem_limit_bytes=4 * 1024 * 1024)
    out_cols = cols // 2
    R = rows + LOW + HIGH
    M1 = up((frames + 1) * R + rows + 3, 16)
    M2 = up((frames - 1) * R + rows + 1, 16)
    first_rows = up(M1 + 2 * R + 2, 8)
    raw_rows = up(M2 + LOW, 8)
    count = up((frames - 1) * (rows + 2) // 2 + rows // 2, 8)
    held = up(2 * count + 1, 8)

    source = [gain_first.reshape(1, c1), gain_second.reshape(1, c2), shortcut]
    source += [conv_first, conv_second, downscale_weight]
    own, g1, g2, wsc, w1, w2m, w2r, wdm, wdr = pl.pallas_call(
        functools.partial(arrange, c1),
        out_shape=[
            pltpu.VMEM(video_in.shape, bf),
            pltpu.VMEM((1, c1), f32),
            pltpu.VMEM((1, c2), f32),
            pltpu.VMEM((LANES, c2), bf),
            pltpu.VMEM((3, 3, 3, LANES, c2), bf),
            pltpu.VMEM((3, 3, 3, LANES, c2), bf),
            pltpu.VMEM((3, 3, 4, rest, c2), bf),
            pltpu.VMEM((3, 3, LANES, c2), bf),
            pltpu.VMEM((3, 4, rest, c2), bf),
        ],
        in_specs=[hbm] * 7,
        out_specs=[vmem] * 9,
        scratch_shapes=[pltpu.SemaphoreType.DMA((19,))],
        compiler_params=small,
        cost_estimate=cost(0),
        name="arrange",
    )(*[pltpu.with_memory_space_constraint(a, pltpu.HBM) for a in [video_in] + source])

    tall = 2 * rows
    got = swap("tm", [video_in] * rounds("tm"))
    *slabs, prev = pl.pallas_call(
        rows_out,
        out_shape=[pltpu.VMEM((2 * frames * HIGH, merged_cols), bf)] * rounds("height")
        + [pltpu.VMEM(video_in.shape, bf)],
        in_specs=[vmem] * (1 + len(got)),
        out_specs=[vmem] * (1 + rounds("height")),
        scratch_shapes=[pltpu.VMEM((2 * frames * HIGH, merged_cols), f32)],
        compiler_params=small,
        cost_estimate=cost(0),
        name="rows_out",
    )(own, *got)
    got = swap("height", slabs)
    first, raw = pl.pallas_call(
        functools.partial(early, dims),
        out_shape=[
            pltpu.VMEM((cols, first_rows, LANES), f32),
            pltpu.VMEM((cols, raw_rows, LANES), f32),
        ],
        in_specs=[vmem] * 3,
        out_specs=[vmem] * 2,
        compiler_params=small,
        cost_estimate=cost(10**9),
        name="early",
    )(own, prev, g1)
    rim, *slabs = pl.pallas_call(
        functools.partial(cols_out, EDGE * c1),
        out_shape=[pltpu.VMEM((2 * frames, 2 + 2 * HIGH, merged_cols), bf)]
        + [pltpu.VMEM((2 * frames, tall, EDGE * c1), bf)] * 2,
        in_specs=[vmem] * (2 + len(got)),
        out_specs=[vmem] * 3,
        scratch_shapes=[pltpu.VMEM((2 * frames, 2 + 2 * HIGH, merged_cols), f32)],
        compiler_params=small,
        cost_estimate=cost(0),
        name="cols_out",
    )(own, prev, *got)
    got_a, got_b = swap("width", slabs)

    hid_in, mer_in = cols - 2, cols - 4
    _, *passed = pl.pallas_call(
        functools.partial(inner, dims),
        out_shape=[
            pltpu.VMEM((cols, first_rows, LANES), f32),
            pltpu.VMEM((cols, raw_rows, LANES), f32),
            pltpu.VMEM((cols, M1, 9 * LANES), bf),
            pltpu.VMEM((hid_in, M2, 15 * LANES), bf),
            pltpu.VMEM((mer_in, held, LANES), f32),
            pltpu.VMEM((mer_in, held, LANES), f32),
        ],
        in_specs=[vmem] * 9,
        out_specs=[vmem] * 6,
        scratch_shapes=[
            pltpu.VMEM((hid_in, M1, LANES), f32),
            pltpu.VMEM((hid_in, M1, LANES), f32),
        ],
        input_output_aliases={7: 0, 8: 1},
        compiler_params=params,
        cost_estimate=cost(4 * 10**9),
        name="inner",
    )(rim, w1, w2m, w2r, wsc, g1, g2, first, raw)
    edge = LOW + HIGH
    return pl.pallas_call(
        functools.partial(outer, dims),
        out_shape=jax.ShapeDtypeStruct((frames, rows // 2, out_cols * c2), bf),
        in_specs=[vmem] * 15,
        out_specs=vmem,
        scratch_shapes=[
            pltpu.VMEM((edge, first_rows, LANES), f32),
            pltpu.VMEM((edge, raw_rows, LANES), f32),
            pltpu.VMEM((edge, M1, 9 * LANES), bf),
            pltpu.VMEM((edge, M1, LANES), f32),
            pltpu.VMEM((edge, M1, LANES), f32),
            pltpu.VMEM((edge, M2, 15 * LANES), bf),
            pltpu.VMEM((edge, held, LANES), f32),
            pltpu.VMEM((edge, held, LANES), f32),
            pltpu.VMEM((out_cols, count, 15 * LANES), bf),
        ],
        compiler_params=params,
        cost_estimate=cost(2 * 10**9),
        name="outer",
    )(got_a, got_b, w1, w2m, w2r, wsc, g1, g2, wdm, wdr, *passed)


def solution(mesh):
    placed = (P("tm", "height", "width"), P(), P(), P(), P(), P(), P())
    return jax.shard_map(
        local, mesh=mesh, in_specs=placed, out_specs=P("tm", "height", "width"), check_vma=False
    )
```

```python
import functools
import jax
import jax.numpy as jnp
from jax import lax
from jax.experimental import pallas as pl
from jax.experimental.pallas import tpu as pltpu
from jax.sharding import PartitionSpec as P

epsilon = 1e-06
AXES = ("tm", "height", "width")
LANES = 128
LOW, HIGH = 2, 3
EDGE = 4


def swap_pairs(axis, parity):
    sizes = [lax.axis_size(name) for name in AXES]
    place = AXES.index(axis)
    count = sizes[place]
    pairs = []
    for t in range(sizes[0]):
        for h in range(sizes[1]):
            for w in range(sizes[2]):
                source = [t, h, w]
                target = [t, h, w]
                other = source[place] + (1 if source[place] % 2 == parity else -1)
                if 0 <= other < count:
                    target[place] = other
                elif axis == "width":
                    target[place] = other % count
                else:
                    target[2] = w ^ 1
                pairs.append(
                    tuple((p[0] * sizes[1] + p[1]) * sizes[2] + p[2] for p in (source, target))
                )
    return pairs


def swap(axis, outgoing):
    return [lax.ppermute(value, AXES, swap_pairs(axis, i)) for i, value in enumerate(outgoing)]


def rounds(axis):
    return 1 if lax.axis_size(axis) == 2 else 2


def outgoing(axis, count, to_next, to_prev):
    even = lax.axis_index(axis) % 2 == 0
    return [jnp.where(even, *pair) for pair in ((to_next, to_prev), (to_prev, to_next))[:count]]


def incoming(axis, values):
    index, count = lax.axis_index(axis), lax.axis_size(axis)
    even = index % 2 == 0
    at_even, at_odd = values[0], values[-1]
    zero = jnp.zeros_like(at_even)
    if len(values) == 1:
        return jnp.where(even, zero, at_even), jnp.where(even, at_even, zero)
    return (
        jnp.where(index == 0, zero, jnp.where(even, at_odd, at_even)),
        jnp.where(index == count - 1, zero, jnp.where(even, at_even, at_odd)),
    )


def rows_out(own, *refs):
    got, slabs, prev, wide = refs[: rounds("tm")], refs[rounds("tm") : -2], refs[-2], refs[-1]
    prev[...] = incoming("tm", [ref[...] for ref in got])[0]
    frames, rows = own.shape[0], own.shape[1]
    for i, slab in enumerate(slabs):
        for f in range(2 * frames):
            block = (prev if f < frames else own)[f % frames].astype(jnp.float32)
            part = outgoing("height", len(slabs), block[rows - HIGH :], block[:HIGH])[i]
            wide[f * HIGH : (f + 1) * HIGH, :] = part
        slab[...] = wide[...].astype(jnp.bfloat16)


def cols_out(width, own, prev, *refs):
    count = rounds("height")
    got, rim, slabs, (above, below) = refs[:count], refs[count], refs[-4:-2], refs[-2:]
    frames, rows, lanes = own.shape
    values = incoming("height", [ref[...].astype(jnp.float32) for ref in got])
    for k in range(lanes // LANES):
        tile = slice(k * LANES, (k + 1) * LANES)
        for ref, value in zip((above, below), values):
            ref[k] = value[:, tile]
        parts = [above[k, pl.ds(r, 2 * frames, stride=HIGH), :] for r in range(HIGH - LOW, HIGH)]
        parts += [below[k, pl.ds(r, 2 * frames, stride=HIGH), :] for r in range(HIGH)]
        parts.append(jnp.zeros((rim.shape[0] - len(parts) * 2 * frames, LANES), jnp.float32))
        rim[:, tile] = jnp.concatenate(parts, axis=0).astype(jnp.bfloat16)
    last = lanes - width
    for f in range(2 * frames):
        source = (prev if f < frames else own)[f % frames]
        for slab, part in zip(slabs, outgoing("width", 2, source[:, last:], source[:, :width])):
            slab[f * rows : (f + 1) * rows, :] = part
    for slab, part in zip(slabs, outgoing("width", 2, rim[:, last:], rim[:, :width])):
        slab[2 * frames * rows :, :] = part


def arrange(c1, x, gain1, gain2, shortcut, conv1, conv2, down, xv, g1, g2, wsc, w1, w2m, w2r, wdm, wdr, sems):
    c2 = g2.shape[1]
    rest = c2 - LANES
    copies = [
        pltpu.make_async_copy(x, xv, sems.at[0]),
        pltpu.make_async_copy(gain1, g1, sems.at[1]),
        pltpu.make_async_copy(gain2, g2, sems.at[2]),
        pltpu.make_async_copy(shortcut, wsc.at[pl.ds(0, c1)], sems.at[3]),
    ]
    for dc in range(3):
        moves = [
            (conv1.at[:, :, dc], w1.at[dc, :, :, pl.ds(0, c1)]),
            (conv2.at[:, :, dc, pl.ds(0, LANES)], w2m.at[dc]),
            (conv2.at[:, :, dc, pl.ds(LANES, rest)], w2r.at[dc, :, pl.ds(0, 3)]),
            (down.at[:, dc, pl.ds(0, LANES)], wdm.at[dc]),
            (down.at[:, dc, pl.ds(LANES, rest)], wdr.at[dc, pl.ds(0, 3)]),
        ]
        for i, (source, target) in enumerate(moves):
            copies.append(pltpu.make_async_copy(source, target, sems.at[4 + 5 * dc + i]))
    for copy in copies:
        copy.start()
    bf = jnp.bfloat16
    wsc[c1:] = jnp.zeros((LANES - c1, c2), bf)
    w1[:, :, :, c1:, :] = jnp.zeros((3, 3, 3, LANES - c1, c2), bf)
    w2r[:, :, 3] = jnp.zeros((3, 3, rest, c2), bf)
    wdr[:, 3] = jnp.zeros((3, rest, c2), bf)
    for copy in copies:
        copy.wait()


class Steps:
    def __init__(self, frames, rows, cols, c1, c2, w1, w2m, w2r, wsc, g1, g2):
        self.frames, self.rows, self.cols, self.c1, self.c2 = frames, rows, cols, c1, c2
        self.rest = c2 - LANES
        self.R = rows + LOW + HIGH
        self.M1 = up((frames + 1) * self.R + rows + 3, 16)
        self.M2 = up((frames - 1) * self.R + rows + 1, 16)
        self.pitch = rows + 2
        self.rim_rows = list(range(LOW)) + list(range(LOW + rows, LOW + rows + HIGH))
        self.w1, self.w2m, self.w2r, self.wsc = w1, w2m, w2r, wsc
        gap = jnp.zeros((1, LANES - c1), jnp.float32)
        self.gain1 = jnp.concatenate([g1[...], gap], axis=-1)
        self.gain2 = None if g2 is None else g2[...]
        t, h, w = [lax.axis_index(name) for name in AXES]
        starts, top, left = [i == 0 for i in (t, h, w)]
        bottom, right = [i == lax.axis_size(name) - 1 for i, name in ((h, "height"), (w, "width"))]
        p = lax.broadcasted_iota(jnp.int32, (self.M1, 1), 0)
        dead = (p < 2 * self.R) & starts
        for f in range(frames + 2):
            q = p - f * self.R
            dead |= ((q == 0) & top) | (((q == rows + 1) | (q == rows + 2)) & bottom)
        self.live1 = jnp.where(dead, 0.0, 1.0).astype(jnp.float32)
        p = lax.broadcasted_iota(jnp.int32, (self.M2, 1), 0)
        dead = p < 0
        for f in range(frames):
            dead |= (p == f * self.R + rows) & bottom
        self.live2 = jnp.where(dead, 0.0, 1.0).astype(jnp.float32)
        self.keep_left = jnp.where(left, 0.0, 1.0).astype(jnp.float32)
        self.keep_right = jnp.where(right, 0.0, 1.0).astype(jnp.float32)

    def spread(self):
        shape = (EDGE * self.c1, EDGE * LANES)
        source = lax.broadcasted_iota(jnp.int32, shape, 0)
        target = lax.broadcasted_iota(jnp.int32, shape, 1)
        slot, lane = target // LANES, target % LANES
        return jnp.where((source == slot * self.c1 + lane) & (lane < self.c1), 1.0, 0.0).astype(jnp.bfloat16)

    def unpack(self, x, spread, lo, hi):
        wide = jnp.dot(x, spread, preferred_element_type=jnp.float32)
        for k in range(lo, hi):
            v = wide[:, k * LANES : (k + 1) * LANES]
            ms = jnp.sum(v * v, axis=-1, keepdims=True) * (1.0 / self.c1)
            u = v * (0.5 * lax.rsqrt(ms + epsilon)) * self.gain1
            yield v, u + u * jnp.tanh(u)

    def place_own(self, c, v, u, first, raw):
        for f in range(2 * self.frames):
            chunk = slice(f * self.rows, (f + 1) * self.rows)
            at = f * self.R + LOW
            first[c, at : at + self.rows, :] = u[chunk]
            if f >= self.frames:
                at -= self.frames * self.R
                raw[c, at : at + self.rows, :] = v[chunk]

    def place_rim(self, c, u, first):
        n = 2 * self.frames
        for e, row in enumerate(self.rim_rows):
            value = jnp.zeros((n, LANES), jnp.float32) if u is None else u[e * n : (e + 1) * n]
            first[c, pl.ds(row, n, stride=self.R), :] = value

    def place_raw(self, c, v, raw):
        at = LOW * 2 * self.frames + self.frames
        raw[c, pl.ds(LOW + self.rows, self.frames, stride=self.R), :] = v[at : at + self.frames]

    def stack_first(self, c, first, stack, at=None):
        at = c if at is None else at
        for k in range(9):
            off = (k // 3) * self.R + k % 3
            stack[at, :, k * LANES : (k + 1) * LANES] = first[c, off : off + self.M1, :].astype(jnp.bfloat16)

    def conv_first(self, get, wanted):
        lhs = [jnp.concatenate([get(c + dc) for dc in range(3)], axis=-1) for c in wanted]
        return jnp.dot(
            jnp.concatenate(lhs, axis=0),
            self.w1[...].reshape(27 * LANES, self.c2),
            preferred_element_type=jnp.float32,
        )

    def conv_rim(self, get, wanted):
        n = 2 * self.frames
        sums = {}
        for dr in range(3):
            lhs = [jnp.concatenate([get(c + dc, dr) for dc in range(3)], axis=-1) for c in wanted]
            part = jnp.dot(
                jnp.concatenate(lhs, axis=0),
                self.w1[:, :, dr].reshape(9 * LANES, self.c2),
                preferred_element_type=jnp.float32,
            )
            tall = part.shape[0] // len(wanted)
            for block in range(3):
                row = self.rim_rows[dr + block] - dr
                for i in range(len(wanted)):
                    value = part[i * tall + block * n : i * tall + (block + 1) * n]
                    sums[i, row] = sums[i, row] + value if (i, row) in sums else value
        return sums

    def act_second(self, hid, keep):
        ms = jnp.sum(hid * hid, axis=-1, keepdims=True) * (1.0 / self.c2)
        scale = 0.5 * lax.rsqrt(ms + epsilon) * self.live1
        u = hid * (scale if keep is None else scale * keep) * self.gain2
        return u + u * jnp.tanh(u)

    def halves(self, c, value, low, high):
        count = value.shape[0]
        low[c, 0:count, :] = value[:, :LANES]
        high[c, 0:count, 0 : self.rest] = value[:, LANES:]
        high[c, 0 : count - 1, self.rest : 2 * self.rest] = value[1:, LANES:]

    def stack_second(self, c, low, high, stack):
        for k in range(9):
            off = (k // 3) * self.R + k % 3
            stack[c, :, k * LANES : (k + 1) * LANES] = low[c, off : off + self.M2, :].astype(jnp.bfloat16)
        for k in range(9, 15):
            off = (k - 9) // 2 * self.R + (k - 9) % 2 * 2
            stack[c, :, k * LANES : (k + 1) * LANES] = high[c, off : off + self.M2, :].astype(jnp.bfloat16)

    def conv_second(self, get, get_raw, wanted):
        mains = [[get(m + dc)[:, : 9 * LANES] for dc in range(3)] for m in wanted]
        rests = [[get(m + dc)[:, 9 * LANES :] for dc in range(3)] for m in wanted]
        lhs = [
            jnp.concatenate(main + rest + [get_raw(m + LOW).astype(jnp.bfloat16)], axis=-1)
            for m, main, rest in zip(wanted, mains, rests)
        ]
        rhs = [self.w2m[...].reshape(27 * LANES, self.c2), self.w2r[...].reshape(18 * LANES, self.c2)]
        return jnp.dot(
            jnp.concatenate(lhs, axis=0),
            jnp.concatenate(rhs + [self.wsc[...]], axis=0),
            preferred_element_type=jnp.float32,
        )

    def merged(self, c, value, keep, low, high):
        value = value * (self.live2 if keep is None else self.live2 * keep)
        n = self.rows + 1
        for f in range(self.frames):
            at = f * self.pitch
            chunk = value[f * self.R : f * self.R + n]
            low[c, at : at + n, :] = chunk[:, :LANES]
            high[c, at : at + n, 0 : self.rest] = chunk[:, LANES:]
            high[c, at : at + n - 1, self.rest : 2 * self.rest] = chunk[1:, LANES:]

    def down(self, lows, highs, wanted, stack, wdm, wdr, result):
        bf = jnp.bfloat16
        count = stack.shape[1]
        for j in wanted:
            for dc in range(3):
                ref, c = lows(2 * j + dc)
                for dr in range(3):
                    k = dc * 3 + dr
                    stack[j, :, k * LANES : (k + 1) * LANES] = ref[c, pl.ds(dr, count, stride=2), :].astype(bf)
                ref, c = highs(2 * j + dc)
                for half in range(2):
                    k = 9 + 2 * dc + half
                    part = ref[c, pl.ds(2 * half, count, stride=2), :]
                    stack[j, :, k * LANES : (k + 1) * LANES] = part.astype(bf)
        acc = jnp.dot(
            jnp.concatenate([stack[j] for j in wanted], axis=0),
            jnp.concatenate([wdm[...].reshape(9 * LANES, self.c2), wdr[...].reshape(6 * LANES, self.c2)], axis=0),
            preferred_element_type=jnp.float32,
        )
        for i, j in enumerate(wanted):
            result(j, acc[i * count : (i + 1) * count])


def early(dims, own, prev, g1, w1, first, raw, acc_a, acc_b, stack1):
    s = Steps(*dims, w1, None, None, None, g1, None)
    tail = 2 * s.frames * s.R
    first[:, tail:, :] = jnp.zeros((first.shape[0], first.shape[1] - tail, LANES), jnp.float32)
    spread = s.spread()
    for group in range(s.cols // EDGE):
        lanes = slice(group * EDGE * s.c1, (group + 1) * EDGE * s.c1)
        x = jnp.concatenate([prev[:, :, lanes], own[:, :, lanes]], axis=0)
        x = x.reshape(2 * s.frames * s.rows, EDGE * s.c1)
        for k, (v, u) in enumerate(s.unpack(x, spread, 0, EDGE)):
            c = group * EDGE + k
            s.place_own(c, v, u, first, raw)
            s.place_rim(c, None, first)
            s.stack_first(c, first, stack1)
    hidden = list(range(LOW, s.cols))
    step = 7
    for start in range(0, len(hidden), step):
        wanted = hidden[start : start + step]
        acc = s.conv_first(lambda c: stack1[c - LOW], wanted)
        for i, c in enumerate(wanted):
            acc_a[c - LOW, 0 : s.M1, :] = acc[i * s.M1 : (i + 1) * s.M1, :LANES]
            acc_b[c - LOW, 0 : s.M1, 0 : s.rest] = acc[i * s.M1 : (i + 1) * s.M1, LANES:]


def inner(
    dims, rim, w1, w2m, w2r, wsc, g1, g2, _first, _raw, _acc_a, _acc_b,
    first, raw, acc_a, acc_b, stack1, stack2, mer_a, mer_b, sec_a, sec_b, rims, stack_rim,
):
    s = Steps(*dims, w1, w2m, w2r, wsc, g1, g2)
    sec_b[...] = jnp.zeros_like(sec_b)
    mer_a[...] = jnp.zeros_like(mer_a)
    mer_b[...] = jnp.zeros_like(mer_b)
    spread = s.spread()
    n = 2 * s.frames
    tall = rim.shape[0]
    rims[:, tall:, :] = jnp.zeros((s.cols, rims.shape[1] - tall, LANES), jnp.float32)
    edge = [0, 1, s.cols - 2, s.cols - 1]
    for group in range(s.cols // EDGE):
        x = rim[:, group * EDGE * s.c1 : (group + 1) * EDGE * s.c1]
        for k, (v, u) in enumerate(s.unpack(x, spread, 0, EDGE)):
            c = group * EDGE + k
            rims[c, 0:tall, :] = u
            s.place_raw(c, v, raw)
            for dr in range(3):
                for dt in range(3):
                    off = dr * n + dt
                    part = rims[c, off : off + stack_rim.shape[2], :]
                    stack_rim[c, dr, :, dt * LANES : (dt + 1) * LANES] = part.astype(jnp.bfloat16)
            if c in edge:
                s.place_rim(c, u, first)
    hidden = list(range(LOW, s.cols))
    step = 7
    for start in range(0, len(hidden), step):
        wanted = hidden[start : start + step]
        gap = jnp.zeros((n, LANES - s.rest), jnp.float32)
        for (i, row), value in s.conv_rim(lambda c, dr: stack_rim[c - LOW, dr], wanted).items():
            c = wanted[i] - LOW
            acc_a[c, pl.ds(row, n, stride=s.R), :] += value[:, :LANES]
            acc_b[c, pl.ds(row, n, stride=s.R), :] += jnp.concatenate([value[:, LANES:], gap], axis=-1)
        for c in wanted:
            hid = jnp.concatenate([acc_a[c - LOW, 0 : s.M1, :], acc_b[c - LOW, 0 : s.M1, : s.rest]], axis=-1)
            s.halves(c - LOW, s.act_second(hid, None), sec_a, sec_b)
            s.stack_second(c - LOW, sec_a, sec_b, stack2)
    for i, c in enumerate(edge):
        s.stack_first(c, first, stack1, i)
    merged = list(range(LOW, s.cols - 2))
    step = 6
    for start in range(0, len(merged), step):
        wanted = merged[start : start + step]
        acc = s.conv_second(
            lambda c: stack2[c - LOW], lambda c: raw[c - LOW, LOW : LOW + s.M2, :], wanted
        )
        for i, c in enumerate(wanted):
            s.merged(c - LOW, acc[i * s.M2 : (i + 1) * s.M2], None, mer_a, mer_b)


def outer(
    dims, got_a, got_b, w1, w2m, w2r, wsc, g1, g2, wdm, wdr, in_raw, in_stack1, in_stack2, in_mer_a, in_mer_b,
    out, first, raw, stack1, sec_a, sec_b, stack2, mer_a, mer_b, stack3,
):
    s = Steps(*dims, w1, w2m, w2r, wsc, g1, g2)
    cols, M1, M2 = s.cols, s.M1, s.M2
    sec_b[...] = jnp.zeros_like(sec_b)
    mer_a[...] = jnp.zeros_like(mer_a)
    mer_b[...] = jnp.zeros_like(mer_b)
    tail = 2 * s.frames * s.R
    first[:, tail:, :] = jnp.zeros((first.shape[0], first.shape[1] - tail, LANES), jnp.float32)
    spread = s.spread()
    left, right = incoming("width", [got_a[...], got_b[...]])
    for x, lo, hi, at in ((left, EDGE - LOW, EDGE, 0), (right, 0, HIGH, LOW)):
        for k, (v, u) in enumerate(s.unpack(x, spread, lo, hi)):
            own_rows = 2 * s.frames * s.rows
            s.place_own(at + k, v[:own_rows], u[:own_rows], first, raw)
            s.place_rim(at + k, u[own_rows:], first)
            s.place_raw(at + k, v[own_rows:], raw)
            s.stack_first(at + k, first, stack1)

    def new_or(own, given, lo, hi):
        return lambda c: given(c - lo) if lo <= c < hi else own(c if c < lo else c - hi + lo)

    def store(j, value):
        n = s.rows // 2
        for f in range(s.frames):
            at = f * s.pitch // 2
            out[f, :, j * s.c2 : (j + 1) * s.c2] = value[at : at + n].astype(jnp.bfloat16)

    lows = new_or(lambda i: (mer_a, i), lambda i: (in_mer_a, i), LOW, cols - 2)
    highs = new_or(lambda i: (mer_b, i), lambda i: (in_mer_b, i), LOW, cols - 2)
    out_cols = cols // 2
    get1 = new_or(lambda i: stack1[i], lambda i: in_stack1[i if i < 2 else i - cols + 4], LOW, LOW + cols)
    get2 = new_or(lambda i: stack2[i], lambda i: in_stack2[i], LOW, cols)
    get_raw = new_or(
        lambda i: raw[i, LOW : LOW + M2, :], lambda i: in_raw[i, LOW : LOW + M2, :], LOW, LOW + cols
    )
    sides = [
        ([0, 1], [s.keep_left, None], [0, 1], [None, None], 0),
        ([cols, cols + 1, cols + 2], [None] + [s.keep_right] * 2, [cols - 2, cols - 1, cols], [None, None, s.keep_right], 2),
    ]
    for wanted, keeps, _, _, at in sides:
        acc = s.conv_first(get1, wanted)
        for i, keep in enumerate(keeps):
            s.halves(at + i, s.act_second(acc[i * M1 : (i + 1) * M1], keep), sec_a, sec_b)
            s.stack_second(at + i, sec_a, sec_b, stack2)
    s.down(lows, highs, list(range(1, out_cols - 2)), stack3, wdm, wdr, store)
    for _, _, wanted, keeps, at in sides:
        acc = s.conv_second(get2, get_raw, wanted)
        for i, keep in enumerate(keeps):
            s.merged(at + i, acc[i * M2 : (i + 1) * M2], keep, mer_a, mer_b)
    s.down(lows, highs, [0, out_cols - 2, out_cols - 1], stack3, wdm, wdr, store)


def up(n, k):
    return -(-n // k) * k


def cost(flops):
    return pl.CostEstimate(flops=flops, bytes_accessed=5 * 10**6, transcendentals=10**5)


def local(video_in, gain_first, gain_second, conv_first, conv_second, shortcut, downscale_weight):
    frames, rows, merged_cols = video_in.shape
    c1, c2 = shortcut.shape
    cols = merged_cols // c1
    rest = c2 - LANES
    dims = (frames, rows, cols, c1, c2)
    bf, f32 = jnp.bfloat16, jnp.float32
    vmem = pl.BlockSpec(memory_space=pltpu.VMEM)
    hbm = pl.BlockSpec(memory_space=pltpu.HBM)
    params = pltpu.CompilerParams(vmem_limit_bytes=14 * 1024 * 1024)
    small = pltpu.CompilerParams(vmem_limit_bytes=4 * 1024 * 1024)
    out_cols = cols // 2
    R = rows + LOW + HIGH
    M1 = up((frames + 1) * R + rows + 3, 16)
    M2 = up((frames - 1) * R + rows + 1, 16)
    first_rows = up(M1 + 2 * R + 2, 8)
    acc_rows = up(2 * frames * R, 8)
    raw_rows = up(M2 + LOW, 8)
    count = up((frames - 1) * (rows + 2) // 2 + rows // 2, 8)
    held = up(2 * count + 1, 8)

    source = [gain_first.reshape(1, c1), gain_second.reshape(1, c2), shortcut]
    source += [conv_first, conv_second, downscale_weight]
    own, g1, g2, wsc, w1, w2m, w2r, wdm, wdr = pl.pallas_call(
        functools.partial(arrange, c1),
        out_shape=[
            pltpu.VMEM(video_in.shape, bf),
            pltpu.VMEM((1, c1), f32),
            pltpu.VMEM((1, c2), f32),
            pltpu.VMEM((LANES, c2), bf),
            pltpu.VMEM((3, 3, 3, LANES, c2), bf),
            pltpu.VMEM((3, 3, 3, LANES, c2), bf),
            pltpu.VMEM((3, 3, 4, rest, c2), bf),
            pltpu.VMEM((3, 3, LANES, c2), bf),
            pltpu.VMEM((3, 4, rest, c2), bf),
        ],
        in_specs=[hbm] * 7,
        out_specs=[vmem] * 9,
        scratch_shapes=[pltpu.SemaphoreType.DMA((19,))],
        compiler_params=small,
        cost_estimate=cost(0),
        name="arrange",
    )(*[pltpu.with_memory_space_constraint(a, pltpu.HBM) for a in [video_in] + source])

    rim_tall = up((LOW + HIGH) * 2 * frames, 16)
    tall = 2 * frames * rows + rim_tall
    got = swap("tm", [video_in] * rounds("tm"))
    *slabs, prev = pl.pallas_call(
        rows_out,
        out_shape=[pltpu.VMEM((2 * frames * HIGH, merged_cols), bf)] * rounds("height")
        + [pltpu.VMEM(video_in.shape, bf)],
        in_specs=[vmem] * (1 + len(got)),
        out_specs=[vmem] * (1 + rounds("height")),
        scratch_shapes=[pltpu.VMEM((2 * frames * HIGH, merged_cols), f32)],
        compiler_params=small,
        cost_estimate=cost(0),
        name="rows_out",
    )(own, *got)
    got = swap("height", slabs)
    hid_in, mer_in = cols - 2, cols - 4
    worked = [
        pltpu.VMEM((cols, first_rows, LANES), f32),
        pltpu.VMEM((cols, raw_rows, LANES), f32),
        pltpu.VMEM((hid_in, acc_rows, LANES), f32),
        pltpu.VMEM((hid_in, acc_rows, LANES), f32),
    ]
    work = pl.pallas_call(
        functools.partial(early, dims),
        out_shape=worked,
        in_specs=[vmem] * 4,
        out_specs=[vmem] * 4,
        scratch_shapes=[pltpu.VMEM((cols, M1, 9 * LANES), bf)],
        compiler_params=params,
        cost_estimate=cost(10**9),
        name="early",
    )(own, prev, g1, w1)
    rim, *slabs = pl.pallas_call(
        functools.partial(cols_out, EDGE * c1),
        out_shape=[pltpu.VMEM((rim_tall, merged_cols), bf)] + [pltpu.VMEM((tall, EDGE * c1), bf)] * 2,
        in_specs=[vmem] * (2 + len(got)),
        out_specs=[vmem] * 3,
        scratch_shapes=[pltpu.VMEM((merged_cols // LANES, 2 * frames * HIGH, LANES), f32)] * 2,
        compiler_params=small,
        cost_estimate=cost(0),
        name="cols_out",
    )(own, prev, *got)
    got_a, got_b = swap("width", slabs)

    _, raw, _, _, *passed = pl.pallas_call(
        functools.partial(inner, dims),
        out_shape=worked
        + [
            pltpu.VMEM((4, M1, 9 * LANES), bf),
            pltpu.VMEM((hid_in, M2, 15 * LANES), bf),
            pltpu.VMEM((mer_in, held, LANES), f32),
            pltpu.VMEM((mer_in, held, LANES), f32),
        ],
        in_specs=[vmem] * 11,
        out_specs=[vmem] * 8,
        scratch_shapes=[
            pltpu.VMEM((hid_in, M1, LANES), f32),
            pltpu.VMEM((hid_in, M1, LANES), f32),
            pltpu.VMEM((cols, rim_tall + 8, LANES), f32),
            pltpu.VMEM((cols, 3, 32, 3 * LANES), bf),
        ],
        input_output_aliases={7: 0, 8: 1, 9: 2, 10: 3},
        compiler_params=params,
        cost_estimate=cost(4 * 10**9),
        name="inner",
    )(rim, w1, w2m, w2r, wsc, g1, g2, *work)
    edge = LOW + HIGH
    return pl.pallas_call(
        functools.partial(outer, dims),
        out_shape=jax.ShapeDtypeStruct((frames, rows // 2, out_cols * c2), bf),
        in_specs=[vmem] * 15,
        out_specs=vmem,
        scratch_shapes=[
            pltpu.VMEM((edge, first_rows, LANES), f32),
            pltpu.VMEM((edge, raw_rows, LANES), f32),
            pltpu.VMEM((edge, M1, 9 * LANES), bf),
            pltpu.VMEM((edge, M1, LANES), f32),
            pltpu.VMEM((edge, M1, LANES), f32),
            pltpu.VMEM((edge, M2, 15 * LANES), bf),
            pltpu.VMEM((edge, held, LANES), f32),
            pltpu.VMEM((edge, held, LANES), f32),
            pltpu.VMEM((out_cols, count, 15 * LANES), bf),
        ],
        compiler_params=params,
        cost_estimate=cost(2 * 10**9),
        name="outer",
    )(got_a, got_b, w1, w2m, w2r, wsc, g1, g2, wdm, wdr, raw, *passed)


def solution(mesh):
    placed = (P("tm", "height", "width"), P(), P(), P(), P(), P(), P())
    return jax.shard_map(
        local, mesh=mesh, in_specs=placed, out_specs=P("tm", "height", "width"), check_vma=False
    )
```

```python
import functools
import jax
import jax.numpy as jnp
from jax import lax
from jax.experimental import pallas as pl
from jax.experimental.pallas import tpu as pltpu
from jax.sharding import PartitionSpec as P

epsilon = 1e-06
AXES = ("tm", "height", "width")
LANES = 128
LOW, HIGH = 2, 3
EDGE = 4


def swap_pairs(axis, parity):
    sizes = [lax.axis_size(name) for name in AXES]
    place = AXES.index(axis)
    count = sizes[place]
    pairs = []
    for t in range(sizes[0]):
        for h in range(sizes[1]):
            for w in range(sizes[2]):
                source = [t, h, w]
                target = [t, h, w]
                other = source[place] + (1 if source[place] % 2 == parity else -1)
                if 0 <= other < count:
                    target[place] = other
                elif axis == "width":
                    target[place] = other % count
                else:
                    target[2] = w ^ 1
                pairs.append(
                    tuple((p[0] * sizes[1] + p[1]) * sizes[2] + p[2] for p in (source, target))
                )
    return pairs


def swap(axis, outgoing):
    return [lax.ppermute(value, AXES, swap_pairs(axis, i)) for i, value in enumerate(outgoing)]


def rounds(axis):
    return 1 if lax.axis_size(axis) == 2 else 2


def outgoing(axis, count, to_next, to_prev):
    even = lax.axis_index(axis) % 2 == 0
    return [jnp.where(even, *pair) for pair in ((to_next, to_prev), (to_prev, to_next))[:count]]


def incoming(axis, values):
    index, count = lax.axis_index(axis), lax.axis_size(axis)
    even = index % 2 == 0
    at_even, at_odd = values[0], values[-1]
    zero = jnp.zeros_like(at_even)
    if len(values) == 1:
        return jnp.where(even, zero, at_even), jnp.where(even, at_even, zero)
    return (
        jnp.where(index == 0, zero, jnp.where(even, at_odd, at_even)),
        jnp.where(index == count - 1, zero, jnp.where(even, at_even, at_odd)),
    )


def rows_out(own, *refs):
    got, slabs, prev, wide = refs[: rounds("tm")], refs[rounds("tm") : -2], refs[-2], refs[-1]
    prev[...] = incoming("tm", [ref[...] for ref in got[::-1]])[0]
    frames, rows = own.shape[0], own.shape[1]
    for i, slab in enumerate(slabs):
        for f in range(2 * frames):
            block = (prev if f < frames else own)[f % frames].astype(jnp.float32)
            part = outgoing("height", len(slabs), block[rows - HIGH :], block[:HIGH])[i]
            wide[f * HIGH : (f + 1) * HIGH, :] = part
        slab[...] = wide[...].astype(jnp.bfloat16)


def cols_out(width, own, prev, *refs):
    count = rounds("height")
    got, rim, slabs, (above, below) = refs[:count], refs[count], refs[-4:-2], refs[-2:]
    frames, rows, lanes = own.shape
    values = incoming("height", [ref[...].astype(jnp.float32) for ref in got])
    for k in range(lanes // LANES):
        tile = slice(k * LANES, (k + 1) * LANES)
        for ref, value in zip((above, below), values):
            ref[k] = value[:, tile]
        parts = [above[k, pl.ds(r, 2 * frames, stride=HIGH), :] for r in range(HIGH - LOW, HIGH)]
        parts += [below[k, pl.ds(r, 2 * frames, stride=HIGH), :] for r in range(HIGH)]
        parts.append(jnp.zeros((rim.shape[0] - len(parts) * 2 * frames, LANES), jnp.float32))
        rim[:, tile] = jnp.concatenate(parts, axis=0).astype(jnp.bfloat16)
    last = lanes - width
    for f in range(2 * frames):
        source = (prev if f < frames else own)[f % frames]
        for slab, part in zip(slabs, outgoing("width", 2, source[:, last:], source[:, :width])):
            slab[f * rows : (f + 1) * rows, :] = part
    for slab, part in zip(slabs, outgoing("width", 2, rim[:, last:], rim[:, :width])):
        slab[2 * frames * rows :, :] = part


def arrange(c1, x, gain1, gain2, shortcut, conv1, conv2, down, xv, g1, g2, wsc, w1, w2m, w2r, wdm, wdr, sems):
    c2 = g2.shape[1]
    rest = c2 - LANES
    copies = [
        pltpu.make_async_copy(x, xv, sems.at[0]),
        pltpu.make_async_copy(gain1, g1, sems.at[1]),
        pltpu.make_async_copy(gain2, g2, sems.at[2]),
        pltpu.make_async_copy(shortcut, wsc.at[pl.ds(0, c1)], sems.at[3]),
    ]
    for dc in range(3):
        moves = [
            (conv1.at[:, :, dc], w1.at[dc, :, :, pl.ds(0, c1)]),
            (conv2.at[:, :, dc, pl.ds(0, LANES)], w2m.at[dc]),
            (conv2.at[:, :, dc, pl.ds(LANES, rest)], w2r.at[dc, :, pl.ds(0, 3)]),
            (down.at[:, dc, pl.ds(0, LANES)], wdm.at[dc]),
            (down.at[:, dc, pl.ds(LANES, rest)], wdr.at[dc, pl.ds(0, 3)]),
        ]
        for i, (source, target) in enumerate(moves):
            copies.append(pltpu.make_async_copy(source, target, sems.at[4 + 5 * dc + i]))
    for copy in copies:
        copy.start()
    bf = jnp.bfloat16
    wsc[c1:] = jnp.zeros((LANES - c1, c2), bf)
    w1[:, :, :, c1:, :] = jnp.zeros((3, 3, 3, LANES - c1, c2), bf)
    w2r[:, :, 3] = jnp.zeros((3, 3, rest, c2), bf)
    wdr[:, 3] = jnp.zeros((3, rest, c2), bf)
    for copy in copies:
        copy.wait()


class Steps:
    def __init__(self, frames, rows, cols, c1, c2, w1, w2m, w2r, wsc, g1, g2):
        self.frames, self.rows, self.cols, self.c1, self.c2 = frames, rows, cols, c1, c2
        self.rest = c2 - LANES
        self.R = rows + LOW + HIGH
        self.M1 = up((frames + 1) * self.R + rows + 3, 16)
        self.M2 = up((frames - 1) * self.R + rows + 1, 16)
        self.pitch = rows + 2
        self.rim_rows = list(range(LOW)) + list(range(LOW + rows, LOW + rows + HIGH))
        self.w1, self.w2m, self.w2r, self.wsc = w1, w2m, w2r, wsc
        gap = jnp.zeros((1, LANES - c1), jnp.float32)
        self.gain1 = jnp.concatenate([g1[...], gap], axis=-1)
        self.gain2 = None if g2 is None else g2[...]
        t, h, w = [lax.axis_index(name) for name in AXES]
        starts, top, left = [i == 0 for i in (t, h, w)]
        bottom, right = [i == lax.axis_size(name) - 1 for i, name in ((h, "height"), (w, "width"))]
        p = lax.broadcasted_iota(jnp.int32, (self.M1, 1), 0)
        dead = (p < 2 * self.R) & starts
        for f in range(frames + 2):
            q = p - f * self.R
            dead |= ((q == 0) & top) | (((q == rows + 1) | (q == rows + 2)) & bottom)
        self.live1 = jnp.where(dead, 0.0, 1.0).astype(jnp.float32)
        p = lax.broadcasted_iota(jnp.int32, (self.M2, 1), 0)
        dead = p < 0
        for f in range(frames):
            dead |= (p == f * self.R + rows) & bottom
        self.live2 = jnp.where(dead, 0.0, 1.0).astype(jnp.float32)
        self.keep_left = jnp.where(left, 0.0, 1.0).astype(jnp.float32)
        self.keep_right = jnp.where(right, 0.0, 1.0).astype(jnp.float32)

    def spread(self):
        shape = (EDGE * self.c1, EDGE * LANES)
        source = lax.broadcasted_iota(jnp.int32, shape, 0)
        target = lax.broadcasted_iota(jnp.int32, shape, 1)
        slot, lane = target // LANES, target % LANES
        return jnp.where((source == slot * self.c1 + lane) & (lane < self.c1), 1.0, 0.0).astype(jnp.bfloat16)

    def unpack(self, x, spread, lo, hi):
        wide = jnp.dot(x, spread, preferred_element_type=jnp.float32)
        for k in range(lo, hi):
            v = wide[:, k * LANES : (k + 1) * LANES]
            ms = jnp.sum(v * v, axis=-1, keepdims=True) * (1.0 / self.c1)
            u = v * (0.5 * lax.rsqrt(ms + epsilon)) * self.gain1
            yield v, u + u * jnp.tanh(u)

    def place_own(self, c, v, u, first, raw):
        for f in range(2 * self.frames):
            chunk = slice(f * self.rows, (f + 1) * self.rows)
            at = f * self.R + LOW
            first[c, at : at + self.rows, :] = u[chunk]
            if f >= self.frames:
                at -= self.frames * self.R
                raw[c, at : at + self.rows, :] = v[chunk]

    def place_rim(self, c, u, first):
        n = 2 * self.frames
        for e, row in enumerate(self.rim_rows):
            value = jnp.zeros((n, LANES), jnp.float32) if u is None else u[e * n : (e + 1) * n]
            first[c, pl.ds(row, n, stride=self.R), :] = value

    def place_raw(self, c, v, raw):
        at = LOW * 2 * self.frames + self.frames
        raw[c, pl.ds(LOW + self.rows, self.frames, stride=self.R), :] = v[at : at + self.frames]

    def stack_first(self, c, first, stack, at=None):
        at = c if at is None else at
        for k in range(9):
            off = (k // 3) * self.R + k % 3
            stack[at, :, k * LANES : (k + 1) * LANES] = first[c, off : off + self.M1, :].astype(jnp.bfloat16)

    def conv_first(self, get, wanted):
        lhs = [jnp.concatenate([get(c + dc) for dc in range(3)], axis=-1) for c in wanted]
        return jnp.dot(
            jnp.concatenate(lhs, axis=0),
            self.w1[...].reshape(27 * LANES, self.c2),
            preferred_element_type=jnp.float32,
        )

    def conv_rim(self, get, wanted):
        n = 2 * self.frames
        sums = {}
        for dr in range(3):
            lhs = [jnp.concatenate([get(c + dc, dr) for dc in range(3)], axis=-1) for c in wanted]
            part = jnp.dot(
                jnp.concatenate(lhs, axis=0),
                self.w1[:, :, dr].reshape(9 * LANES, self.c2),
                preferred_element_type=jnp.float32,
            )
            tall = part.shape[0] // len(wanted)
            for block in range(3):
                row = self.rim_rows[dr + block] - dr
                for i in range(len(wanted)):
                    value = part[i * tall + block * n : i * tall + (block + 1) * n]
                    sums[i, row] = sums[i, row] + value if (i, row) in sums else value
        return sums

    def act_second(self, hid, keep):
        ms = jnp.sum(hid * hid, axis=-1, keepdims=True) * (1.0 / self.c2)
        scale = 0.5 * lax.rsqrt(ms + epsilon) * self.live1
        u = hid * (scale if keep is None else scale * keep) * self.gain2
        return u + u * jnp.tanh(u)

    def halves(self, c, value, low, high):
        count = value.shape[0]
        low[c, 0:count, :] = value[:, :LANES]
        high[c, 0:count, 0 : self.rest] = value[:, LANES:]
        high[c, 0 : count - 1, self.rest : 2 * self.rest] = value[1:, LANES:]

    def stack_second(self, c, low, high, stack):
        for k in range(9):
            off = (k // 3) * self.R + k % 3
            stack[c, :, k * LANES : (k + 1) * LANES] = low[c, off : off + self.M2, :].astype(jnp.bfloat16)
        for k in range(9, 15):
            off = (k - 9) // 2 * self.R + (k - 9) % 2 * 2
            stack[c, :, k * LANES : (k + 1) * LANES] = high[c, off : off + self.M2, :].astype(jnp.bfloat16)

    def conv_second(self, get, get_raw, wanted):
        mains = [[get(m + dc)[:, : 9 * LANES] for dc in range(3)] for m in wanted]
        rests = [[get(m + dc)[:, 9 * LANES :] for dc in range(3)] for m in wanted]
        lhs = [
            jnp.concatenate(main + rest + [get_raw(m + LOW).astype(jnp.bfloat16)], axis=-1)
            for m, main, rest in zip(wanted, mains, rests)
        ]
        rhs = [self.w2m[...].reshape(27 * LANES, self.c2), self.w2r[...].reshape(18 * LANES, self.c2)]
        return jnp.dot(
            jnp.concatenate(lhs, axis=0),
            jnp.concatenate(rhs + [self.wsc[...]], axis=0),
            preferred_element_type=jnp.float32,
        )

    def merged(self, c, value, keep, low, high):
        value = value * (self.live2 if keep is None else self.live2 * keep)
        n = self.rows + 1
        for f in range(self.frames):
            at = f * self.pitch
            chunk = value[f * self.R : f * self.R + n]
            low[c, at : at + n, :] = chunk[:, :LANES]
            high[c, at : at + n, 0 : self.rest] = chunk[:, LANES:]
            high[c, at : at + n - 1, self.rest : 2 * self.rest] = chunk[1:, LANES:]

    def down(self, lows, highs, wanted, stack, wdm, wdr, result):
        bf = jnp.bfloat16
        count = stack.shape[1]
        for j in wanted:
            for dc in range(3):
                ref, c = lows(2 * j + dc)
                for dr in range(3):
                    k = dc * 3 + dr
                    stack[j, :, k * LANES : (k + 1) * LANES] = ref[c, pl.ds(dr, count, stride=2), :].astype(bf)
                ref, c = highs(2 * j + dc)
                for half in range(2):
                    k = 9 + 2 * dc + half
                    part = ref[c, pl.ds(2 * half, count, stride=2), :]
                    stack[j, :, k * LANES : (k + 1) * LANES] = part.astype(bf)
        acc = jnp.dot(
            jnp.concatenate([stack[j] for j in wanted], axis=0),
            jnp.concatenate([wdm[...].reshape(9 * LANES, self.c2), wdr[...].reshape(6 * LANES, self.c2)], axis=0),
            preferred_element_type=jnp.float32,
        )
        for i, j in enumerate(wanted):
            result(j, acc[i * count : (i + 1) * count])


def early(dims, own, prev, g1, w1, first, raw, acc_a, acc_b, stack1):
    s = Steps(*dims, w1, None, None, None, g1, None)
    tail = 2 * s.frames * s.R
    first[:, tail:, :] = jnp.zeros((first.shape[0], first.shape[1] - tail, LANES), jnp.float32)
    spread = s.spread()
    for group in range(s.cols // EDGE):
        lanes = slice(group * EDGE * s.c1, (group + 1) * EDGE * s.c1)
        x = jnp.concatenate([prev[:, :, lanes], own[:, :, lanes]], axis=0)
        x = x.reshape(2 * s.frames * s.rows, EDGE * s.c1)
        for k, (v, u) in enumerate(s.unpack(x, spread, 0, EDGE)):
            c = group * EDGE + k
            s.place_own(c, v, u, first, raw)
            s.place_rim(c, None, first)
            s.stack_first(c, first, stack1)
    hidden = list(range(LOW, s.cols))
    step = 7
    for start in range(0, len(hidden), step):
        wanted = hidden[start : start + step]
        acc = s.conv_first(lambda c: stack1[c - LOW], wanted)
        for i, c in enumerate(wanted):
            acc_a[c - LOW, 0 : s.M1, :] = acc[i * s.M1 : (i + 1) * s.M1, :LANES]
            acc_b[c - LOW, 0 : s.M1, 0 : s.rest] = acc[i * s.M1 : (i + 1) * s.M1, LANES:]


def inner(
    dims, rim, w1, w2m, w2r, wsc, g1, g2, _first, _raw, _acc_a, _acc_b,
    first, raw, acc_a, acc_b, stack1, stack2, mer_a, mer_b, sec_a, sec_b, rims, stack_rim,
):
    s = Steps(*dims, w1, w2m, w2r, wsc, g1, g2)
    sec_b[...] = jnp.zeros_like(sec_b)
    mer_a[...] = jnp.zeros_like(mer_a)
    mer_b[...] = jnp.zeros_like(mer_b)
    spread = s.spread()
    n = 2 * s.frames
    tall = rim.shape[0]
    rims[:, tall:, :] = jnp.zeros((s.cols, rims.shape[1] - tall, LANES), jnp.float32)
    edge = [0, 1, s.cols - 2, s.cols - 1]
    for group in range(s.cols // EDGE):
        x = rim[:, group * EDGE * s.c1 : (group + 1) * EDGE * s.c1]
        for k, (v, u) in enumerate(s.unpack(x, spread, 0, EDGE)):
            c = group * EDGE + k
            rims[c, 0:tall, :] = u
            s.place_raw(c, v, raw)
            for dr in range(3):
                for dt in range(3):
                    off = dr * n + dt
                    part = rims[c, off : off + stack_rim.shape[2], :]
                    stack_rim[c, dr, :, dt * LANES : (dt + 1) * LANES] = part.astype(jnp.bfloat16)
            if c in edge:
                s.place_rim(c, u, first)
    hidden = list(range(LOW, s.cols))
    step = 7
    for start in range(0, len(hidden), step):
        wanted = hidden[start : start + step]
        gap = jnp.zeros((n, LANES - s.rest), jnp.float32)
        for (i, row), value in s.conv_rim(lambda c, dr: stack_rim[c - LOW, dr], wanted).items():
            c = wanted[i] - LOW
            acc_a[c, pl.ds(row, n, stride=s.R), :] += value[:, :LANES]
            acc_b[c, pl.ds(row, n, stride=s.R), :] += jnp.concatenate([value[:, LANES:], gap], axis=-1)
        for c in wanted:
            hid = jnp.concatenate([acc_a[c - LOW, 0 : s.M1, :], acc_b[c - LOW, 0 : s.M1, : s.rest]], axis=-1)
            s.halves(c - LOW, s.act_second(hid, None), sec_a, sec_b)
            s.stack_second(c - LOW, sec_a, sec_b, stack2)
    for i, c in enumerate(edge):
        s.stack_first(c, first, stack1, i)
    merged = list(range(LOW, s.cols - 2))
    step = 6
    for start in range(0, len(merged), step):
        wanted = merged[start : start + step]
        acc = s.conv_second(
            lambda c: stack2[c - LOW], lambda c: raw[c - LOW, LOW : LOW + s.M2, :], wanted
        )
        for i, c in enumerate(wanted):
            s.merged(c - LOW, acc[i * s.M2 : (i + 1) * s.M2], None, mer_a, mer_b)


def outer(
    dims, got_a, got_b, w1, w2m, w2r, wsc, g1, g2, wdm, wdr, in_raw, in_stack1, in_stack2, in_mer_a, in_mer_b,
    out, first, raw, stack1, sec_a, sec_b, stack2, mer_a, mer_b, stack3,
):
    s = Steps(*dims, w1, w2m, w2r, wsc, g1, g2)
    cols, M1, M2 = s.cols, s.M1, s.M2
    sec_b[...] = jnp.zeros_like(sec_b)
    mer_a[...] = jnp.zeros_like(mer_a)
    mer_b[...] = jnp.zeros_like(mer_b)
    tail = 2 * s.frames * s.R
    first[:, tail:, :] = jnp.zeros((first.shape[0], first.shape[1] - tail, LANES), jnp.float32)
    spread = s.spread()
    left, right = incoming("width", [got_a[...], got_b[...]])
    for x, lo, hi, at in ((left, EDGE - LOW, EDGE, 0), (right, 0, HIGH, LOW)):
        for k, (v, u) in enumerate(s.unpack(x, spread, lo, hi)):
            own_rows = 2 * s.frames * s.rows
            s.place_own(at + k, v[:own_rows], u[:own_rows], first, raw)
            s.place_rim(at + k, u[own_rows:], first)
            s.place_raw(at + k, v[own_rows:], raw)
            s.stack_first(at + k, first, stack1)

    def new_or(own, given, lo, hi):
        return lambda c: given(c - lo) if lo <= c < hi else own(c if c < lo else c - hi + lo)

    def store(j, value):
        n = s.rows // 2
        for f in range(s.frames):
            at = f * s.pitch // 2
            out[f, :, j * s.c2 : (j + 1) * s.c2] = value[at : at + n].astype(jnp.bfloat16)

    lows = new_or(lambda i: (mer_a, i), lambda i: (in_mer_a, i), LOW, cols - 2)
    highs = new_or(lambda i: (mer_b, i), lambda i: (in_mer_b, i), LOW, cols - 2)
    out_cols = cols // 2
    get1 = new_or(lambda i: stack1[i], lambda i: in_stack1[i if i < 2 else i - cols + 4], LOW, LOW + cols)
    get2 = new_or(lambda i: stack2[i], lambda i: in_stack2[i], LOW, cols)
    get_raw = new_or(
        lambda i: raw[i, LOW : LOW + M2, :], lambda i: in_raw[i, LOW : LOW + M2, :], LOW, LOW + cols
    )
    sides = [
        ([0, 1], [s.keep_left, None], [0, 1], [None, None], 0),
        ([cols, cols + 1, cols + 2], [None] + [s.keep_right] * 2, [cols - 2, cols - 1, cols], [None, None, s.keep_right], 2),
    ]
    s.down(lows, highs, list(range(1, out_cols - 2)), stack3, wdm, wdr, store)
    accs = [s.conv_first(get1, side[0]) for side in sides]
    for acc, (wanted, keeps, _, _, at) in zip(accs, sides):
        for i, keep in enumerate(keeps):
            s.halves(at + i, s.act_second(acc[i * M1 : (i + 1) * M1], keep), sec_a, sec_b)
            s.stack_second(at + i, sec_a, sec_b, stack2)
    accs = [s.conv_second(get2, get_raw, side[2]) for side in sides]
    for acc, (_, _, wanted, keeps, at) in zip(accs, sides):
        for i, keep in enumerate(keeps):
            s.merged(at + i, acc[i * M2 : (i + 1) * M2], keep, mer_a, mer_b)
    s.down(lows, highs, [0, out_cols - 2, out_cols - 1], stack3, wdm, wdr, store)


def up(n, k):
    return -(-n // k) * k


def cost(flops):
    return pl.CostEstimate(flops=flops, bytes_accessed=5 * 10**6, transcendentals=10**5)


def local(video_in, gain_first, gain_second, conv_first, conv_second, shortcut, downscale_weight):
    frames, rows, merged_cols = video_in.shape
    c1, c2 = shortcut.shape
    cols = merged_cols // c1
    rest = c2 - LANES
    dims = (frames, rows, cols, c1, c2)
    bf, f32 = jnp.bfloat16, jnp.float32
    vmem = pl.BlockSpec(memory_space=pltpu.VMEM)
    hbm = pl.BlockSpec(memory_space=pltpu.HBM)
    params = pltpu.CompilerParams(vmem_limit_bytes=14 * 1024 * 1024)
    small = pltpu.CompilerParams(vmem_limit_bytes=4 * 1024 * 1024)
    out_cols = cols // 2
    R = rows + LOW + HIGH
    M1 = up((frames + 1) * R + rows + 3, 16)
    M2 = up((frames - 1) * R + rows + 1, 16)
    first_rows = up(M1 + 2 * R + 2, 8)
    acc_rows = up(2 * frames * R, 8)
    raw_rows = up(M2 + LOW, 8)
    count = up((frames - 1) * (rows + 2) // 2 + rows // 2, 8)
    held = up(2 * count + 1, 8)

    source = [gain_first.reshape(1, c1), gain_second.reshape(1, c2), shortcut]
    source += [conv_first, conv_second, downscale_weight]
    own, g1, g2, wsc, w1, w2m, w2r, wdm, wdr = pl.pallas_call(
        functools.partial(arrange, c1),
        out_shape=[
            pltpu.VMEM(video_in.shape, bf),
            pltpu.VMEM((1, c1), f32),
            pltpu.VMEM((1, c2), f32),
            pltpu.VMEM((LANES, c2), bf),
            pltpu.VMEM((3, 3, 3, LANES, c2), bf),
            pltpu.VMEM((3, 3, 3, LANES, c2), bf),
            pltpu.VMEM((3, 3, 4, rest, c2), bf),
            pltpu.VMEM((3, 3, LANES, c2), bf),
            pltpu.VMEM((3, 4, rest, c2), bf),
        ],
        in_specs=[hbm] * 7,
        out_specs=[vmem] * 9,
        scratch_shapes=[pltpu.SemaphoreType.DMA((19,))],
        compiler_params=small,
        cost_estimate=cost(0),
        name="arrange",
    )(*[pltpu.with_memory_space_constraint(a, pltpu.HBM) for a in [video_in] + source])

    rim_tall = up((LOW + HIGH) * 2 * frames, 16)
    tall = 2 * frames * rows + rim_tall
    got = swap("tm", [video_in] * rounds("tm"))
    *slabs, prev = pl.pallas_call(
        rows_out,
        out_shape=[pltpu.VMEM((2 * frames * HIGH, merged_cols), bf)] * rounds("height")
        + [pltpu.VMEM(video_in.shape, bf)],
        in_specs=[vmem] * (1 + len(got)),
        out_specs=[vmem] * (1 + rounds("height")),
        scratch_shapes=[pltpu.VMEM((2 * frames * HIGH, merged_cols), f32)],
        compiler_params=small,
        cost_estimate=cost(0),
        name="rows_out",
    )(own, *got[::-1])
    got = swap("height", slabs)
    hid_in, mer_in = cols - 2, cols - 4
    worked = [
        pltpu.VMEM((cols, first_rows, LANES), f32),
        pltpu.VMEM((cols, raw_rows, LANES), f32),
        pltpu.VMEM((hid_in, acc_rows, LANES), f32),
        pltpu.VMEM((hid_in, acc_rows, LANES), f32),
    ]
    work = pl.pallas_call(
        functools.partial(early, dims),
        out_shape=worked,
        in_specs=[vmem] * 4,
        out_specs=[vmem] * 4,
        scratch_shapes=[pltpu.VMEM((cols, M1, 9 * LANES), bf)],
        compiler_params=params,
        cost_estimate=cost(10**9),
        name="early",
    )(own, prev, g1, w1)
    rim, *slabs = pl.pallas_call(
        functools.partial(cols_out, EDGE * c1),
        out_shape=[pltpu.VMEM((rim_tall, merged_cols), bf)] + [pltpu.VMEM((tall, EDGE * c1), bf)] * 2,
        in_specs=[vmem] * (2 + len(got)),
        out_specs=[vmem] * 3,
        scratch_shapes=[pltpu.VMEM((merged_cols // LANES, 2 * frames * HIGH, LANES), f32)] * 2,
        compiler_params=small,
        cost_estimate=cost(0),
        name="cols_out",
    )(own, prev, *got)
    got_a, got_b = swap("width", slabs)

    _, raw, _, _, *passed = pl.pallas_call(
        functools.partial(inner, dims),
        out_shape=worked
        + [
            pltpu.VMEM((4, M1, 9 * LANES), bf),
            pltpu.VMEM((hid_in, M2, 15 * LANES), bf),
            pltpu.VMEM((mer_in, held, LANES), f32),
            pltpu.VMEM((mer_in, held, LANES), f32),
        ],
        in_specs=[vmem] * 11,
        out_specs=[vmem] * 8,
        scratch_shapes=[
            pltpu.VMEM((hid_in, M1, LANES), f32),
            pltpu.VMEM((hid_in, M1, LANES), f32),
            pltpu.VMEM((cols, rim_tall + 8, LANES), f32),
            pltpu.VMEM((cols, 3, 32, 3 * LANES), bf),
        ],
        input_output_aliases={7: 0, 8: 1, 9: 2, 10: 3},
        compiler_params=params,
        cost_estimate=cost(4 * 10**9),
        name="inner",
    )(rim, w1, w2m, w2r, wsc, g1, g2, *work)
    edge = LOW + HIGH
    return pl.pallas_call(
        functools.partial(outer, dims),
        out_shape=jax.ShapeDtypeStruct((frames, rows // 2, out_cols * c2), bf),
        in_specs=[vmem] * 15,
        out_specs=vmem,
        scratch_shapes=[
            pltpu.VMEM((edge, first_rows, LANES), f32),
            pltpu.VMEM((edge, raw_rows, LANES), f32),
            pltpu.VMEM((edge, M1, 9 * LANES), bf),
            pltpu.VMEM((edge, M1, LANES), f32),
            pltpu.VMEM((edge, M1, LANES), f32),
            pltpu.VMEM((edge, M2, 15 * LANES), bf),
            pltpu.VMEM((edge, held, LANES), f32),
            pltpu.VMEM((edge, held, LANES), f32),
            pltpu.VMEM((out_cols, count, 15 * LANES), bf),
        ],
        compiler_params=params,
        cost_estimate=cost(2 * 10**9),
        name="outer",
    )(got_a, got_b, w1, w2m, w2r, wsc, g1, g2, wdm, wdr, raw, *passed)


def solution(mesh):
    placed = (P("tm", "height", "width"), P(), P(), P(), P(), P(), P())
    return jax.shard_map(
        local, mesh=mesh, in_specs=placed, out_specs=P("tm", "height", "width"), check_vma=False
    )
```

```python
import functools
import jax
import jax.numpy as jnp
from jax import lax
from jax.experimental import pallas as pl
from jax.experimental.pallas import tpu as pltpu
from jax.sharding import PartitionSpec as P

epsilon = 1e-06
AXES = ("tm", "height", "width")
LANES = 128
LOW, HIGH = 2, 3
EDGE = 4


def rounds(axis):
    if lax.axis_size(axis) == 2:
        return 1
    return 3 if axis == "tm" else 2


def round_of(axis, low):
    if axis == "tm":
        return jnp.where(low % 2 == 1, 1, low % 4) if isinstance(low, jax.Array) else (1 if low % 2 else low % 4)
    return low % 2


def swap_pairs(axis, turn):
    sizes = [lax.axis_size(name) for name in AXES]
    place = AXES.index(axis)
    count = sizes[place]
    pairs = []
    for t in range(sizes[0]):
        for h in range(sizes[1]):
            for w in range(sizes[2]):
                source = [t, h, w]
                target = [t, h, w]
                mine = source[place]
                if mine + 1 < count and round_of(axis, mine) == turn:
                    target[place] = mine + 1
                elif mine > 0 and round_of(axis, mine - 1) == turn:
                    target[place] = mine - 1
                elif axis == "width":
                    target[place] = count - 1 - mine
                else:
                    target[2] = w ^ 1
                pairs.append(
                    tuple((p[0] * sizes[1] + p[1]) * sizes[2] + p[2] for p in (source, target))
                )
    return pairs


def swap(axis, outgoing):
    return [lax.ppermute(value, AXES, swap_pairs(axis, i)) for i, value in enumerate(outgoing)]


def outgoing(axis, count, to_next, to_prev):
    even = lax.axis_index(axis) % 2 == 0
    return [jnp.where(even, *pair) for pair in ((to_next, to_prev), (to_prev, to_next))[:count]]


def incoming(axis, values):
    index, count = lax.axis_index(axis), lax.axis_size(axis)
    even = index % 2 == 0
    at_even, at_odd = values[0], values[-1]
    zero = jnp.zeros_like(at_even)
    if len(values) == 1:
        return jnp.where(even, zero, at_even), jnp.where(even, at_even, zero)
    return (
        jnp.where(index == 0, zero, jnp.where(even, at_odd, at_even)),
        jnp.where(index == count - 1, zero, jnp.where(even, at_even, at_odd)),
    )


def rows_out(own, *refs):
    got, slabs, prev, wide = refs[: rounds("tm")], refs[rounds("tm") : -2], refs[-2], refs[-1]
    index = lax.axis_index("tm")
    prev[...] = jnp.zeros(prev.shape, prev.dtype)
    for i, ref in zip([0, 2, 1] if len(got) == 3 else range(len(got)), got):

        @pl.when((index > 0) & (round_of("tm", index - 1) == i))
        def _(ref=ref):
            prev[...] = ref[...]

    frames, rows = own.shape[0], own.shape[1]
    for i, slab in enumerate(slabs):
        for f in range(2 * frames):
            block = (prev if f < frames else own)[f % frames].astype(jnp.float32)
            part = outgoing("height", len(slabs), block[rows - HIGH :], block[:HIGH])[i]
            wide[f * HIGH : (f + 1) * HIGH, :] = part
        slab[...] = wide[...].astype(jnp.bfloat16)


def cols_out(width, own, prev, *refs):
    count = rounds("height")
    got, rim, slabs, (above, below) = refs[:count], refs[count], refs[-4:-2], refs[-2:]
    frames, rows, lanes = own.shape
    values = incoming("height", [ref[...].astype(jnp.float32) for ref in got])
    for k in range(lanes // LANES):
        tile = slice(k * LANES, (k + 1) * LANES)
        for ref, value in zip((above, below), values):
            ref[k] = value[:, tile]
        parts = [above[k, pl.ds(r, 2 * frames, stride=HIGH), :] for r in range(HIGH - LOW, HIGH)]
        parts += [below[k, pl.ds(r, 2 * frames, stride=HIGH), :] for r in range(HIGH)]
        parts.append(jnp.zeros((rim.shape[0] - len(parts) * 2 * frames, LANES), jnp.float32))
        rim[:, tile] = jnp.concatenate(parts, axis=0).astype(jnp.bfloat16)
    last = lanes - width
    for f in range(2 * frames):
        source = (prev if f < frames else own)[f % frames]
        for slab, part in zip(slabs, outgoing("width", 2, source[:, last:], source[:, :width])):
            slab[f * rows : (f + 1) * rows, :] = part
    for slab, part in zip(slabs, outgoing("width", 2, rim[:, last:], rim[:, :width])):
        slab[2 * frames * rows :, :] = part


def arrange(c1, x, gain1, gain2, shortcut, conv1, conv2, down, xv, g1, g2, wsc, w1, w2m, w2r, wdm, wdr, sems):
    c2 = g2.shape[1]
    rest = c2 - LANES
    copies = [
        pltpu.make_async_copy(x, xv, sems.at[0]),
        pltpu.make_async_copy(gain1, g1, sems.at[1]),
        pltpu.make_async_copy(gain2, g2, sems.at[2]),
        pltpu.make_async_copy(shortcut, wsc.at[pl.ds(0, c1)], sems.at[3]),
    ]
    for dc in range(3):
        moves = [
            (conv1.at[:, :, dc], w1.at[dc, :, :, pl.ds(0, c1)]),
            (conv2.at[:, :, dc, pl.ds(0, LANES)], w2m.at[dc]),
            (conv2.at[:, :, dc, pl.ds(LANES, rest)], w2r.at[dc, :, pl.ds(0, 3)]),
            (down.at[:, dc, pl.ds(0, LANES)], wdm.at[dc]),
            (down.at[:, dc, pl.ds(LANES, rest)], wdr.at[dc, pl.ds(0, 3)]),
        ]
        for i, (source, target) in enumerate(moves):
            copies.append(pltpu.make_async_copy(source, target, sems.at[4 + 5 * dc + i]))
    for copy in copies:
        copy.start()
    bf = jnp.bfloat16
    wsc[c1:] = jnp.zeros((LANES - c1, c2), bf)
    w1[:, :, :, c1:, :] = jnp.zeros((3, 3, 3, LANES - c1, c2), bf)
    w2r[:, :, 3] = jnp.zeros((3, 3, rest, c2), bf)
    wdr[:, 3] = jnp.zeros((3, rest, c2), bf)
    for copy in copies:
        copy.wait()


class Steps:
    def __init__(self, frames, rows, cols, c1, c2, w1, w2m, w2r, wsc, g1, g2):
        self.frames, self.rows, self.cols, self.c1, self.c2 = frames, rows, cols, c1, c2
        self.rest = c2 - LANES
        self.R = rows + LOW + HIGH
        self.M1 = up((frames + 1) * self.R + rows + 3, 16)
        self.M2 = up((frames - 1) * self.R + rows + 1, 16)
        self.pitch = rows + 2
        self.rim_rows = list(range(LOW)) + list(range(LOW + rows, LOW + rows + HIGH))
        self.w1, self.w2m, self.w2r, self.wsc = w1, w2m, w2r, wsc
        gap = jnp.zeros((1, LANES - c1), jnp.float32)
        self.gain1 = jnp.concatenate([g1[...], gap], axis=-1)
        self.gain2 = None if g2 is None else g2[...]
        t, h, w = [lax.axis_index(name) for name in AXES]
        starts, top, left = [i == 0 for i in (t, h, w)]
        bottom, right = [i == lax.axis_size(name) - 1 for i, name in ((h, "height"), (w, "width"))]
        p = lax.broadcasted_iota(jnp.int32, (self.M1, 1), 0)
        dead = (p < 2 * self.R) & starts
        for f in range(frames + 2):
            q = p - f * self.R
            dead |= ((q == 0) & top) | (((q == rows + 1) | (q == rows + 2)) & bottom)
        self.live1 = jnp.where(dead, 0.0, 1.0).astype(jnp.float32)
        p = lax.broadcasted_iota(jnp.int32, (self.M2, 1), 0)
        dead = p < 0
        for f in range(frames):
            dead |= (p == f * self.R + rows) & bottom
        self.live2 = jnp.where(dead, 0.0, 1.0).astype(jnp.float32)
        self.keep_left = jnp.where(left, 0.0, 1.0).astype(jnp.float32)
        self.keep_right = jnp.where(right, 0.0, 1.0).astype(jnp.float32)

    def spread(self):
        shape = (EDGE * self.c1, EDGE * LANES)
        source = lax.broadcasted_iota(jnp.int32, shape, 0)
        target = lax.broadcasted_iota(jnp.int32, shape, 1)
        slot, lane = target // LANES, target % LANES
        return jnp.where((source == slot * self.c1 + lane) & (lane < self.c1), 1.0, 0.0).astype(jnp.bfloat16)

    def unpack(self, x, spread, lo, hi):
        wide = jnp.dot(x, spread, preferred_element_type=jnp.float32)
        for k in range(lo, hi):
            v = wide[:, k * LANES : (k + 1) * LANES]
            ms = jnp.sum(v * v, axis=-1, keepdims=True) * (1.0 / self.c1)
            u = v * (0.5 * lax.rsqrt(ms + epsilon)) * self.gain1
            yield v, u + u * jnp.tanh(u)

    def place_own(self, c, v, u, first, raw):
        for f in range(2 * self.frames):
            chunk = slice(f * self.rows, (f + 1) * self.rows)
            at = f * self.R + LOW
            first[c, at : at + self.rows, :] = u[chunk]
            if f >= self.frames:
                at -= self.frames * self.R
                raw[c, at : at + self.rows, :] = v[chunk]

    def place_rim(self, c, u, first):
        n = 2 * self.frames
        for e, row in enumerate(self.rim_rows):
            value = jnp.zeros((n, LANES), jnp.float32) if u is None else u[e * n : (e + 1) * n]
            first[c, pl.ds(row, n, stride=self.R), :] = value

    def place_raw(self, c, v, raw):
        at = LOW * 2 * self.frames + self.frames
        raw[c, pl.ds(LOW + self.rows, self.frames, stride=self.R), :] = v[at : at + self.frames]

    def stack_first(self, c, first, stack, at=None):
        at = c if at is None else at
        for k in range(9):
            off = (k // 3) * self.R + k % 3
            stack[at, :, k * LANES : (k + 1) * LANES] = first[c, off : off + self.M1, :].astype(jnp.bfloat16)

    def conv_first(self, get, wanted):
        lhs = [jnp.concatenate([get(c + dc) for dc in range(3)], axis=-1) for c in wanted]
        return jnp.dot(
            jnp.concatenate(lhs, axis=0),
            self.w1[...].reshape(27 * LANES, self.c2),
            preferred_element_type=jnp.float32,
        )

    def conv_rim(self, get, wanted):
        n = 2 * self.frames
        sums = {}
        for dr in range(3):
            lhs = [jnp.concatenate([get(c + dc, dr) for dc in range(3)], axis=-1) for c in wanted]
            part = jnp.dot(
                jnp.concatenate(lhs, axis=0),
                self.w1[:, :, dr].reshape(9 * LANES, self.c2),
                preferred_element_type=jnp.float32,
            )
            tall = part.shape[0] // len(wanted)
            for block in range(3):
                row = self.rim_rows[dr + block] - dr
                for i in range(len(wanted)):
                    value = part[i * tall + block * n : i * tall + (block + 1) * n]
                    sums[i, row] = sums[i, row] + value if (i, row) in sums else value
        return sums

    def act_second(self, hid, keep):
        ms = jnp.sum(hid * hid, axis=-1, keepdims=True) * (1.0 / self.c2)
        scale = 0.5 * lax.rsqrt(ms + epsilon) * self.live1
        u = hid * (scale if keep is None else scale * keep) * self.gain2
        return u + u * jnp.tanh(u)

    def halves(self, c, value, low, high):
        count = value.shape[0]
        low[c, 0:count, :] = value[:, :LANES]
        high[c, 0:count, 0 : self.rest] = value[:, LANES:]
        high[c, 0 : count - 1, self.rest : 2 * self.rest] = value[1:, LANES:]

    def stack_second(self, c, low, high, stack):
        for k in range(9):
            off = (k // 3) * self.R + k % 3
            stack[c, :, k * LANES : (k + 1) * LANES] = low[c, off : off + self.M2, :].astype(jnp.bfloat16)
        for k in range(9, 15):
            off = (k - 9) // 2 * self.R + (k - 9) % 2 * 2
            stack[c, :, k * LANES : (k + 1) * LANES] = high[c, off : off + self.M2, :].astype(jnp.bfloat16)

    def conv_second(self, get, get_raw, wanted):
        mains = [[get(m + dc)[:, : 9 * LANES] for dc in range(3)] for m in wanted]
        rests = [[get(m + dc)[:, 9 * LANES :] for dc in range(3)] for m in wanted]
        lhs = [
            jnp.concatenate(main + rest + [get_raw(m + LOW).astype(jnp.bfloat16)], axis=-1)
            for m, main, rest in zip(wanted, mains, rests)
        ]
        rhs = [self.w2m[...].reshape(27 * LANES, self.c2), self.w2r[...].reshape(18 * LANES, self.c2)]
        return jnp.dot(
            jnp.concatenate(lhs, axis=0),
            jnp.concatenate(rhs + [self.wsc[...]], axis=0),
            preferred_element_type=jnp.float32,
        )

    def merged(self, c, value, keep, low, high):
        value = value * (self.live2 if keep is None else self.live2 * keep)
        n = self.rows + 1
        for f in range(self.frames):
            at = f * self.pitch
            chunk = value[f * self.R : f * self.R + n]
            low[c, at : at + n, :] = chunk[:, :LANES]
            high[c, at : at + n, 0 : self.rest] = chunk[:, LANES:]
            high[c, at : at + n - 1, self.rest : 2 * self.rest] = chunk[1:, LANES:]

    def down(self, lows, highs, wanted, stack, wdm, wdr, result):
        bf = jnp.bfloat16
        count = stack.shape[1]
        for j in wanted:
            for dc in range(3):
                ref, c = lows(2 * j + dc)
                for dr in range(3):
                    k = dc * 3 + dr
                    stack[j, :, k * LANES : (k + 1) * LANES] = ref[c, pl.ds(dr, count, stride=2), :].astype(bf)
                ref, c = highs(2 * j + dc)
                for half in range(2):
                    k = 9 + 2 * dc + half
                    part = ref[c, pl.ds(2 * half, count, stride=2), :]
                    stack[j, :, k * LANES : (k + 1) * LANES] = part.astype(bf)
        acc = jnp.dot(
            jnp.concatenate([stack[j] for j in wanted], axis=0),
            jnp.concatenate([wdm[...].reshape(9 * LANES, self.c2), wdr[...].reshape(6 * LANES, self.c2)], axis=0),
            preferred_element_type=jnp.float32,
        )
        for i, j in enumerate(wanted):
            result(j, acc[i * count : (i + 1) * count])


def early(dims, own, prev, g1, w1, first, raw, acc_a, acc_b, stack1):
    s = Steps(*dims, w1, None, None, None, g1, None)
    tail = 2 * s.frames * s.R
    first[:, tail:, :] = jnp.zeros((first.shape[0], first.shape[1] - tail, LANES), jnp.float32)
    spread = s.spread()
    for group in range(s.cols // EDGE):
        lanes = slice(group * EDGE * s.c1, (group + 1) * EDGE * s.c1)
        x = jnp.concatenate([prev[:, :, lanes], own[:, :, lanes]], axis=0)
        x = x.reshape(2 * s.frames * s.rows, EDGE * s.c1)
        for k, (v, u) in enumerate(s.unpack(x, spread, 0, EDGE)):
            c = group * EDGE + k
            s.place_own(c, v, u, first, raw)
            s.place_rim(c, None, first)
            s.stack_first(c, first, stack1)
    hidden = list(range(LOW, s.cols))
    step = 7
    for start in range(0, len(hidden), step):
        wanted = hidden[start : start + step]
        acc = s.conv_first(lambda c: stack1[c - LOW], wanted)
        for i, c in enumerate(wanted):
            acc_a[c - LOW, 0 : s.M1, :] = acc[i * s.M1 : (i + 1) * s.M1, :LANES]
            acc_b[c - LOW, 0 : s.M1, 0 : s.rest] = acc[i * s.M1 : (i + 1) * s.M1, LANES:]


def inner(
    dims, rim, w1, w2m, w2r, wsc, g1, g2, _first, _raw, _acc_a, _acc_b,
    first, raw, acc_a, acc_b, stack1, stack2, mer_a, mer_b, sec_a, sec_b, rims, stack_rim,
):
    s = Steps(*dims, w1, w2m, w2r, wsc, g1, g2)
    sec_b[...] = jnp.zeros_like(sec_b)
    mer_a[...] = jnp.zeros_like(mer_a)
    mer_b[...] = jnp.zeros_like(mer_b)
    spread = s.spread()
    n = 2 * s.frames
    tall = rim.shape[0]
    rims[:, tall:, :] = jnp.zeros((s.cols, rims.shape[1] - tall, LANES), jnp.float32)
    edge = [0, 1, s.cols - 2, s.cols - 1]
    for group in range(s.cols // EDGE):
        x = rim[:, group * EDGE * s.c1 : (group + 1) * EDGE * s.c1]
        for k, (v, u) in enumerate(s.unpack(x, spread, 0, EDGE)):
            c = group * EDGE + k
            rims[c, 0:tall, :] = u
            s.place_raw(c, v, raw)
            for dr in range(3):
                for dt in range(3):
                    off = dr * n + dt
                    part = rims[c, off : off + stack_rim.shape[2], :]
                    stack_rim[c, dr, :, dt * LANES : (dt + 1) * LANES] = part.astype(jnp.bfloat16)
            if c in edge:
                s.place_rim(c, u, first)
    hidden = list(range(LOW, s.cols))
    step = 7
    for start in range(0, len(hidden), step):
        wanted = hidden[start : start + step]
        gap = jnp.zeros((n, LANES - s.rest), jnp.float32)
        for (i, row), value in s.conv_rim(lambda c, dr: stack_rim[c - LOW, dr], wanted).items():
            c = wanted[i] - LOW
            acc_a[c, pl.ds(row, n, stride=s.R), :] += value[:, :LANES]
            acc_b[c, pl.ds(row, n, stride=s.R), :] += jnp.concatenate([value[:, LANES:], gap], axis=-1)
        for c in wanted:
            hid = jnp.concatenate([acc_a[c - LOW, 0 : s.M1, :], acc_b[c - LOW, 0 : s.M1, : s.rest]], axis=-1)
            s.halves(c - LOW, s.act_second(hid, None), sec_a, sec_b)
            s.stack_second(c - LOW, sec_a, sec_b, stack2)
    for i, c in enumerate(edge):
        s.stack_first(c, first, stack1, i)
    merged = list(range(LOW, s.cols - 2))
    step = 6
    for start in range(0, len(merged), step):
        wanted = merged[start : start + step]
        acc = s.conv_second(
            lambda c: stack2[c - LOW], lambda c: raw[c - LOW, LOW : LOW + s.M2, :], wanted
        )
        for i, c in enumerate(wanted):
            s.merged(c - LOW, acc[i * s.M2 : (i + 1) * s.M2], None, mer_a, mer_b)


def outer(
    dims, got_b, got_a, w1, w2m, w2r, wsc, g1, g2, wdm, wdr, in_raw, in_stack1, in_stack2, in_mer_a, in_mer_b,
    out, first, raw, stack1, sec_a, sec_b, stack2, mer_a, mer_b, stack3,
):
    s = Steps(*dims, w1, w2m, w2r, wsc, g1, g2)
    cols, M1, M2 = s.cols, s.M1, s.M2
    sec_b[...] = jnp.zeros_like(sec_b)
    mer_a[...] = jnp.zeros_like(mer_a)
    mer_b[...] = jnp.zeros_like(mer_b)
    tail = 2 * s.frames * s.R
    first[:, tail:, :] = jnp.zeros((first.shape[0], first.shape[1] - tail, LANES), jnp.float32)
    spread = s.spread()
    left, right = incoming("width", [got_a[...], got_b[...]])
    for x, lo, hi, at in ((left, EDGE - LOW, EDGE, 0), (right, 0, HIGH, LOW)):
        for k, (v, u) in enumerate(s.unpack(x, spread, lo, hi)):
            own_rows = 2 * s.frames * s.rows
            s.place_own(at + k, v[:own_rows], u[:own_rows], first, raw)
            s.place_rim(at + k, u[own_rows:], first)
            s.place_raw(at + k, v[own_rows:], raw)
            s.stack_first(at + k, first, stack1)

    def new_or(own, given, lo, hi):
        return lambda c: given(c - lo) if lo <= c < hi else own(c if c < lo else c - hi + lo)

    def store(j, value):
        n = s.rows // 2
        for f in range(s.frames):
            at = f * s.pitch // 2
            out[f, :, j * s.c2 : (j + 1) * s.c2] = value[at : at + n].astype(jnp.bfloat16)

    lows = new_or(lambda i: (mer_a, i), lambda i: (in_mer_a, i), LOW, cols - 2)
    highs = new_or(lambda i: (mer_b, i), lambda i: (in_mer_b, i), LOW, cols - 2)
    out_cols = cols // 2
    get1 = new_or(lambda i: stack1[i], lambda i: in_stack1[i if i < 2 else i - cols + 4], LOW, LOW + cols)
    get2 = new_or(lambda i: stack2[i], lambda i: in_stack2[i], LOW, cols)
    get_raw = new_or(
        lambda i: raw[i, LOW : LOW + M2, :], lambda i: in_raw[i, LOW : LOW + M2, :], LOW, LOW + cols
    )
    sides = [
        ([0, 1], [s.keep_left, None], [0, 1], [None, None], 0),
        ([cols, cols + 1, cols + 2], [None] + [s.keep_right] * 2, [cols - 2, cols - 1, cols], [None, None, s.keep_right], 2),
    ]
    s.down(lows, highs, list(range(1, out_cols - 2)), stack3, wdm, wdr, store)
    accs = [s.conv_first(get1, side[0]) for side in sides]
    for acc, (wanted, keeps, _, _, at) in zip(accs, sides):
        for i, keep in enumerate(keeps):
            s.halves(at + i, s.act_second(acc[i * M1 : (i + 1) * M1], keep), sec_a, sec_b)
            s.stack_second(at + i, sec_a, sec_b, stack2)
    accs = [s.conv_second(get2, get_raw, side[2]) for side in sides]
    for acc, (_, _, wanted, keeps, at) in zip(accs, sides):
        for i, keep in enumerate(keeps):
            s.merged(at + i, acc[i * M2 : (i + 1) * M2], keep, mer_a, mer_b)
    s.down(lows, highs, [0, out_cols - 2, out_cols - 1], stack3, wdm, wdr, store)


def up(n, k):
    return -(-n // k) * k


def cost(flops):
    return pl.CostEstimate(flops=flops, bytes_accessed=5 * 10**6, transcendentals=10**5)


def local(video_in, gain_first, gain_second, conv_first, conv_second, shortcut, downscale_weight):
    frames, rows, merged_cols = video_in.shape
    c1, c2 = shortcut.shape
    cols = merged_cols // c1
    rest = c2 - LANES
    dims = (frames, rows, cols, c1, c2)
    bf, f32 = jnp.bfloat16, jnp.float32
    vmem = pl.BlockSpec(memory_space=pltpu.VMEM)
    hbm = pl.BlockSpec(memory_space=pltpu.HBM)
    params = pltpu.CompilerParams(vmem_limit_bytes=14 * 1024 * 1024)
    small = pltpu.CompilerParams(vmem_limit_bytes=4 * 1024 * 1024)
    out_cols = cols // 2
    R = rows + LOW + HIGH
    M1 = up((frames + 1) * R + rows + 3, 16)
    M2 = up((frames - 1) * R + rows + 1, 16)
    first_rows = up(M1 + 2 * R + 2, 8)
    acc_rows = up(2 * frames * R, 8)
    raw_rows = up(M2 + LOW, 8)
    count = up((frames - 1) * (rows + 2) // 2 + rows // 2, 8)
    held = up(2 * count + 1, 8)

    source = [gain_first.reshape(1, c1), gain_second.reshape(1, c2), shortcut]
    source += [conv_first, conv_second, downscale_weight]
    own, g1, g2, wsc, w1, w2m, w2r, wdm, wdr = pl.pallas_call(
        functools.partial(arrange, c1),
        out_shape=[
            pltpu.VMEM(video_in.shape, bf),
            pltpu.VMEM((1, c1), f32),
            pltpu.VMEM((1, c2), f32),
            pltpu.VMEM((LANES, c2), bf),
            pltpu.VMEM((3, 3, 3, LANES, c2), bf),
            pltpu.VMEM((3, 3, 3, LANES, c2), bf),
            pltpu.VMEM((3, 3, 4, rest, c2), bf),
            pltpu.VMEM((3, 3, LANES, c2), bf),
            pltpu.VMEM((3, 4, rest, c2), bf),
        ],
        in_specs=[hbm] * 7,
        out_specs=[vmem] * 9,
        scratch_shapes=[pltpu.SemaphoreType.DMA((19,))],
        compiler_params=small,
        cost_estimate=cost(0),
        name="arrange",
    )(*[pltpu.with_memory_space_constraint(a, pltpu.HBM) for a in [video_in] + source])

    rim_tall = up((LOW + HIGH) * 2 * frames, 16)
    tall = 2 * frames * rows + rim_tall
    got = swap("tm", [video_in] * rounds("tm"))
    *slabs, prev = pl.pallas_call(
        rows_out,
        out_shape=[pltpu.VMEM((2 * frames * HIGH, merged_cols), bf)] * rounds("height")
        + [pltpu.VMEM(video_in.shape, bf)],
        in_specs=[vmem] * (1 + len(got)),
        out_specs=[vmem] * (1 + rounds("height")),
        scratch_shapes=[pltpu.VMEM((2 * frames * HIGH, merged_cols), f32)],
        compiler_params=small,
        cost_estimate=cost(0),
        name="rows_out",
    )(own, *[got[i] for i in ([0, 2, 1] if len(got) == 3 else range(len(got)))])
    got = swap("height", slabs)
    hid_in, mer_in = cols - 2, cols - 4
    worked = [
        pltpu.VMEM((cols, first_rows, LANES), f32),
        pltpu.VMEM((cols, raw_rows, LANES), f32),
        pltpu.VMEM((hid_in, acc_rows, LANES), f32),
        pltpu.VMEM((hid_in, acc_rows, LANES), f32),
    ]
    work = pl.pallas_call(
        functools.partial(early, dims),
        out_shape=worked,
        in_specs=[vmem] * 4,
        out_specs=[vmem] * 4,
        scratch_shapes=[pltpu.VMEM((cols, M1, 9 * LANES), bf)],
        compiler_params=params,
        cost_estimate=cost(10**9),
        name="early",
    )(own, prev, g1, w1)
    rim, *slabs = pl.pallas_call(
        functools.partial(cols_out, EDGE * c1),
        out_shape=[pltpu.VMEM((rim_tall, merged_cols), bf)] + [pltpu.VMEM((tall, EDGE * c1), bf)] * 2,
        in_specs=[vmem] * (2 + len(got)),
        out_specs=[vmem] * 3,
        scratch_shapes=[pltpu.VMEM((merged_cols // LANES, 2 * frames * HIGH, LANES), f32)] * 2,
        compiler_params=small,
        cost_estimate=cost(0),
        name="cols_out",
    )(own, prev, *got)
    got_a, got_b = swap("width", slabs)

    _, raw, _, _, *passed = pl.pallas_call(
        functools.partial(inner, dims),
        out_shape=worked
        + [
            pltpu.VMEM((4, M1, 9 * LANES), bf),
            pltpu.VMEM((hid_in, M2, 15 * LANES), bf),
            pltpu.VMEM((mer_in, held, LANES), f32),
            pltpu.VMEM((mer_in, held, LANES), f32),
        ],
        in_specs=[vmem] * 11,
        out_specs=[vmem] * 8,
        scratch_shapes=[
            pltpu.VMEM((hid_in, M1, LANES), f32),
            pltpu.VMEM((hid_in, M1, LANES), f32),
            pltpu.VMEM((cols, rim_tall + 8, LANES), f32),
            pltpu.VMEM((cols, 3, 32, 3 * LANES), bf),
        ],
        input_output_aliases={7: 0, 8: 1, 9: 2, 10: 3},
        compiler_params=params,
        cost_estimate=cost(4 * 10**9),
        name="inner",
    )(rim, w1, w2m, w2r, wsc, g1, g2, *work)
    edge = LOW + HIGH
    return pl.pallas_call(
        functools.partial(outer, dims),
        out_shape=jax.ShapeDtypeStruct((frames, rows // 2, out_cols * c2), bf),
        in_specs=[vmem] * 15,
        out_specs=vmem,
        scratch_shapes=[
            pltpu.VMEM((edge, first_rows, LANES), f32),
            pltpu.VMEM((edge, raw_rows, LANES), f32),
            pltpu.VMEM((edge, M1, 9 * LANES), bf),
            pltpu.VMEM((edge, M1, LANES), f32),
            pltpu.VMEM((edge, M1, LANES), f32),
            pltpu.VMEM((edge, M2, 15 * LANES), bf),
            pltpu.VMEM((edge, held, LANES), f32),
            pltpu.VMEM((edge, held, LANES), f32),
            pltpu.VMEM((out_cols, count, 15 * LANES), bf),
        ],
        compiler_params=params,
        cost_estimate=cost(2 * 10**9),
        name="outer",
    )(got_b, got_a, w1, w2m, w2r, wsc, g1, g2, wdm, wdr, raw, *passed)


def solution(mesh):
    placed = (P("tm", "height", "width"), P(), P(), P(), P(), P(), P())
    return jax.shard_map(
        local, mesh=mesh, in_specs=placed, out_specs=P("tm", "height", "width"), check_vma=False
    )
```

```python
import functools
import jax
import jax.numpy as jnp
from jax import lax
from jax.experimental import pallas as pl
from jax.experimental.pallas import tpu as pltpu
from jax.sharding import PartitionSpec as P

epsilon = 1e-06
AXES = ("tm", "height", "width")
LANES = 128
LOW, HIGH = 2, 3
EDGE = 4


def rounds(axis):
    if lax.axis_size(axis) == 2:
        return 1
    return 3 if axis == "tm" else 2


def round_of(axis, low):
    if axis == "tm":
        return jnp.where(low % 2 == 1, 1, low % 4) if isinstance(low, jax.Array) else (1 if low % 2 else low % 4)
    return low % 2


def swap_pairs(axis, turn):
    sizes = [lax.axis_size(name) for name in AXES]
    place = AXES.index(axis)
    count = sizes[place]
    pairs = []
    for t in range(sizes[0]):
        for h in range(sizes[1]):
            for w in range(sizes[2]):
                source = [t, h, w]
                target = [t, h, w]
                mine = source[place]
                if mine + 1 < count and round_of(axis, mine) == turn:
                    target[place] = mine + 1
                elif mine > 0 and round_of(axis, mine - 1) == turn:
                    target[place] = mine - 1
                elif axis == "width":
                    target[place] = count - 1 - mine
                else:
                    target[2] = w ^ 1
                pairs.append(
                    tuple((p[0] * sizes[1] + p[1]) * sizes[2] + p[2] for p in (source, target))
                )
    return pairs


def swap(axis, outgoing):
    return [lax.ppermute(value, AXES, swap_pairs(axis, i)) for i, value in enumerate(outgoing)]


def outgoing(axis, count, to_next, to_prev):
    even = lax.axis_index(axis) % 2 == 0
    return [jnp.where(even, *pair) for pair in ((to_next, to_prev), (to_prev, to_next))[:count]]


def incoming(axis, values):
    index, count = lax.axis_index(axis), lax.axis_size(axis)
    even = index % 2 == 0
    at_even, at_odd = values[0], values[-1]
    zero = jnp.zeros_like(at_even)
    if len(values) == 1:
        return jnp.where(even, zero, at_even), jnp.where(even, at_even, zero)
    return (
        jnp.where(index == 0, zero, jnp.where(even, at_odd, at_even)),
        jnp.where(index == count - 1, zero, jnp.where(even, at_even, at_odd)),
    )


def rows_out(own, *refs):
    got, slabs, prev, wide = refs[: rounds("tm")], refs[rounds("tm") : -2], refs[-2], refs[-1]
    index = lax.axis_index("tm")
    prev[...] = jnp.zeros(prev.shape, prev.dtype)
    for i, ref in zip([0, 2, 1] if len(got) == 3 else range(len(got)), got):

        @pl.when((index > 0) & (round_of("tm", index - 1) == i))
        def _(ref=ref):
            prev[...] = ref[...]

    frames, rows = own.shape[0], own.shape[1]
    for i, slab in enumerate(slabs):
        for f in range(2 * frames):
            block = (prev if f < frames else own)[f % frames].astype(jnp.float32)
            part = outgoing("height", len(slabs), block[rows - HIGH :], block[:HIGH])[i]
            wide[f * HIGH : (f + 1) * HIGH, :] = part
        slab[...] = wide[...].astype(jnp.bfloat16)


def cols_out(width, own, prev, *refs):
    count = rounds("height")
    got, rim, slabs, (above, below) = refs[:count], refs[count], refs[-4:-2], refs[-2:]
    frames, rows, lanes = own.shape
    values = incoming("height", [ref[...].astype(jnp.float32) for ref in got])
    for k in range(lanes // LANES):
        tile = slice(k * LANES, (k + 1) * LANES)
        for ref, value in zip((above, below), values):
            ref[k] = value[:, tile]
        parts = [above[k, pl.ds(r, 2 * frames, stride=HIGH), :] for r in range(HIGH - LOW, HIGH)]
        parts += [below[k, pl.ds(r, 2 * frames, stride=HIGH), :] for r in range(HIGH)]
        parts.append(jnp.zeros((rim.shape[0] - len(parts) * 2 * frames, LANES), jnp.float32))
        rim[:, tile] = jnp.concatenate(parts, axis=0).astype(jnp.bfloat16)
    last = lanes - width
    for f in range(2 * frames):
        source = (prev if f < frames else own)[f % frames]
        for slab, part in zip(slabs, outgoing("width", 2, source[:, last:], source[:, :width])):
            slab[f * rows : (f + 1) * rows, :] = part
    for slab, part in zip(slabs, outgoing("width", 2, rim[:, last:], rim[:, :width])):
        slab[2 * frames * rows :, :] = part


def arrange(c1, x, gain1, gain2, shortcut, conv1, conv2, down, xv, g1, g2, wsc, w1, w2m, w2r, wdm, wdr, sems):
    c2 = g2.shape[1]
    rest = c2 - LANES
    copies = [
        pltpu.make_async_copy(x, xv, sems.at[0]),
        pltpu.make_async_copy(gain1, g1, sems.at[1]),
        pltpu.make_async_copy(gain2, g2, sems.at[2]),
        pltpu.make_async_copy(shortcut, wsc.at[pl.ds(0, c1)], sems.at[3]),
    ]
    for dc in range(3):
        moves = [
            (conv1.at[:, :, dc], w1.at[dc, :, :, pl.ds(0, c1)]),
            (conv2.at[:, :, dc, pl.ds(0, LANES)], w2m.at[dc]),
            (conv2.at[:, :, dc, pl.ds(LANES, rest)], w2r.at[dc, :, pl.ds(0, 3)]),
            (down.at[:, dc, pl.ds(0, LANES)], wdm.at[dc]),
            (down.at[:, dc, pl.ds(LANES, rest)], wdr.at[dc, pl.ds(0, 3)]),
        ]
        for i, (source, target) in enumerate(moves):
            copies.append(pltpu.make_async_copy(source, target, sems.at[4 + 5 * dc + i]))
    for copy in copies:
        copy.start()
    bf = jnp.bfloat16
    wsc[c1:] = jnp.zeros((LANES - c1, c2), bf)
    w1[:, :, :, c1:, :] = jnp.zeros((3, 3, 3, LANES - c1, c2), bf)
    w2r[:, :, 3] = jnp.zeros((3, 3, rest, c2), bf)
    wdr[:, 3] = jnp.zeros((3, rest, c2), bf)
    for copy in copies:
        copy.wait()


class Steps:
    def __init__(self, frames, rows, cols, c1, c2, w1, w2m, w2r, wsc, g1, g2):
        self.frames, self.rows, self.cols, self.c1, self.c2 = frames, rows, cols, c1, c2
        self.rest = c2 - LANES
        self.R = rows + LOW + HIGH
        self.M1 = up((frames + 1) * self.R + rows + 3, 16)
        self.M2 = up((frames - 1) * self.R + rows + 1, 16)
        self.pitch = rows + 2
        self.rim_rows = list(range(LOW)) + list(range(LOW + rows, LOW + rows + HIGH))
        self.w1, self.w2m, self.w2r, self.wsc = w1, w2m, w2r, wsc
        gap = jnp.zeros((1, LANES - c1), jnp.float32)
        self.gain1 = jnp.concatenate([g1[...], gap], axis=-1)
        self.gain2 = None if g2 is None else g2[...]
        t, h, w = [lax.axis_index(name) for name in AXES]
        starts, top, left = [i == 0 for i in (t, h, w)]
        bottom, right = [i == lax.axis_size(name) - 1 for i, name in ((h, "height"), (w, "width"))]
        p = lax.broadcasted_iota(jnp.int32, (self.M1, 1), 0)
        dead = (p < 2 * self.R) & starts
        for f in range(frames + 2):
            q = p - f * self.R
            dead |= ((q == 0) & top) | (((q == rows + 1) | (q == rows + 2)) & bottom)
        self.live1 = jnp.where(dead, 0.0, 1.0).astype(jnp.float32)
        p = lax.broadcasted_iota(jnp.int32, (self.M2, 1), 0)
        dead = p < 0
        for f in range(frames):
            dead |= (p == f * self.R + rows) & bottom
        self.live2 = jnp.where(dead, 0.0, 1.0).astype(jnp.float32)
        self.keep_left = jnp.where(left, 0.0, 1.0).astype(jnp.float32)
        self.keep_right = jnp.where(right, 0.0, 1.0).astype(jnp.float32)

    def spread(self):
        shape = (EDGE * self.c1, EDGE * LANES)
        source = lax.broadcasted_iota(jnp.int32, shape, 0)
        target = lax.broadcasted_iota(jnp.int32, shape, 1)
        slot, lane = target // LANES, target % LANES
        return jnp.where((source == slot * self.c1 + lane) & (lane < self.c1), 1.0, 0.0).astype(jnp.bfloat16)

    def unpack(self, x, spread, lo, hi):
        wide = jnp.dot(x, spread, preferred_element_type=jnp.float32)
        for k in range(lo, hi):
            v = wide[:, k * LANES : (k + 1) * LANES]
            ms = jnp.sum(v * v, axis=-1, keepdims=True) * (1.0 / self.c1)
            u = v * (0.5 * lax.rsqrt(ms + epsilon)) * self.gain1
            yield v, u + u * jnp.tanh(u)

    def place_own(self, c, v, u, first, raw):
        for f in range(2 * self.frames):
            chunk = slice(f * self.rows, (f + 1) * self.rows)
            at = f * self.R + LOW
            first[c, at : at + self.rows, :] = u[chunk]
            if f >= self.frames:
                at -= self.frames * self.R
                raw[c, at : at + self.rows, :] = v[chunk]

    def place_rim(self, c, u, first):
        n = 2 * self.frames
        for e, row in enumerate(self.rim_rows):
            value = jnp.zeros((n, LANES), jnp.float32) if u is None else u[e * n : (e + 1) * n]
            first[c, pl.ds(row, n, stride=self.R), :] = value

    def place_raw(self, c, v, raw):
        at = LOW * 2 * self.frames + self.frames
        raw[c, pl.ds(LOW + self.rows, self.frames, stride=self.R), :] = v[at : at + self.frames]

    def stack_first(self, c, first, stack, at=None):
        at = c if at is None else at
        for k in range(9):
            off = (k // 3) * self.R + k % 3
            stack[at, :, k * LANES : (k + 1) * LANES] = first[c, off : off + self.M1, :].astype(jnp.bfloat16)

    def conv_first(self, get, wanted):
        lhs = [jnp.concatenate([get(c + dc) for dc in range(3)], axis=-1) for c in wanted]
        return jnp.dot(
            jnp.concatenate(lhs, axis=0),
            self.w1[...].reshape(27 * LANES, self.c2),
            preferred_element_type=jnp.float32,
        )

    def conv_rim(self, get, wanted):
        n = 2 * self.frames
        sums = {}
        for dr in range(3):
            lhs = [jnp.concatenate([get(c + dc, dr) for dc in range(3)], axis=-1) for c in wanted]
            part = jnp.dot(
                jnp.concatenate(lhs, axis=0),
                self.w1[:, :, dr].reshape(9 * LANES, self.c2),
                preferred_element_type=jnp.float32,
            )
            tall = part.shape[0] // len(wanted)
            for block in range(3):
                row = self.rim_rows[dr + block] - dr
                for i in range(len(wanted)):
                    value = part[i * tall + block * n : i * tall + (block + 1) * n]
                    sums[i, row] = sums[i, row] + value if (i, row) in sums else value
        return sums

    def act_second(self, hid, keep):
        ms = jnp.sum(hid * hid, axis=-1, keepdims=True) * (1.0 / self.c2)
        scale = 0.5 * lax.rsqrt(ms + epsilon) * self.live1
        u = hid * (scale if keep is None else scale * keep) * self.gain2
        return u + u * jnp.tanh(u)

    def halves(self, c, value, low, high):
        count = value.shape[0]
        low[c, 0:count, :] = value[:, :LANES]
        high[c, 0:count, 0 : self.rest] = value[:, LANES:]
        high[c, 0 : count - 1, self.rest : 2 * self.rest] = value[1:, LANES:]

    def stack_second(self, c, low, high, stack):
        for k in range(9):
            off = (k // 3) * self.R + k % 3
            stack[c, :, k * LANES : (k + 1) * LANES] = low[c, off : off + self.M2, :].astype(jnp.bfloat16)
        for k in range(9, 15):
            off = (k - 9) // 2 * self.R + (k - 9) % 2 * 2
            stack[c, :, k * LANES : (k + 1) * LANES] = high[c, off : off + self.M2, :].astype(jnp.bfloat16)

    def conv_second(self, get, get_raw, wanted):
        mains = [[get(m + dc)[:, : 9 * LANES] for dc in range(3)] for m in wanted]
        rests = [[get(m + dc)[:, 9 * LANES :] for dc in range(3)] for m in wanted]
        lhs = [
            jnp.concatenate(main + rest + [get_raw(m + LOW).astype(jnp.bfloat16)], axis=-1)
            for m, main, rest in zip(wanted, mains, rests)
        ]
        rhs = [self.w2m[...].reshape(27 * LANES, self.c2), self.w2r[...].reshape(18 * LANES, self.c2)]
        return jnp.dot(
            jnp.concatenate(lhs, axis=0),
            jnp.concatenate(rhs + [self.wsc[...]], axis=0),
            preferred_element_type=jnp.float32,
        )

    def merged(self, c, value, keep, low, high):
        value = value * (self.live2 if keep is None else self.live2 * keep)
        n = self.rows + 1
        for f in range(self.frames):
            at = f * self.pitch
            chunk = value[f * self.R : f * self.R + n]
            low[c, at : at + n, :] = chunk[:, :LANES]
            high[c, at : at + n, 0 : self.rest] = chunk[:, LANES:]
            high[c, at : at + n - 1, self.rest : 2 * self.rest] = chunk[1:, LANES:]
            gap = jnp.zeros((1, self.rest), jnp.float32)
            high[c, at + n - 1 : at + n, self.rest : 2 * self.rest] = gap

    def down(self, lows, highs, wanted, stack, wdm, wdr, result):
        bf = jnp.bfloat16
        count = stack.shape[1]
        for j in wanted:
            for dc in range(3):
                ref, c = lows(2 * j + dc)
                for dr in range(3):
                    k = dc * 3 + dr
                    stack[j, :, k * LANES : (k + 1) * LANES] = ref[c, pl.ds(dr, count, stride=2), :].astype(bf)
                ref, c = highs(2 * j + dc)
                for half in range(2):
                    k = 9 + 2 * dc + half
                    part = ref[c, pl.ds(2 * half, count, stride=2), :]
                    stack[j, :, k * LANES : (k + 1) * LANES] = part.astype(bf)
        acc = jnp.dot(
            jnp.concatenate([stack[j] for j in wanted], axis=0),
            jnp.concatenate([wdm[...].reshape(9 * LANES, self.c2), wdr[...].reshape(6 * LANES, self.c2)], axis=0),
            preferred_element_type=jnp.float32,
        )
        for i, j in enumerate(wanted):
            result(j, acc[i * count : (i + 1) * count])


def early(dims, own, prev, g1, w1, first, raw, acc_a, acc_b, stack1):
    s = Steps(*dims, w1, None, None, None, g1, None)
    tail = 2 * s.frames * s.R
    first[:, tail:, :] = jnp.zeros((first.shape[0], first.shape[1] - tail, LANES), jnp.float32)
    spread = s.spread()
    for group in range(s.cols // EDGE):
        lanes = slice(group * EDGE * s.c1, (group + 1) * EDGE * s.c1)
        x = jnp.concatenate([prev[:, :, lanes], own[:, :, lanes]], axis=0)
        x = x.reshape(2 * s.frames * s.rows, EDGE * s.c1)
        for k, (v, u) in enumerate(s.unpack(x, spread, 0, EDGE)):
            c = group * EDGE + k
            s.place_own(c, v, u, first, raw)
            s.place_rim(c, None, first)
            s.stack_first(c, first, stack1)
    hidden = list(range(LOW, s.cols))
    step = 14
    for start in range(0, len(hidden), step):
        wanted = hidden[start : start + step]
        acc = s.conv_first(lambda c: stack1[c - LOW], wanted)
        for i, c in enumerate(wanted):
            acc_a[c - LOW, 0 : s.M1, :] = acc[i * s.M1 : (i + 1) * s.M1, :LANES]
            acc_b[c - LOW, 0 : s.M1, 0 : s.rest] = acc[i * s.M1 : (i + 1) * s.M1, LANES:]


def inner(
    dims, rim, w1, w2m, w2r, wsc, g1, g2, _first, _raw, _acc_a, _acc_b,
    first, raw, acc_a, acc_b, stack1, stack2, mer_a, mer_b, sec_a, sec_b, rims, stack_rim,
):
    s = Steps(*dims, w1, w2m, w2r, wsc, g1, g2)
    spread = s.spread()
    n = 2 * s.frames
    tall = rim.shape[0]
    rims[:, tall:, :] = jnp.zeros((s.cols, rims.shape[1] - tall, LANES), jnp.float32)
    edge = [0, 1, s.cols - 2, s.cols - 1]
    for group in range(s.cols // EDGE):
        x = rim[:, group * EDGE * s.c1 : (group + 1) * EDGE * s.c1]
        for k, (v, u) in enumerate(s.unpack(x, spread, 0, EDGE)):
            c = group * EDGE + k
            rims[c, 0:tall, :] = u
            s.place_raw(c, v, raw)
            for dr in range(3):
                for dt in range(3):
                    off = dr * n + dt
                    part = rims[c, off : off + stack_rim.shape[2], :]
                    stack_rim[c, dr, :, dt * LANES : (dt + 1) * LANES] = part.astype(jnp.bfloat16)
            if c in edge:
                s.place_rim(c, u, first)
    hidden = list(range(LOW, s.cols))
    step = 5
    for start in range(0, len(hidden), step):
        wanted = hidden[start : start + step]
        gap = jnp.zeros((n, LANES - s.rest), jnp.float32)
        for (i, row), value in s.conv_rim(lambda c, dr: stack_rim[c - LOW, dr], wanted).items():
            c = wanted[i] - LOW
            acc_a[c, pl.ds(row, n, stride=s.R), :] += value[:, :LANES]
            acc_b[c, pl.ds(row, n, stride=s.R), :] += jnp.concatenate([value[:, LANES:], gap], axis=-1)
        for c in wanted:
            hid = jnp.concatenate([acc_a[c - LOW, 0 : s.M1, :], acc_b[c - LOW, 0 : s.M1, : s.rest]], axis=-1)
            s.halves(c - LOW, s.act_second(hid, None), sec_a, sec_b)
            s.stack_second(c - LOW, sec_a, sec_b, stack2)
    for i, c in enumerate(edge):
        s.stack_first(c, first, stack1, i)
    merged = list(range(LOW, s.cols - 2))
    step = 3
    for start in range(0, len(merged), step):
        wanted = merged[start : start + step]
        acc = s.conv_second(
            lambda c: stack2[c - LOW], lambda c: raw[c - LOW, LOW : LOW + s.M2, :], wanted
        )
        for i, c in enumerate(wanted):
            s.merged(c - LOW, acc[i * s.M2 : (i + 1) * s.M2], None, mer_a, mer_b)


def outer(
    dims, got_b, got_a, w1, w2m, w2r, wsc, g1, g2, wdm, wdr, in_raw, in_stack1, in_stack2, in_mer_a, in_mer_b,
    out, first, raw, stack1, sec_a, sec_b, stack2, mer_a, mer_b, stack3,
):
    s = Steps(*dims, w1, w2m, w2r, wsc, g1, g2)
    cols, M1, M2 = s.cols, s.M1, s.M2
    tail = 2 * s.frames * s.R
    first[:, tail:, :] = jnp.zeros((first.shape[0], first.shape[1] - tail, LANES), jnp.float32)
    spread = s.spread()
    left, right = incoming("width", [got_a[...], got_b[...]])
    for x, lo, hi, at in ((left, EDGE - LOW, EDGE, 0), (right, 0, HIGH, LOW)):
        for k, (v, u) in enumerate(s.unpack(x, spread, lo, hi)):
            own_rows = 2 * s.frames * s.rows
            s.place_own(at + k, v[:own_rows], u[:own_rows], first, raw)
            s.place_rim(at + k, u[own_rows:], first)
            s.place_raw(at + k, v[own_rows:], raw)
            s.stack_first(at + k, first, stack1)

    def new_or(own, given, lo, hi):
        return lambda c: given(c - lo) if lo <= c < hi else own(c if c < lo else c - hi + lo)

    def store(j, value):
        n = s.rows // 2
        for f in range(s.frames):
            at = f * s.pitch // 2
            out[f, :, j * s.c2 : (j + 1) * s.c2] = value[at : at + n].astype(jnp.bfloat16)

    lows = new_or(lambda i: (mer_a, i), lambda i: (in_mer_a, i), LOW, cols - 2)
    highs = new_or(lambda i: (mer_b, i), lambda i: (in_mer_b, i), LOW, cols - 2)
    out_cols = cols // 2
    get1 = new_or(lambda i: stack1[i], lambda i: in_stack1[i if i < 2 else i - cols + 4], LOW, LOW + cols)
    get2 = new_or(lambda i: stack2[i], lambda i: in_stack2[i], LOW, cols)
    get_raw = new_or(
        lambda i: raw[i, LOW : LOW + M2, :], lambda i: in_raw[i, LOW : LOW + M2, :], LOW, LOW + cols
    )
    sides = [
        ([0, 1], [s.keep_left, None], [0, 1], [None, None], 0),
        ([cols, cols + 1, cols + 2], [None] + [s.keep_right] * 2, [cols - 2, cols - 1, cols], [None, None, s.keep_right], 2),
    ]
    s.down(lows, highs, list(range(1, out_cols - 2)), stack3, wdm, wdr, store)
    accs = [s.conv_first(get1, side[0]) for side in sides]
    for acc, (wanted, keeps, _, _, at) in zip(accs, sides):
        for i, keep in enumerate(keeps):
            s.halves(at + i, s.act_second(acc[i * M1 : (i + 1) * M1], keep), sec_a, sec_b)
            s.stack_second(at + i, sec_a, sec_b, stack2)
    accs = [s.conv_second(get2, get_raw, side[2]) for side in sides]
    for acc, (_, _, wanted, keeps, at) in zip(accs, sides):
        for i, keep in enumerate(keeps):
            s.merged(at + i, acc[i * M2 : (i + 1) * M2], keep, mer_a, mer_b)
    s.down(lows, highs, [0, out_cols - 2, out_cols - 1], stack3, wdm, wdr, store)


def up(n, k):
    return -(-n // k) * k


def cost(flops):
    return pl.CostEstimate(flops=flops, bytes_accessed=5 * 10**6, transcendentals=10**5)


def local(video_in, gain_first, gain_second, conv_first, conv_second, shortcut, downscale_weight):
    frames, rows, merged_cols = video_in.shape
    c1, c2 = shortcut.shape
    cols = merged_cols // c1
    rest = c2 - LANES
    dims = (frames, rows, cols, c1, c2)
    bf, f32 = jnp.bfloat16, jnp.float32
    vmem = pl.BlockSpec(memory_space=pltpu.VMEM)
    hbm = pl.BlockSpec(memory_space=pltpu.HBM)
    params = pltpu.CompilerParams(vmem_limit_bytes=14 * 1024 * 1024)
    small = pltpu.CompilerParams(vmem_limit_bytes=4 * 1024 * 1024)
    out_cols = cols // 2
    R = rows + LOW + HIGH
    M1 = up((frames + 1) * R + rows + 3, 16)
    M2 = up((frames - 1) * R + rows + 1, 16)
    first_rows = up(M1 + 2 * R + 2, 8)
    acc_rows = up(2 * frames * R, 8)
    raw_rows = up(M2 + LOW, 8)
    count = up((frames - 1) * (rows + 2) // 2 + rows // 2, 8)
    held = up(2 * count + 1, 8)

    source = [gain_first.reshape(1, c1), gain_second.reshape(1, c2), shortcut]
    source += [conv_first, conv_second, downscale_weight]
    own, g1, g2, wsc, w1, w2m, w2r, wdm, wdr = pl.pallas_call(
        functools.partial(arrange, c1),
        out_shape=[
            pltpu.VMEM(video_in.shape, bf),
            pltpu.VMEM((1, c1), f32),
            pltpu.VMEM((1, c2), f32),
            pltpu.VMEM((LANES, c2), bf),
            pltpu.VMEM((3, 3, 3, LANES, c2), bf),
            pltpu.VMEM((3, 3, 3, LANES, c2), bf),
            pltpu.VMEM((3, 3, 4, rest, c2), bf),
            pltpu.VMEM((3, 3, LANES, c2), bf),
            pltpu.VMEM((3, 4, rest, c2), bf),
        ],
        in_specs=[hbm] * 7,
        out_specs=[vmem] * 9,
        scratch_shapes=[pltpu.SemaphoreType.DMA((19,))],
        compiler_params=small,
        cost_estimate=cost(0),
        name="arrange",
    )(*[pltpu.with_memory_space_constraint(a, pltpu.HBM) for a in [video_in] + source])

    rim_tall = up((LOW + HIGH) * 2 * frames, 16)
    tall = 2 * frames * rows + rim_tall
    got = swap("tm", [video_in] * rounds("tm"))
    *slabs, prev = pl.pallas_call(
        rows_out,
        out_shape=[pltpu.VMEM((2 * frames * HIGH, merged_cols), bf)] * rounds("height")
        + [pltpu.VMEM(video_in.shape, bf)],
        in_specs=[vmem] * (1 + len(got)),
        out_specs=[vmem] * (1 + rounds("height")),
        scratch_shapes=[pltpu.VMEM((2 * frames * HIGH, merged_cols), f32)],
        compiler_params=small,
        cost_estimate=cost(0),
        name="rows_out",
    )(own, *[got[i] for i in ([0, 2, 1] if len(got) == 3 else range(len(got)))])
    got = swap("height", slabs)
    hid_in, mer_in = cols - 2, cols - 4
    worked = [
        pltpu.VMEM((cols, first_rows, LANES), f32),
        pltpu.VMEM((cols, raw_rows, LANES), f32),
        pltpu.VMEM((hid_in, acc_rows, LANES), f32),
        pltpu.VMEM((hid_in, acc_rows, LANES), f32),
    ]
    work = pl.pallas_call(
        functools.partial(early, dims),
        out_shape=worked,
        in_specs=[vmem] * 4,
        out_specs=[vmem] * 4,
        scratch_shapes=[pltpu.VMEM((cols, M1, 9 * LANES), bf)],
        compiler_params=params,
        cost_estimate=cost(10**9),
        name="early",
    )(own, prev, g1, w1)
    rim, *slabs = pl.pallas_call(
        functools.partial(cols_out, EDGE * c1),
        out_shape=[pltpu.VMEM((rim_tall, merged_cols), bf)] + [pltpu.VMEM((tall, EDGE * c1), bf)] * 2,
        in_specs=[vmem] * (2 + len(got)),
        out_specs=[vmem] * 3,
        scratch_shapes=[pltpu.VMEM((merged_cols // LANES, 2 * frames * HIGH, LANES), f32)] * 2,
        compiler_params=small,
        cost_estimate=cost(0),
        name="cols_out",
    )(own, prev, *got)
    got_a, got_b = swap("width", slabs)

    _, raw, _, _, *passed = pl.pallas_call(
        functools.partial(inner, dims),
        out_shape=worked
        + [
            pltpu.VMEM((4, M1, 9 * LANES), bf),
            pltpu.VMEM((hid_in, M2, 15 * LANES), bf),
            pltpu.VMEM((mer_in, held, LANES), f32),
            pltpu.VMEM((mer_in, held, LANES), f32),
        ],
        in_specs=[vmem] * 11,
        out_specs=[vmem] * 8,
        scratch_shapes=[
            pltpu.VMEM((hid_in, M1, LANES), f32),
            pltpu.VMEM((hid_in, M1, LANES), f32),
            pltpu.VMEM((cols, rim_tall + 8, LANES), f32),
            pltpu.VMEM((cols, 3, 32, 3 * LANES), bf),
        ],
        input_output_aliases={7: 0, 8: 1, 9: 2, 10: 3},
        compiler_params=params,
        cost_estimate=cost(4 * 10**9),
        name="inner",
    )(rim, w1, w2m, w2r, wsc, g1, g2, *work)
    edge = LOW + HIGH
    return pl.pallas_call(
        functools.partial(outer, dims),
        out_shape=jax.ShapeDtypeStruct((frames, rows // 2, out_cols * c2), bf),
        in_specs=[vmem] * 15,
        out_specs=vmem,
        scratch_shapes=[
            pltpu.VMEM((edge, first_rows, LANES), f32),
            pltpu.VMEM((edge, raw_rows, LANES), f32),
            pltpu.VMEM((edge, M1, 9 * LANES), bf),
            pltpu.VMEM((edge, M1, LANES), f32),
            pltpu.VMEM((edge, M1, LANES), f32),
            pltpu.VMEM((edge, M2, 15 * LANES), bf),
            pltpu.VMEM((edge, held, LANES), f32),
            pltpu.VMEM((edge, held, LANES), f32),
            pltpu.VMEM((out_cols, count, 15 * LANES), bf),
        ],
        compiler_params=params,
        cost_estimate=cost(2 * 10**9),
        name="outer",
    )(got_b, got_a, w1, w2m, w2r, wsc, g1, g2, wdm, wdr, raw, *passed)


def solution(mesh):
    placed = (P("tm", "height", "width"), P(), P(), P(), P(), P(), P())
    return jax.shard_map(
        local, mesh=mesh, in_specs=placed, out_specs=P("tm", "height", "width"), check_vma=False
    )
```

```python
import functools
import jax
import jax.numpy as jnp
from jax import lax
from jax.experimental import pallas as pl
from jax.experimental.pallas import tpu as pltpu
from jax.sharding import PartitionSpec as P

epsilon = 1e-06
AXES = ("tm", "height", "width")
LANES = 128
LOW, HIGH = 2, 3
EDGE = 4


def rounds(axis):
    if lax.axis_size(axis) == 2:
        return 1
    return 3 if axis == "tm" else 2


def round_of(axis, low):
    if axis == "tm":
        return jnp.where(low % 2 == 1, 1, low % 4) if isinstance(low, jax.Array) else (1 if low % 2 else low % 4)
    return low % 2


def swap_pairs(axis, turn):
    sizes = [lax.axis_size(name) for name in AXES]
    place = AXES.index(axis)
    count = sizes[place]
    pairs = []
    for t in range(sizes[0]):
        for h in range(sizes[1]):
            for w in range(sizes[2]):
                source = [t, h, w]
                target = [t, h, w]
                mine = source[place]
                if mine + 1 < count and round_of(axis, mine) == turn:
                    target[place] = mine + 1
                elif mine > 0 and round_of(axis, mine - 1) == turn:
                    target[place] = mine - 1
                elif axis == "width":
                    target[place] = count - 1 - mine
                else:
                    target[2] = w ^ 1
                pairs.append(
                    tuple((p[0] * sizes[1] + p[1]) * sizes[2] + p[2] for p in (source, target))
                )
    return pairs


def swap(axis, outgoing):
    return [lax.ppermute(value, AXES, swap_pairs(axis, i)) for i, value in enumerate(outgoing)]


def outgoing(axis, count, to_next, to_prev):
    even = lax.axis_index(axis) % 2 == 0
    return [jnp.where(even, *pair) for pair in ((to_next, to_prev), (to_prev, to_next))[:count]]


def incoming(axis, values):
    index, count = lax.axis_index(axis), lax.axis_size(axis)
    even = index % 2 == 0
    at_even, at_odd = values[0], values[-1]
    zero = jnp.zeros_like(at_even)
    if len(values) == 1:
        return jnp.where(even, zero, at_even), jnp.where(even, at_even, zero)
    return (
        jnp.where(index == 0, zero, jnp.where(even, at_odd, at_even)),
        jnp.where(index == count - 1, zero, jnp.where(even, at_even, at_odd)),
    )


def rows_out(own, *refs):
    got, slabs, prev, wide = refs[: rounds("tm")], refs[rounds("tm") : -2], refs[-2], refs[-1]
    index = lax.axis_index("tm")
    prev[...] = jnp.zeros(prev.shape, prev.dtype)
    for i, ref in zip([0, 2, 1] if len(got) == 3 else range(len(got)), got):

        @pl.when((index > 0) & (round_of("tm", index - 1) == i))
        def _(ref=ref):
            prev[...] = ref[...]

    frames, rows = own.shape[0], own.shape[1]
    for i, slab in enumerate(slabs):
        for f in range(2 * frames):
            block = (prev if f < frames else own)[f % frames].astype(jnp.float32)
            part = outgoing("height", len(slabs), block[rows - HIGH :], block[:HIGH])[i]
            wide[f * HIGH : (f + 1) * HIGH, :] = part
        slab[...] = wide[...].astype(jnp.bfloat16)


def cols_out(width, own, prev, *refs):
    count = rounds("height")
    got, rim, slabs, (above, below) = refs[:count], refs[count], refs[-4:-2], refs[-2:]
    frames, rows, lanes = own.shape
    values = incoming("height", [ref[...].astype(jnp.float32) for ref in got])
    for k in range(lanes // LANES):
        tile = slice(k * LANES, (k + 1) * LANES)
        for ref, value in zip((above, below), values):
            ref[k, 0 : 2 * frames * HIGH, :] = value[:, tile]
        parts = [above[k, pl.ds(r, 2 * frames, stride=HIGH), :] for r in range(HIGH - LOW, HIGH)]
        parts += [below[k, pl.ds(r, 2 * frames, stride=HIGH), :] for r in range(HIGH)]
        parts.append(jnp.zeros((rim.shape[0] - len(parts) * 2 * frames, LANES), jnp.float32))
        rim[:, tile] = jnp.concatenate(parts, axis=0).astype(jnp.bfloat16)
    last = lanes - width
    for f in range(2 * frames):
        source = (prev if f < frames else own)[f % frames]
        for slab, part in zip(slabs, outgoing("width", 2, source[:, last:], source[:, :width])):
            slab[f * rows : (f + 1) * rows, :] = part
    for slab, part in zip(slabs, outgoing("width", 2, rim[:, last:], rim[:, :width])):
        slab[2 * frames * rows :, :] = part


def arrange(c1, x, gain1, gain2, shortcut, conv1, conv2, down, xv, g1, g2, wsc, w1, w2m, w2r, wdm, wdr, sems):
    c2 = g2.shape[1]
    rest = c2 - LANES
    copies = [
        pltpu.make_async_copy(x, xv, sems.at[0]),
        pltpu.make_async_copy(gain1, g1, sems.at[1]),
        pltpu.make_async_copy(gain2, g2, sems.at[2]),
        pltpu.make_async_copy(shortcut, wsc.at[pl.ds(0, c1)], sems.at[3]),
    ]
    for dc in range(3):
        moves = [
            (conv1.at[:, :, dc], w1.at[dc, :, :, pl.ds(0, c1)]),
            (conv2.at[:, :, dc, pl.ds(0, LANES)], w2m.at[dc]),
            (conv2.at[:, :, dc, pl.ds(LANES, rest)], w2r.at[dc, :, pl.ds(0, 3)]),
            (down.at[:, dc, pl.ds(0, LANES)], wdm.at[dc]),
            (down.at[:, dc, pl.ds(LANES, rest)], wdr.at[dc, pl.ds(0, 3)]),
        ]
        for i, (source, target) in enumerate(moves):
            copies.append(pltpu.make_async_copy(source, target, sems.at[4 + 5 * dc + i]))
    for copy in copies:
        copy.start()
    bf = jnp.bfloat16
    wsc[c1:] = jnp.zeros((LANES - c1, c2), bf)
    w1[:, :, :, c1:, :] = jnp.zeros((3, 3, 3, LANES - c1, c2), bf)
    w2r[:, :, 3] = jnp.zeros((3, 3, rest, c2), bf)
    wdr[:, 3] = jnp.zeros((3, rest, c2), bf)
    for copy in copies:
        copy.wait()


class Steps:
    def __init__(self, frames, rows, cols, c1, c2, w1, w2m, w2r, wsc, g1, g2):
        self.frames, self.rows, self.cols, self.c1, self.c2 = frames, rows, cols, c1, c2
        self.rest = c2 - LANES
        self.R = rows + LOW + HIGH
        self.M1 = up((frames + 1) * self.R + rows + 3, 16)
        self.M2 = up((frames - 1) * self.R + rows + 1, 16)
        self.pitch = rows + 2
        self.rim_rows = list(range(LOW)) + list(range(LOW + rows, LOW + rows + HIGH))
        self.w1, self.w2m, self.w2r, self.wsc = w1, w2m, w2r, wsc
        gap = jnp.zeros((1, LANES - c1), jnp.float32)
        self.gain1 = jnp.concatenate([g1[...], gap], axis=-1)
        self.gain2 = None if g2 is None else g2[...]
        t, h, w = [lax.axis_index(name) for name in AXES]
        starts, top, left = [i == 0 for i in (t, h, w)]
        bottom, right = [i == lax.axis_size(name) - 1 for i, name in ((h, "height"), (w, "width"))]
        p = lax.broadcasted_iota(jnp.int32, (self.M1, 1), 0)
        dead = (p < 2 * self.R) & starts
        for f in range(frames + 2):
            q = p - f * self.R
            dead |= ((q == 0) & top) | (((q == rows + 1) | (q == rows + 2)) & bottom)
        self.live1 = jnp.where(dead, 0.0, 1.0).astype(jnp.float32)
        p = lax.broadcasted_iota(jnp.int32, (self.M2, 1), 0)
        dead = p < 0
        for f in range(frames):
            dead |= (p == f * self.R + rows) & bottom
        self.live2 = jnp.where(dead, 0.0, 1.0).astype(jnp.float32)
        self.keep_left = jnp.where(left, 0.0, 1.0).astype(jnp.float32)
        self.keep_right = jnp.where(right, 0.0, 1.0).astype(jnp.float32)

    def spread(self):
        shape = (EDGE * self.c1, EDGE * LANES)
        source = lax.broadcasted_iota(jnp.int32, shape, 0)
        target = lax.broadcasted_iota(jnp.int32, shape, 1)
        slot, lane = target // LANES, target % LANES
        return jnp.where((source == slot * self.c1 + lane) & (lane < self.c1), 1.0, 0.0).astype(jnp.bfloat16)

    def unpack(self, x, spread, lo, hi):
        wide = jnp.dot(x, spread, preferred_element_type=jnp.float32)
        for k in range(lo, hi):
            v = wide[:, k * LANES : (k + 1) * LANES]
            ms = jnp.sum(v * v, axis=-1, keepdims=True) * (1.0 / self.c1)
            u = v * (0.5 * lax.rsqrt(ms + epsilon)) * self.gain1
            yield v, u + u * jnp.tanh(u)

    def place_own(self, c, v, u, first, raw):
        for f in range(2 * self.frames):
            chunk = slice(f * self.rows, (f + 1) * self.rows)
            at = f * self.R + LOW
            first[c, at : at + self.rows, :] = u[chunk]
            if f >= self.frames:
                at -= self.frames * self.R
                raw[c, at : at + self.rows, :] = v[chunk]

    def place_rim(self, c, u, first):
        n = 2 * self.frames
        for e, row in enumerate(self.rim_rows):
            value = jnp.zeros((n, LANES), jnp.float32) if u is None else u[e * n : (e + 1) * n]
            first[c, pl.ds(row, n, stride=self.R), :] = value

    def place_raw(self, c, v, raw):
        at = LOW * 2 * self.frames + self.frames
        raw[c, pl.ds(LOW + self.rows, self.frames, stride=self.R), :] = v[at : at + self.frames]

    def stack_first(self, c, first, stack, at=None):
        at = c if at is None else at
        for k in range(9):
            off = (k // 3) * self.R + k % 3
            stack[at, :, k * LANES : (k + 1) * LANES] = first[c, off : off + self.M1, :].astype(jnp.bfloat16)

    def conv_first(self, get, wanted):
        lhs = [jnp.concatenate([get(c + dc) for dc in range(3)], axis=-1) for c in wanted]
        return jnp.dot(
            jnp.concatenate(lhs, axis=0),
            self.w1[...].reshape(27 * LANES, self.c2),
            preferred_element_type=jnp.float32,
        )

    def conv_rim(self, get, wanted):
        n = 2 * self.frames
        sums = {}
        for dr in range(3):
            lhs = [jnp.concatenate([get(c + dc, dr) for dc in range(3)], axis=-1) for c in wanted]
            part = jnp.dot(
                jnp.concatenate(lhs, axis=0),
                self.w1[:, :, dr].reshape(9 * LANES, self.c2),
                preferred_element_type=jnp.float32,
            )
            tall = part.shape[0] // len(wanted)
            for block in range(3):
                row = self.rim_rows[dr + block] - dr
                for i in range(len(wanted)):
                    value = part[i * tall + block * n : i * tall + (block + 1) * n]
                    sums[i, row] = sums[i, row] + value if (i, row) in sums else value
        return sums

    def act_second(self, hid, keep):
        ms = jnp.sum(hid * hid, axis=-1, keepdims=True) * (1.0 / self.c2)
        scale = 0.5 * lax.rsqrt(ms + epsilon) * self.live1
        u = hid * (scale if keep is None else scale * keep) * self.gain2
        return u + u * jnp.tanh(u)

    def halves(self, c, value, low, high):
        count = value.shape[0]
        low[c, 0:count, :] = value[:, :LANES]
        high[c, 0:count, 0 : self.rest] = value[:, LANES:]
        high[c, 0 : count - 1, self.rest : 2 * self.rest] = value[1:, LANES:]

    def stack_second(self, c, low, high, stack):
        for k in range(9):
            off = (k // 3) * self.R + k % 3
            stack[c, :, k * LANES : (k + 1) * LANES] = low[c, off : off + self.M2, :].astype(jnp.bfloat16)
        for k in range(9, 15):
            off = (k - 9) // 2 * self.R + (k - 9) % 2 * 2
            stack[c, :, k * LANES : (k + 1) * LANES] = high[c, off : off + self.M2, :].astype(jnp.bfloat16)

    def conv_second(self, get, get_raw, wanted):
        mains = [[get(m + dc)[:, : 9 * LANES] for dc in range(3)] for m in wanted]
        rests = [[get(m + dc)[:, 9 * LANES :] for dc in range(3)] for m in wanted]
        lhs = [
            jnp.concatenate(main + rest + [get_raw(m + LOW).astype(jnp.bfloat16)], axis=-1)
            for m, main, rest in zip(wanted, mains, rests)
        ]
        rhs = [self.w2m[...].reshape(27 * LANES, self.c2), self.w2r[...].reshape(18 * LANES, self.c2)]
        return jnp.dot(
            jnp.concatenate(lhs, axis=0),
            jnp.concatenate(rhs + [self.wsc[...]], axis=0),
            preferred_element_type=jnp.float32,
        )

    def merged(self, c, value, keep, low, high):
        value = value * (self.live2 if keep is None else self.live2 * keep)
        n = self.rows + 1
        for f in range(self.frames):
            at = f * self.pitch
            chunk = value[f * self.R : f * self.R + n]
            low[c, at : at + n, :] = chunk[:, :LANES]
            high[c, at : at + n, 0 : self.rest] = chunk[:, LANES:]
            high[c, at : at + n - 1, self.rest : 2 * self.rest] = chunk[1:, LANES:]
            gap = jnp.zeros((1, self.rest), jnp.float32)
            high[c, at + n - 1 : at + n, self.rest : 2 * self.rest] = gap

    def down(self, lows, highs, wanted, stack, wdm, wdr, result):
        bf = jnp.bfloat16
        count = stack.shape[1]
        for j in wanted:
            for dc in range(3):
                ref, c = lows(2 * j + dc)
                for dr in range(3):
                    k = dc * 3 + dr
                    stack[j, :, k * LANES : (k + 1) * LANES] = ref[c, pl.ds(dr, count, stride=2), :].astype(bf)
                ref, c = highs(2 * j + dc)
                for half in range(2):
                    k = 9 + 2 * dc + half
                    part = ref[c, pl.ds(2 * half, count, stride=2), :]
                    stack[j, :, k * LANES : (k + 1) * LANES] = part.astype(bf)
        acc = jnp.dot(
            jnp.concatenate([stack[j] for j in wanted], axis=0),
            jnp.concatenate([wdm[...].reshape(9 * LANES, self.c2), wdr[...].reshape(6 * LANES, self.c2)], axis=0),
            preferred_element_type=jnp.float32,
        )
        for i, j in enumerate(wanted):
            result(j, acc[i * count : (i + 1) * count])


def early(dims, own, prev, g1, w1, first, raw, acc_a, acc_b, stack1):
    s = Steps(*dims, w1, None, None, None, g1, None)
    tail = 2 * s.frames * s.R
    first[:, tail:, :] = jnp.zeros((first.shape[0], first.shape[1] - tail, LANES), jnp.float32)
    spread = s.spread()
    for group in range(s.cols // EDGE):
        lanes = slice(group * EDGE * s.c1, (group + 1) * EDGE * s.c1)
        x = jnp.concatenate([prev[:, :, lanes], own[:, :, lanes]], axis=0)
        x = x.reshape(2 * s.frames * s.rows, EDGE * s.c1)
        for k, (v, u) in enumerate(s.unpack(x, spread, 0, EDGE)):
            c = group * EDGE + k
            s.place_own(c, v, u, first, raw)
            s.place_rim(c, None, first)
            s.stack_first(c, first, stack1)
    hidden = list(range(LOW, s.cols))
    step = 14
    for start in range(0, len(hidden), step):
        wanted = hidden[start : start + step]
        acc = s.conv_first(lambda c: stack1[c - LOW], wanted)
        for i, c in enumerate(wanted):
            acc_a[c - LOW, 0 : s.M1, :] = acc[i * s.M1 : (i + 1) * s.M1, :LANES]
            acc_b[c - LOW, 0 : s.M1, 0 : s.rest] = acc[i * s.M1 : (i + 1) * s.M1, LANES:]


def inner(
    dims, rim, w1, w2m, w2r, wsc, g1, g2, _first, _raw, _acc_a, _acc_b,
    first, raw, acc_a, acc_b, stack1, stack2, mer_a, mer_b, sec_a, sec_b, rims, stack_rim,
):
    s = Steps(*dims, w1, w2m, w2r, wsc, g1, g2)
    spread = s.spread()
    n = 2 * s.frames
    tall = rim.shape[0]
    rims[:, tall:, :] = jnp.zeros((s.cols, rims.shape[1] - tall, LANES), jnp.float32)
    edge = [0, 1, s.cols - 2, s.cols - 1]
    for group in range(s.cols // EDGE):
        x = rim[:, group * EDGE * s.c1 : (group + 1) * EDGE * s.c1]
        for k, (v, u) in enumerate(s.unpack(x, spread, 0, EDGE)):
            c = group * EDGE + k
            rims[c, 0:tall, :] = u
            s.place_raw(c, v, raw)
            for dr in range(3):
                for dt in range(3):
                    off = dr * n + dt
                    part = rims[c, off : off + stack_rim.shape[2], :]
                    stack_rim[c, dr, :, dt * LANES : (dt + 1) * LANES] = part.astype(jnp.bfloat16)
            if c in edge:
                s.place_rim(c, u, first)
    hidden = list(range(LOW, s.cols))
    step = 5
    for start in range(0, len(hidden), step):
        wanted = hidden[start : start + step]
        gap = jnp.zeros((n, LANES - s.rest), jnp.float32)
        for (i, row), value in s.conv_rim(lambda c, dr: stack_rim[c - LOW, dr], wanted).items():
            c = wanted[i] - LOW
            acc_a[c, pl.ds(row, n, stride=s.R), :] += value[:, :LANES]
            acc_b[c, pl.ds(row, n, stride=s.R), :] += jnp.concatenate([value[:, LANES:], gap], axis=-1)
        for c in wanted:
            hid = jnp.concatenate([acc_a[c - LOW, 0 : s.M1, :], acc_b[c - LOW, 0 : s.M1, : s.rest]], axis=-1)
            s.halves(c - LOW, s.act_second(hid, None), sec_a, sec_b)
            s.stack_second(c - LOW, sec_a, sec_b, stack2)
    for i, c in enumerate(edge):
        s.stack_first(c, first, stack1, i)
    merged = list(range(LOW, s.cols - 2))
    step = 3
    for start in range(0, len(merged), step):
        wanted = merged[start : start + step]
        acc = s.conv_second(
            lambda c: stack2[c - LOW], lambda c: raw[c - LOW, LOW : LOW + s.M2, :], wanted
        )
        for i, c in enumerate(wanted):
            s.merged(c - LOW, acc[i * s.M2 : (i + 1) * s.M2], None, mer_a, mer_b)


def outer(
    dims, got_b, got_a, w1, w2m, w2r, wsc, g1, g2, wdm, wdr, in_raw, in_stack1, in_stack2, in_mer_a, in_mer_b,
    out, first, raw, stack1, sec_a, sec_b, stack2, mer_a, mer_b, stack3,
):
    s = Steps(*dims, w1, w2m, w2r, wsc, g1, g2)
    cols, M1, M2 = s.cols, s.M1, s.M2
    tail = 2 * s.frames * s.R
    first[:, tail:, :] = jnp.zeros((first.shape[0], first.shape[1] - tail, LANES), jnp.float32)
    spread = s.spread()
    left, right = incoming("width", [got_a[...], got_b[...]])
    for x, lo, hi, at in ((left, EDGE - LOW, EDGE, 0), (right, 0, HIGH, LOW)):
        for k, (v, u) in enumerate(s.unpack(x, spread, lo, hi)):
            own_rows = 2 * s.frames * s.rows
            s.place_own(at + k, v[:own_rows], u[:own_rows], first, raw)
            s.place_rim(at + k, u[own_rows:], first)
            s.place_raw(at + k, v[own_rows:], raw)
            s.stack_first(at + k, first, stack1)

    def new_or(own, given, lo, hi):
        return lambda c: given(c - lo) if lo <= c < hi else own(c if c < lo else c - hi + lo)

    def store(j, value):
        n = s.rows // 2
        for f in range(s.frames):
            at = f * s.pitch // 2
            out[f, :, j * s.c2 : (j + 1) * s.c2] = value[at : at + n].astype(jnp.bfloat16)

    lows = new_or(lambda i: (mer_a, i), lambda i: (in_mer_a, i), LOW, cols - 2)
    highs = new_or(lambda i: (mer_b, i), lambda i: (in_mer_b, i), LOW, cols - 2)
    out_cols = cols // 2
    get1 = new_or(lambda i: stack1[i], lambda i: in_stack1[i if i < 2 else i - cols + 4], LOW, LOW + cols)
    get2 = new_or(lambda i: stack2[i], lambda i: in_stack2[i], LOW, cols)
    get_raw = new_or(
        lambda i: raw[i, LOW : LOW + M2, :], lambda i: in_raw[i, LOW : LOW + M2, :], LOW, LOW + cols
    )
    sides = [
        ([0, 1], [s.keep_left, None], [0, 1], [None, None], 0),
        ([cols, cols + 1, cols + 2], [None] + [s.keep_right] * 2, [cols - 2, cols - 1, cols], [None, None, s.keep_right], 2),
    ]
    s.down(lows, highs, list(range(1, out_cols - 2)), stack3, wdm, wdr, store)
    accs = [s.conv_first(get1, side[0]) for side in sides]
    for acc, (wanted, keeps, _, _, at) in zip(accs, sides):
        for i, keep in enumerate(keeps):
            s.halves(at + i, s.act_second(acc[i * M1 : (i + 1) * M1], keep), sec_a, sec_b)
            s.stack_second(at + i, sec_a, sec_b, stack2)
    accs = [s.conv_second(get2, get_raw, side[2]) for side in sides]
    for acc, (_, _, wanted, keeps, at) in zip(accs, sides):
        for i, keep in enumerate(keeps):
            s.merged(at + i, acc[i * M2 : (i + 1) * M2], keep, mer_a, mer_b)
    s.down(lows, highs, [0, out_cols - 2, out_cols - 1], stack3, wdm, wdr, store)


def up(n, k):
    return -(-n // k) * k


def cost(flops):
    return pl.CostEstimate(flops=flops, bytes_accessed=5 * 10**6, transcendentals=10**5)


def local(video_in, gain_first, gain_second, conv_first, conv_second, shortcut, downscale_weight):
    frames, rows, merged_cols = video_in.shape
    c1, c2 = shortcut.shape
    cols = merged_cols // c1
    rest = c2 - LANES
    dims = (frames, rows, cols, c1, c2)
    bf, f32 = jnp.bfloat16, jnp.float32
    vmem = pl.BlockSpec(memory_space=pltpu.VMEM)
    hbm = pl.BlockSpec(memory_space=pltpu.HBM)
    params = pltpu.CompilerParams(vmem_limit_bytes=14 * 1024 * 1024)
    small = pltpu.CompilerParams(vmem_limit_bytes=4 * 1024 * 1024)
    out_cols = cols // 2
    R = rows + LOW + HIGH
    M1 = up((frames + 1) * R + rows + 3, 16)
    M2 = up((frames - 1) * R + rows + 1, 16)
    first_rows = up(max(M1 + 2 * R + 2, (2 * frames + 1) * R), 8)
    acc_rows = up((2 * frames + 1) * R, 8)
    raw_rows = up(max(M2 + LOW, (frames + 1) * R), 8)
    count = up((frames - 1) * (rows + 2) // 2 + rows // 2, 8)
    held = up(2 * count + 1, 8)

    source = [gain_first.reshape(1, c1), gain_second.reshape(1, c2), shortcut]
    source += [conv_first, conv_second, downscale_weight]
    own, g1, g2, wsc, w1, w2m, w2r, wdm, wdr = pl.pallas_call(
        functools.partial(arrange, c1),
        out_shape=[
            pltpu.VMEM(video_in.shape, bf),
            pltpu.VMEM((1, c1), f32),
            pltpu.VMEM((1, c2), f32),
            pltpu.VMEM((LANES, c2), bf),
            pltpu.VMEM((3, 3, 3, LANES, c2), bf),
            pltpu.VMEM((3, 3, 3, LANES, c2), bf),
            pltpu.VMEM((3, 3, 4, rest, c2), bf),
            pltpu.VMEM((3, 3, LANES, c2), bf),
            pltpu.VMEM((3, 4, rest, c2), bf),
        ],
        in_specs=[hbm] * 7,
        out_specs=[vmem] * 9,
        scratch_shapes=[pltpu.SemaphoreType.DMA((19,))],
        compiler_params=small,
        cost_estimate=cost(0),
        name="arrange",
    )(*[pltpu.with_memory_space_constraint(a, pltpu.HBM) for a in [video_in] + source])

    rim_tall = up((LOW + HIGH) * 2 * frames, 16)
    tall = 2 * frames * rows + rim_tall
    got = swap("tm", [video_in] * rounds("tm"))
    *slabs, prev = pl.pallas_call(
        rows_out,
        out_shape=[pltpu.VMEM((2 * frames * HIGH, merged_cols), bf)] * rounds("height")
        + [pltpu.VMEM(video_in.shape, bf)],
        in_specs=[vmem] * (1 + len(got)),
        out_specs=[vmem] * (1 + rounds("height")),
        scratch_shapes=[pltpu.VMEM((2 * frames * HIGH, merged_cols), f32)],
        compiler_params=small,
        cost_estimate=cost(0),
        name="rows_out",
    )(own, *[got[i] for i in ([0, 2, 1] if len(got) == 3 else range(len(got)))])
    got = swap("height", slabs)
    hid_in, mer_in = cols - 2, cols - 4
    worked = [
        pltpu.VMEM((cols, first_rows, LANES), f32),
        pltpu.VMEM((cols, raw_rows, LANES), f32),
        pltpu.VMEM((hid_in, acc_rows, LANES), f32),
        pltpu.VMEM((hid_in, acc_rows, LANES), f32),
    ]
    work = pl.pallas_call(
        functools.partial(early, dims),
        out_shape=worked,
        in_specs=[vmem] * 4,
        out_specs=[vmem] * 4,
        scratch_shapes=[pltpu.VMEM((cols, M1, 9 * LANES), bf)],
        compiler_params=params,
        cost_estimate=cost(10**9),
        name="early",
    )(own, prev, g1, w1)
    rim, *slabs = pl.pallas_call(
        functools.partial(cols_out, EDGE * c1),
        out_shape=[pltpu.VMEM((rim_tall, merged_cols), bf)] + [pltpu.VMEM((tall, EDGE * c1), bf)] * 2,
        in_specs=[vmem] * (2 + len(got)),
        out_specs=[vmem] * 3,
        scratch_shapes=[pltpu.VMEM((merged_cols // LANES, up((2 * frames + 1) * HIGH, 8), LANES), f32)] * 2,
        compiler_params=small,
        cost_estimate=cost(0),
        name="cols_out",
    )(own, prev, *got)
    got_a, got_b = swap("width", slabs)

    _, raw, _, _, *passed = pl.pallas_call(
        functools.partial(inner, dims),
        out_shape=worked
        + [
            pltpu.VMEM((4, M1, 9 * LANES), bf),
            pltpu.VMEM((hid_in, M2, 15 * LANES), bf),
            pltpu.VMEM((mer_in, held, LANES), f32),
            pltpu.VMEM((mer_in, held, LANES), f32),
        ],
        in_specs=[vmem] * 11,
        out_specs=[vmem] * 8,
        scratch_shapes=[
            pltpu.VMEM((hid_in, M1, LANES), f32),
            pltpu.VMEM((hid_in, M1, LANES), f32),
            pltpu.VMEM((cols, rim_tall + 8, LANES), f32),
            pltpu.VMEM((cols, 3, 32, 3 * LANES), bf),
        ],
        input_output_aliases={7: 0, 8: 1, 9: 2, 10: 3},
        compiler_params=params,
        cost_estimate=cost(4 * 10**9),
        name="inner",
    )(rim, w1, w2m, w2r, wsc, g1, g2, *work)
    edge = LOW + HIGH
    return pl.pallas_call(
        functools.partial(outer, dims),
        out_shape=jax.ShapeDtypeStruct((frames, rows // 2, out_cols * c2), bf),
        in_specs=[vmem] * 15,
        out_specs=vmem,
        scratch_shapes=[
            pltpu.VMEM((edge, first_rows, LANES), f32),
            pltpu.VMEM((edge, raw_rows, LANES), f32),
            pltpu.VMEM((edge, M1, 9 * LANES), bf),
            pltpu.VMEM((edge, M1, LANES), f32),
            pltpu.VMEM((edge, M1, LANES), f32),
            pltpu.VMEM((edge, M2, 15 * LANES), bf),
            pltpu.VMEM((edge, held, LANES), f32),
            pltpu.VMEM((edge, held, LANES), f32),
            pltpu.VMEM((out_cols, count, 15 * LANES), bf),
        ],
        compiler_params=params,
        cost_estimate=cost(2 * 10**9),
        name="outer",
    )(got_b, got_a, w1, w2m, w2r, wsc, g1, g2, wdm, wdr, raw, *passed)


def solution(mesh):
    placed = (P("tm", "height", "width"), P(), P(), P(), P(), P(), P())
    return jax.shard_map(
        local, mesh=mesh, in_specs=placed, out_specs=P("tm", "height", "width"), check_vma=False
    )
```

```python
import functools
import jax
import jax.numpy as jnp
from jax import lax
from jax.experimental import pallas as pl
from jax.experimental.pallas import tpu as pltpu
from jax.sharding import PartitionSpec as P

epsilon = 1e-06
AXES = ("tm", "height", "width")
LANES = 128
LOW, HIGH = 2, 3
EDGE = 4


def rounds(axis):
    if lax.axis_size(axis) == 2:
        return 1
    return 3 if axis == "tm" else 2


def round_of(axis, low):
    if axis == "tm":
        return jnp.where(low % 2 == 1, 1, low % 4) if isinstance(low, jax.Array) else (1 if low % 2 else low % 4)
    return low % 2


def swap_pairs(axis, turn):
    sizes = [lax.axis_size(name) for name in AXES]
    place = AXES.index(axis)
    count = sizes[place]
    pairs = []
    for t in range(sizes[0]):
        for h in range(sizes[1]):
            for w in range(sizes[2]):
                source = [t, h, w]
                target = [t, h, w]
                mine = source[place]
                if mine + 1 < count and round_of(axis, mine) == turn:
                    target[place] = mine + 1
                elif mine > 0 and round_of(axis, mine - 1) == turn:
                    target[place] = mine - 1
                elif axis == "width":
                    target[place] = count - 1 - mine
                else:
                    target[2] = w ^ 1
                pairs.append(
                    tuple((p[0] * sizes[1] + p[1]) * sizes[2] + p[2] for p in (source, target))
                )
    return pairs


def swap(axis, outgoing):
    return [lax.ppermute(value, AXES, swap_pairs(axis, i)) for i, value in enumerate(outgoing)]


def outgoing(axis, count, to_next, to_prev):
    even = lax.axis_index(axis) % 2 == 0
    return [jnp.where(even, *pair) for pair in ((to_next, to_prev), (to_prev, to_next))[:count]]


def incoming(axis, values):
    index, count = lax.axis_index(axis), lax.axis_size(axis)
    even = index % 2 == 0
    at_even, at_odd = values[0], values[-1]
    zero = jnp.zeros_like(at_even)
    if len(values) == 1:
        return jnp.where(even, zero, at_even), jnp.where(even, at_even, zero)
    return (
        jnp.where(index == 0, zero, jnp.where(even, at_odd, at_even)),
        jnp.where(index == count - 1, zero, jnp.where(even, at_even, at_odd)),
    )


def rows_out(own, *refs):
    got, slabs, prev, wide = refs[: rounds("tm")], refs[rounds("tm") : -2], refs[-2], refs[-1]
    index = lax.axis_index("tm")
    prev[...] = jnp.zeros(prev.shape, prev.dtype)
    for i, ref in zip([0, 2, 1] if len(got) == 3 else range(len(got)), got):

        @pl.when((index > 0) & (round_of("tm", index - 1) == i))
        def _(ref=ref):
            prev[...] = ref[...]

    frames, rows = own.shape[0], own.shape[1]
    for i, slab in enumerate(slabs):
        for f in range(2 * frames):
            block = (prev if f < frames else own)[f % frames].astype(jnp.float32)
            part = outgoing("height", len(slabs), block[rows - HIGH :], block[:HIGH])[i]
            wide[f * HIGH : (f + 1) * HIGH, :] = part
        slab[...] = wide[...].astype(jnp.bfloat16)


def cols_out(width, own, prev, *refs):
    count = rounds("height")
    got, rim, slabs, (above, below) = refs[:count], refs[count], refs[-4:-2], refs[-2:]
    frames, rows, lanes = own.shape
    values = incoming("height", [ref[...].astype(jnp.float32) for ref in got])
    for k in range(lanes // LANES):
        tile = slice(k * LANES, (k + 1) * LANES)
        for ref, value in zip((above, below), values):
            ref[k, 0 : 2 * frames * HIGH, :] = value[:, tile]
        parts = [above[k, pl.ds(r, 2 * frames, stride=HIGH), :] for r in range(HIGH - LOW, HIGH)]
        parts += [below[k, pl.ds(r, 2 * frames, stride=HIGH), :] for r in range(HIGH)]
        parts.append(jnp.zeros((rim.shape[0] - len(parts) * 2 * frames, LANES), jnp.float32))
        rim[:, tile] = jnp.concatenate(parts, axis=0).astype(jnp.bfloat16)
    last = lanes - width
    for f in range(2 * frames):
        source = (prev if f < frames else own)[f % frames]
        for slab, part in zip(slabs, outgoing("width", 2, source[:, last:], source[:, :width])):
            slab[f * rows : (f + 1) * rows, :] = part
    for slab, part in zip(slabs, outgoing("width", 2, rim[:, last:], rim[:, :width])):
        slab[2 * frames * rows :, :] = part


def arrange(c1, x, gain1, gain2, shortcut, conv1, conv2, down, xv, g1, g2, wsc, w1, w2m, w2r, wdm, wdr, sems):
    c2 = g2.shape[1]
    rest = c2 - LANES
    copies = [
        pltpu.make_async_copy(x, xv, sems.at[0]),
        pltpu.make_async_copy(gain1, g1, sems.at[1]),
        pltpu.make_async_copy(gain2, g2, sems.at[2]),
        pltpu.make_async_copy(shortcut, wsc.at[pl.ds(0, c1)], sems.at[3]),
    ]
    for dc in range(3):
        moves = [
            (conv1.at[:, :, dc], w1.at[dc, :, :, pl.ds(0, c1)]),
            (conv2.at[:, :, dc, pl.ds(0, LANES)], w2m.at[dc]),
            (conv2.at[:, :, dc, pl.ds(LANES, rest)], w2r.at[dc, :, pl.ds(0, 3)]),
            (down.at[:, dc, pl.ds(0, LANES)], wdm.at[dc]),
            (down.at[:, dc, pl.ds(LANES, rest)], wdr.at[dc, pl.ds(0, 3)]),
        ]
        for i, (source, target) in enumerate(moves):
            copies.append(pltpu.make_async_copy(source, target, sems.at[4 + 5 * dc + i]))
    for copy in copies:
        copy.start()
    bf = jnp.bfloat16
    wsc[c1:] = jnp.zeros((LANES - c1, c2), bf)
    w1[:, :, :, c1:, :] = jnp.zeros((3, 3, 3, LANES - c1, c2), bf)
    w2r[:, :, 3] = jnp.zeros((3, 3, rest, c2), bf)
    wdr[:, 3] = jnp.zeros((3, rest, c2), bf)
    for copy in copies:
        copy.wait()


class Steps:
    def __init__(self, frames, rows, cols, c1, c2, w1, w2m, w2r, wsc, g1, g2):
        self.frames, self.rows, self.cols, self.c1, self.c2 = frames, rows, cols, c1, c2
        self.rest = c2 - LANES
        self.R = rows + LOW + HIGH
        self.M1 = up((frames + 1) * self.R + rows + 3, 16)
        self.M2 = up((frames - 1) * self.R + rows + 1, 16)
        self.pitch = rows + 2
        self.rim_rows = list(range(LOW)) + list(range(LOW + rows, LOW + rows + HIGH))
        self.w1, self.w2m, self.w2r, self.wsc = w1, w2m, w2r, wsc
        gap = jnp.zeros((1, LANES - c1), jnp.float32)
        self.gain1 = jnp.concatenate([g1[...], gap], axis=-1)
        self.gain2 = None if g2 is None else g2[...]
        t, h, w = [lax.axis_index(name) for name in AXES]
        starts, top, left = [i == 0 for i in (t, h, w)]
        bottom, right = [i == lax.axis_size(name) - 1 for i, name in ((h, "height"), (w, "width"))]
        p = lax.broadcasted_iota(jnp.int32, (self.M1, 1), 0)
        dead = (p < 2 * self.R) & starts
        for f in range(frames + 2):
            q = p - f * self.R
            dead |= ((q == 0) & top) | (((q == rows + 1) | (q == rows + 2)) & bottom)
        self.live1 = jnp.where(dead, 0.0, 1.0).astype(jnp.float32)
        p = lax.broadcasted_iota(jnp.int32, (self.M2, 1), 0)
        dead = p < 0
        for f in range(frames):
            dead |= (p == f * self.R + rows) & bottom
        self.live2 = jnp.where(dead, 0.0, 1.0).astype(jnp.float32)
        self.keep_left = jnp.where(left, 0.0, 1.0).astype(jnp.float32)
        self.keep_right = jnp.where(right, 0.0, 1.0).astype(jnp.float32)

    def spread(self):
        shape = (EDGE * self.c1, EDGE * LANES)
        source = lax.broadcasted_iota(jnp.int32, shape, 0)
        target = lax.broadcasted_iota(jnp.int32, shape, 1)
        slot, lane = target // LANES, target % LANES
        return jnp.where((source == slot * self.c1 + lane) & (lane < self.c1), 1.0, 0.0).astype(jnp.bfloat16)

    def unpack(self, x, spread, lo, hi):
        wide = jnp.dot(x, spread, preferred_element_type=jnp.float32)
        for k in range(lo, hi):
            v = wide[:, k * LANES : (k + 1) * LANES]
            ms = jnp.sum(v * v, axis=-1, keepdims=True) * (1.0 / self.c1)
            u = v * (0.5 * lax.rsqrt(ms + epsilon)) * self.gain1
            yield v, u + u * jnp.tanh(u)

    def place_own(self, c, v, u, first, raw):
        for f in range(2 * self.frames):
            chunk = slice(f * self.rows, (f + 1) * self.rows)
            at = f * self.R + LOW
            first[c, at : at + self.rows, :] = u[chunk]
            if f >= self.frames:
                at -= self.frames * self.R
                raw[c, at : at + self.rows, :] = v[chunk]

    def place_rim(self, c, u, first):
        n = 2 * self.frames
        for e, row in enumerate(self.rim_rows):
            value = jnp.zeros((n, LANES), jnp.float32) if u is None else u[e * n : (e + 1) * n]
            first[c, pl.ds(row, n, stride=self.R), :] = value

    def place_raw(self, c, v, raw):
        at = LOW * 2 * self.frames + self.frames
        raw[c, pl.ds(LOW + self.rows, self.frames, stride=self.R), :] = v[at : at + self.frames]

    def stack_first(self, c, first, stack, at=None):
        at = c if at is None else at
        for k in range(9):
            off = (k // 3) * self.R + k % 3
            stack[at, :, k * LANES : (k + 1) * LANES] = first[c, off : off + self.M1, :].astype(jnp.bfloat16)

    def conv_first(self, get, wanted):
        lhs = [jnp.concatenate([get(c + dc) for dc in range(3)], axis=-1) for c in wanted]
        return jnp.dot(
            jnp.concatenate(lhs, axis=0),
            self.w1[...].reshape(27 * LANES, self.c2),
            preferred_element_type=jnp.float32,
        )

    def conv_rim(self, get, wanted):
        n = 2 * self.frames
        sums = {}
        for dr in range(3):
            lhs = [jnp.concatenate([get(c + dc, dr) for dc in range(3)], axis=-1) for c in wanted[::2]]
            part = jnp.dot(
                jnp.concatenate(lhs, axis=0),
                self.w1[:, :, dr].reshape(9 * LANES, self.c2),
                preferred_element_type=jnp.float32,
            )
            tall = part.shape[0] // len(wanted)
            for block in range(3):
                row = self.rim_rows[dr + block] - dr
                for i in range(len(wanted)):
                    value = part[i * tall + block * n : i * tall + (block + 1) * n]
                    sums[i, row] = sums[i, row] + value if (i, row) in sums else value
        return sums

    def act_second(self, hid, keep):
        ms = jnp.sum(hid * hid, axis=-1, keepdims=True) * (1.0 / self.c2)
        scale = 0.5 * lax.rsqrt(ms + epsilon) * self.live1
        u = hid * (scale if keep is None else scale * keep) * self.gain2
        return u + u * jnp.tanh(u)

    def halves(self, c, value, low, high):
        count = value.shape[0]
        low[c, 0:count, :] = value[:, :LANES]
        high[c, 0:count, 0 : self.rest] = value[:, LANES:]
        high[c, 0 : count - 1, self.rest : 2 * self.rest] = value[1:, LANES:]

    def stack_second(self, c, low, high, stack):
        for k in range(9):
            off = (k // 3) * self.R + k % 3
            stack[c, :, k * LANES : (k + 1) * LANES] = low[c, off : off + self.M2, :].astype(jnp.bfloat16)
        for k in range(9, 15):
            off = (k - 9) // 2 * self.R + (k - 9) % 2 * 2
            stack[c, :, k * LANES : (k + 1) * LANES] = high[c, off : off + self.M2, :].astype(jnp.bfloat16)

    def conv_second(self, get, get_raw, wanted):
        mains = [[get(m + dc)[:, : 9 * LANES] for dc in range(3)] for m in wanted]
        rests = [[get(m + dc)[:, 9 * LANES :] for dc in range(3)] for m in wanted]
        lhs = [
            jnp.concatenate(main + rest + [get_raw(m + LOW).astype(jnp.bfloat16)], axis=-1)
            for m, main, rest in zip(wanted, mains, rests)
        ]
        rhs = [self.w2m[...].reshape(27 * LANES, self.c2), self.w2r[...].reshape(18 * LANES, self.c2)]
        return jnp.dot(
            jnp.concatenate(lhs, axis=0),
            jnp.concatenate(rhs + [self.wsc[...]], axis=0),
            preferred_element_type=jnp.float32,
        )

    def merged(self, c, value, keep, low, high):
        value = value * (self.live2 if keep is None else self.live2 * keep)
        n = self.rows + 1
        for f in range(self.frames):
            at = f * self.pitch
            chunk = value[f * self.R : f * self.R + n]
            low[c, at : at + n, :] = chunk[:, :LANES]
            high[c, at : at + n, 0 : self.rest] = chunk[:, LANES:]
            high[c, at : at + n - 1, self.rest : 2 * self.rest] = chunk[1:, LANES:]
            gap = jnp.zeros((1, self.rest), jnp.float32)
            high[c, at + n - 1 : at + n, self.rest : 2 * self.rest] = gap

    def down(self, lows, highs, wanted, stack, wdm, wdr, result):
        bf = jnp.bfloat16
        count = stack.shape[1]
        for j in wanted:
            for dc in range(3):
                ref, c = lows(2 * j + dc)
                for dr in range(3):
                    k = dc * 3 + dr
                    stack[j, :, k * LANES : (k + 1) * LANES] = ref[c, pl.ds(dr, count, stride=2), :].astype(bf)
                ref, c = highs(2 * j + dc)
                for half in range(2):
                    k = 9 + 2 * dc + half
                    part = ref[c, pl.ds(2 * half, count, stride=2), :]
                    stack[j, :, k * LANES : (k + 1) * LANES] = part.astype(bf)
        acc = jnp.dot(
            jnp.concatenate([stack[j] for j in wanted], axis=0),
            jnp.concatenate([wdm[...].reshape(9 * LANES, self.c2), wdr[...].reshape(6 * LANES, self.c2)], axis=0),
            preferred_element_type=jnp.float32,
        )
        for i, j in enumerate(wanted):
            result(j, acc[i * count : (i + 1) * count])


def early(dims, own, prev, g1, w1, first, raw, acc_a, acc_b, stack1):
    s = Steps(*dims, w1, None, None, None, g1, None)
    tail = 2 * s.frames * s.R
    first[:, tail:, :] = jnp.zeros((first.shape[0], first.shape[1] - tail, LANES), jnp.float32)
    spread = s.spread()
    for group in range(s.cols // EDGE):
        lanes = slice(group * EDGE * s.c1, (group + 1) * EDGE * s.c1)
        x = jnp.concatenate([prev[:, :, lanes], own[:, :, lanes]], axis=0)
        x = x.reshape(2 * s.frames * s.rows, EDGE * s.c1)
        for k, (v, u) in enumerate(s.unpack(x, spread, 0, EDGE)):
            c = group * EDGE + k
            s.place_own(c, v, u, first, raw)
            s.place_rim(c, None, first)
            s.stack_first(c, first, stack1)
    hidden = list(range(LOW, s.cols))
    step = 14
    for start in range(0, len(hidden), step):
        wanted = hidden[start : start + step]
        acc = s.conv_first(lambda c: stack1[c - LOW], wanted)
        for i, c in enumerate(wanted):
            acc_a[c - LOW, 0 : s.M1, :] = acc[i * s.M1 : (i + 1) * s.M1, :LANES]
            acc_b[c - LOW, 0 : s.M1, 0 : s.rest] = acc[i * s.M1 : (i + 1) * s.M1, LANES:]


def inner(
    dims, rim, w1, w2m, w2r, wsc, g1, g2, _first, _raw, _acc_a, _acc_b,
    first, raw, acc_a, acc_b, stack1, stack2, mer_a, mer_b, sec_a, sec_b, rims, stack_rim,
):
    s = Steps(*dims, w1, w2m, w2r, wsc, g1, g2)
    spread = s.spread()
    n = 2 * s.frames
    tall = rim.shape[0]
    rims[:, tall:, :] = jnp.zeros((s.cols, rims.shape[1] - tall, LANES), jnp.float32)
    edge = [0, 1, s.cols - 2, s.cols - 1]
    for group in range(s.cols // EDGE):
        x = rim[:, group * EDGE * s.c1 : (group + 1) * EDGE * s.c1]
        for k, (v, u) in enumerate(s.unpack(x, spread, 0, EDGE)):
            c = group * EDGE + k
            rims[c, 0:tall, :] = u
            s.place_raw(c, v, raw)
            if c in edge:
                s.place_rim(c, u, first)
    for c in range(s.cols - 1):
        for dr in range(3):
            for dt in range(3):
                rows = slice(dr * n + dt, dr * n + dt + 3 * n)
                part = jnp.concatenate([rims[c, rows, :], rims[c + 1, rows, :]], axis=0)
                stack_rim[c, dr, :, dt * LANES : (dt + 1) * LANES] = part.astype(jnp.bfloat16)
    hidden = list(range(LOW, s.cols))
    step = 6
    for start in range(0, len(hidden), step):
        wanted = hidden[start : start + step]
        gap = jnp.zeros((n, LANES - s.rest), jnp.float32)
        for (i, row), value in s.conv_rim(lambda c, dr: stack_rim[c - LOW, dr], wanted).items():
            c = wanted[i] - LOW
            acc_a[c, pl.ds(row, n, stride=s.R), :] += value[:, :LANES]
            acc_b[c, pl.ds(row, n, stride=s.R), :] += jnp.concatenate([value[:, LANES:], gap], axis=-1)
        for c in wanted:
            hid = jnp.concatenate([acc_a[c - LOW, 0 : s.M1, :], acc_b[c - LOW, 0 : s.M1, : s.rest]], axis=-1)
            s.halves(c - LOW, s.act_second(hid, None), sec_a, sec_b)
            s.stack_second(c - LOW, sec_a, sec_b, stack2)
    for i, c in enumerate(edge):
        s.stack_first(c, first, stack1, i)
    merged = list(range(LOW, s.cols - 2))
    step = 3
    for start in range(0, len(merged), step):
        wanted = merged[start : start + step]
        acc = s.conv_second(
            lambda c: stack2[c - LOW], lambda c: raw[c - LOW, LOW : LOW + s.M2, :], wanted
        )
        for i, c in enumerate(wanted):
            s.merged(c - LOW, acc[i * s.M2 : (i + 1) * s.M2], None, mer_a, mer_b)


def outer(
    dims, got_b, got_a, w1, w2m, w2r, wsc, g1, g2, wdm, wdr, in_raw, in_stack1, in_stack2, in_mer_a, in_mer_b,
    out, first, raw, stack1, sec_a, sec_b, stack2, mer_a, mer_b, stack3,
):
    s = Steps(*dims, w1, w2m, w2r, wsc, g1, g2)
    cols, M1, M2 = s.cols, s.M1, s.M2
    tail = 2 * s.frames * s.R
    first[:, tail:, :] = jnp.zeros((first.shape[0], first.shape[1] - tail, LANES), jnp.float32)
    spread = s.spread()
    left, right = incoming("width", [got_a[...], got_b[...]])
    for x, lo, hi, at in ((left, EDGE - LOW, EDGE, 0), (right, 0, HIGH, LOW)):
        for k, (v, u) in enumerate(s.unpack(x, spread, lo, hi)):
            own_rows = 2 * s.frames * s.rows
            s.place_own(at + k, v[:own_rows], u[:own_rows], first, raw)
            s.place_rim(at + k, u[own_rows:], first)
            s.place_raw(at + k, v[own_rows:], raw)
            s.stack_first(at + k, first, stack1)

    def new_or(own, given, lo, hi):
        return lambda c: given(c - lo) if lo <= c < hi else own(c if c < lo else c - hi + lo)

    def store(j, value):
        n = s.rows // 2
        for f in range(s.frames):
            at = f * s.pitch // 2
            out[f, :, j * s.c2 : (j + 1) * s.c2] = value[at : at + n].astype(jnp.bfloat16)

    lows = new_or(lambda i: (mer_a, i), lambda i: (in_mer_a, i), LOW, cols - 2)
    highs = new_or(lambda i: (mer_b, i), lambda i: (in_mer_b, i), LOW, cols - 2)
    out_cols = cols // 2
    get1 = new_or(lambda i: stack1[i], lambda i: in_stack1[i if i < 2 else i - cols + 4], LOW, LOW + cols)
    get2 = new_or(lambda i: stack2[i], lambda i: in_stack2[i], LOW, cols)
    get_raw = new_or(
        lambda i: raw[i, LOW : LOW + M2, :], lambda i: in_raw[i, LOW : LOW + M2, :], LOW, LOW + cols
    )
    sides = [
        ([0, 1], [s.keep_left, None], [0, 1], [None, None], 0),
        ([cols, cols + 1, cols + 2], [None] + [s.keep_right] * 2, [cols - 2, cols - 1, cols], [None, None, s.keep_right], 2),
    ]
    s.down(lows, highs, list(range(1, out_cols - 2)), stack3, wdm, wdr, store)
    accs = [s.conv_first(get1, side[0]) for side in sides]
    for acc, (wanted, keeps, _, _, at) in zip(accs, sides):
        for i, keep in enumerate(keeps):
            s.halves(at + i, s.act_second(acc[i * M1 : (i + 1) * M1], keep), sec_a, sec_b)
            s.stack_second(at + i, sec_a, sec_b, stack2)
    accs = [s.conv_second(get2, get_raw, side[2]) for side in sides]
    for acc, (_, _, wanted, keeps, at) in zip(accs, sides):
        for i, keep in enumerate(keeps):
            s.merged(at + i, acc[i * M2 : (i + 1) * M2], keep, mer_a, mer_b)
    s.down(lows, highs, [0, out_cols - 2, out_cols - 1], stack3, wdm, wdr, store)


def up(n, k):
    return -(-n // k) * k


def cost(flops):
    return pl.CostEstimate(flops=flops, bytes_accessed=5 * 10**6, transcendentals=10**5)


def local(video_in, gain_first, gain_second, conv_first, conv_second, shortcut, downscale_weight):
    frames, rows, merged_cols = video_in.shape
    c1, c2 = shortcut.shape
    cols = merged_cols // c1
    rest = c2 - LANES
    dims = (frames, rows, cols, c1, c2)
    bf, f32 = jnp.bfloat16, jnp.float32
    vmem = pl.BlockSpec(memory_space=pltpu.VMEM)
    hbm = pl.BlockSpec(memory_space=pltpu.HBM)
    params = pltpu.CompilerParams(vmem_limit_bytes=14 * 1024 * 1024)
    small = pltpu.CompilerParams(vmem_limit_bytes=4 * 1024 * 1024)
    out_cols = cols // 2
    R = rows + LOW + HIGH
    M1 = up((frames + 1) * R + rows + 3, 16)
    M2 = up((frames - 1) * R + rows + 1, 16)
    first_rows = up(max(M1 + 2 * R + 2, (2 * frames + 1) * R), 8)
    acc_rows = up((2 * frames + 1) * R, 8)
    raw_rows = up(max(M2 + LOW, (frames + 1) * R), 8)
    count = up((frames - 1) * (rows + 2) // 2 + rows // 2, 8)
    held = up(2 * count + 1, 8)

    source = [gain_first.reshape(1, c1), gain_second.reshape(1, c2), shortcut]
    source += [conv_first, conv_second, downscale_weight]
    own, g1, g2, wsc, w1, w2m, w2r, wdm, wdr = pl.pallas_call(
        functools.partial(arrange, c1),
        out_shape=[
            pltpu.VMEM(video_in.shape, bf),
            pltpu.VMEM((1, c1), f32),
            pltpu.VMEM((1, c2), f32),
            pltpu.VMEM((LANES, c2), bf),
            pltpu.VMEM((3, 3, 3, LANES, c2), bf),
            pltpu.VMEM((3, 3, 3, LANES, c2), bf),
            pltpu.VMEM((3, 3, 4, rest, c2), bf),
            pltpu.VMEM((3, 3, LANES, c2), bf),
            pltpu.VMEM((3, 4, rest, c2), bf),
        ],
        in_specs=[hbm] * 7,
        out_specs=[vmem] * 9,
        scratch_shapes=[pltpu.SemaphoreType.DMA((19,))],
        compiler_params=small,
        cost_estimate=cost(0),
        name="arrange",
    )(*[pltpu.with_memory_space_constraint(a, pltpu.HBM) for a in [video_in] + source])

    rim_tall = up((LOW + HIGH) * 2 * frames, 16)
    tall = 2 * frames * rows + rim_tall
    got = swap("tm", [video_in] * rounds("tm"))
    *slabs, prev = pl.pallas_call(
        rows_out,
        out_shape=[pltpu.VMEM((2 * frames * HIGH, merged_cols), bf)] * rounds("height")
        + [pltpu.VMEM(video_in.shape, bf)],
        in_specs=[vmem] * (1 + len(got)),
        out_specs=[vmem] * (1 + rounds("height")),
        scratch_shapes=[pltpu.VMEM((2 * frames * HIGH, merged_cols), f32)],
        compiler_params=small,
        cost_estimate=cost(0),
        name="rows_out",
    )(own, *[got[i] for i in ([0, 2, 1] if len(got) == 3 else range(len(got)))])
    got = swap("height", slabs)
    hid_in, mer_in = cols - 2, cols - 4
    worked = [
        pltpu.VMEM((cols, first_rows, LANES), f32),
        pltpu.VMEM((cols, raw_rows, LANES), f32),
        pltpu.VMEM((hid_in, acc_rows, LANES), f32),
        pltpu.VMEM((hid_in, acc_rows, LANES), f32),
    ]
    work = pl.pallas_call(
        functools.partial(early, dims),
        out_shape=worked,
        in_specs=[vmem] * 4,
        out_specs=[vmem] * 4,
        scratch_shapes=[pltpu.VMEM((cols, M1, 9 * LANES), bf)],
        compiler_params=params,
        cost_estimate=cost(10**9),
        name="early",
    )(own, prev, g1, w1)
    rim, *slabs = pl.pallas_call(
        functools.partial(cols_out, EDGE * c1),
        out_shape=[pltpu.VMEM((rim_tall, merged_cols), bf)] + [pltpu.VMEM((tall, EDGE * c1), bf)] * 2,
        in_specs=[vmem] * (2 + len(got)),
        out_specs=[vmem] * 3,
        scratch_shapes=[pltpu.VMEM((merged_cols // LANES, up((2 * frames + 1) * HIGH, 8), LANES), f32)] * 2,
        compiler_params=small,
        cost_estimate=cost(0),
        name="cols_out",
    )(own, prev, *got)
    got_a, got_b = swap("width", slabs)

    _, raw, _, _, *passed = pl.pallas_call(
        functools.partial(inner, dims),
        out_shape=worked
        + [
            pltpu.VMEM((4, M1, 9 * LANES), bf),
            pltpu.VMEM((hid_in, M2, 15 * LANES), bf),
            pltpu.VMEM((mer_in, held, LANES), f32),
            pltpu.VMEM((mer_in, held, LANES), f32),
        ],
        in_specs=[vmem] * 11,
        out_specs=[vmem] * 8,
        scratch_shapes=[
            pltpu.VMEM((hid_in, M1, LANES), f32),
            pltpu.VMEM((hid_in, M1, LANES), f32),
            pltpu.VMEM((cols, rim_tall + 8, LANES), f32),
            pltpu.VMEM((cols - 1, 3, 12 * frames, 3 * LANES), bf),
        ],
        input_output_aliases={7: 0, 8: 1, 9: 2, 10: 3},
        compiler_params=params,
        cost_estimate=cost(4 * 10**9),
        name="inner",
    )(rim, w1, w2m, w2r, wsc, g1, g2, *work)
    edge = LOW + HIGH
    return pl.pallas_call(
        functools.partial(outer, dims),
        out_shape=jax.ShapeDtypeStruct((frames, rows // 2, out_cols * c2), bf),
        in_specs=[vmem] * 15,
        out_specs=vmem,
        scratch_shapes=[
            pltpu.VMEM((edge, first_rows, LANES), f32),
            pltpu.VMEM((edge, raw_rows, LANES), f32),
            pltpu.VMEM((edge, M1, 9 * LANES), bf),
            pltpu.VMEM((edge, M1, LANES), f32),
            pltpu.VMEM((edge, M1, LANES), f32),
            pltpu.VMEM((edge, M2, 15 * LANES), bf),
            pltpu.VMEM((edge, held, LANES), f32),
            pltpu.VMEM((edge, held, LANES), f32),
            pltpu.VMEM((out_cols, count, 15 * LANES), bf),
        ],
        compiler_params=params,
        cost_estimate=cost(2 * 10**9),
        name="outer",
    )(got_b, got_a, w1, w2m, w2r, wsc, g1, g2, wdm, wdr, raw, *passed)


def solution(mesh):
    placed = (P("tm", "height", "width"), P(), P(), P(), P(), P(), P())
    return jax.shard_map(
        local, mesh=mesh, in_specs=placed, out_specs=P("tm", "height", "width"), check_vma=False
    )
```

```python
import functools
import jax
import jax.numpy as jnp
from jax import lax
from jax.experimental import pallas as pl
from jax.experimental.pallas import tpu as pltpu
from jax.sharding import PartitionSpec as P

epsilon = 1e-06
AXES = ("tm", "height", "width")
LANES = 128
LOW, HIGH = 2, 3
EDGE = 4


def rounds(axis):
    if lax.axis_size(axis) == 2:
        return 1
    return 3 if axis == "tm" else 2


def round_of(axis, low):
    if axis == "tm":
        return jnp.where(low % 2 == 1, 1, low % 4) if isinstance(low, jax.Array) else (1 if low % 2 else low % 4)
    return low % 2


def swap_pairs(axis, turn):
    sizes = [lax.axis_size(name) for name in AXES]
    place = AXES.index(axis)
    count = sizes[place]
    pairs = []
    for t in range(sizes[0]):
        for h in range(sizes[1]):
            for w in range(sizes[2]):
                source = [t, h, w]
                target = [t, h, w]
                mine = source[place]
                if mine + 1 < count and round_of(axis, mine) == turn:
                    target[place] = mine + 1
                elif mine > 0 and round_of(axis, mine - 1) == turn:
                    target[place] = mine - 1
                elif axis == "width":
                    target[place] = count - 1 - mine
                else:
                    target[2] = w ^ 1
                pairs.append(
                    tuple((p[0] * sizes[1] + p[1]) * sizes[2] + p[2] for p in (source, target))
                )
    return pairs


def swap(axis, outgoing):
    return [lax.ppermute(value, AXES, swap_pairs(axis, i)) for i, value in enumerate(outgoing)]


def outgoing(axis, count, to_next, to_prev):
    even = lax.axis_index(axis) % 2 == 0
    return [jnp.where(even, *pair) for pair in ((to_next, to_prev), (to_prev, to_next))[:count]]


def incoming(axis, values):
    index, count = lax.axis_index(axis), lax.axis_size(axis)
    even = index % 2 == 0
    at_even, at_odd = values[0], values[-1]
    zero = jnp.zeros_like(at_even)
    if len(values) == 1:
        return jnp.where(even, zero, at_even), jnp.where(even, at_even, zero)
    return (
        jnp.where(index == 0, zero, jnp.where(even, at_odd, at_even)),
        jnp.where(index == count - 1, zero, jnp.where(even, at_even, at_odd)),
    )


def rows_out(own, *refs):
    got, slabs, prev, wide = refs[: rounds("tm")], refs[rounds("tm") : -2], refs[-2], refs[-1]
    index = lax.axis_index("tm")
    prev[...] = jnp.zeros(prev.shape, prev.dtype)
    for i, ref in zip([0, 2, 1] if len(got) == 3 else range(len(got)), got):

        @pl.when((index > 0) & (round_of("tm", index - 1) == i))
        def _(ref=ref):
            prev[...] = ref[...]

    frames, rows = own.shape[0], own.shape[1]
    for i, slab in enumerate(slabs):
        for f in range(2 * frames):
            block = (prev if f < frames else own)[f % frames].astype(jnp.float32)
            part = outgoing("height", len(slabs), block[rows - HIGH :], block[:HIGH])[i]
            wide[f * HIGH : (f + 1) * HIGH, :] = part
        slab[...] = wide[...].astype(jnp.bfloat16)


def cols_out(width, own, prev, *refs):
    count = rounds("height")
    got, rim, slabs, (above, below) = refs[:count], refs[count], refs[-4:-2], refs[-2:]
    frames, rows, lanes = own.shape
    values = incoming("height", [ref[...].astype(jnp.float32) for ref in got])
    for k in range(lanes // LANES):
        tile = slice(k * LANES, (k + 1) * LANES)
        for ref, value in zip((above, below), values):
            ref[k, 0 : 2 * frames * HIGH, :] = value[:, tile]
        parts = [above[k, pl.ds(r, 2 * frames, stride=HIGH), :] for r in range(HIGH - LOW, HIGH)]
        parts += [below[k, pl.ds(r, 2 * frames, stride=HIGH), :] for r in range(HIGH)]
        parts.append(jnp.zeros((rim.shape[0] - len(parts) * 2 * frames, LANES), jnp.float32))
        rim[:, tile] = jnp.concatenate(parts, axis=0).astype(jnp.bfloat16)
    last = lanes - width
    for f in range(2 * frames):
        source = (prev if f < frames else own)[f % frames]
        for slab, part in zip(slabs, outgoing("width", 2, source[:, last:], source[:, :width])):
            slab[f * rows : (f + 1) * rows, :] = part
    for slab, part in zip(slabs, outgoing("width", 2, rim[:, last:], rim[:, :width])):
        slab[2 * frames * rows :, :] = part


def arrange(c1, x, gain1, gain2, shortcut, conv1, conv2, down, xv, g1, g2, wsc, w1, w2m, w2r, wdm, wdr, sems):
    c2 = g2.shape[1]
    rest = c2 - LANES
    copies = [
        pltpu.make_async_copy(x, xv, sems.at[0]),
        pltpu.make_async_copy(gain1, g1, sems.at[1]),
        pltpu.make_async_copy(gain2, g2, sems.at[2]),
        pltpu.make_async_copy(shortcut, wsc.at[pl.ds(0, c1)], sems.at[3]),
    ]
    for dc in range(3):
        moves = [
            (conv1.at[:, :, dc], w1.at[dc, :, :, pl.ds(0, c1)]),
            (conv2.at[:, :, dc, pl.ds(0, LANES)], w2m.at[dc]),
            (conv2.at[:, :, dc, pl.ds(LANES, rest)], w2r.at[dc, :, pl.ds(0, 3)]),
            (down.at[:, dc, pl.ds(0, LANES)], wdm.at[dc]),
            (down.at[:, dc, pl.ds(LANES, rest)], wdr.at[dc, pl.ds(0, 3)]),
        ]
        for i, (source, target) in enumerate(moves):
            copies.append(pltpu.make_async_copy(source, target, sems.at[4 + 5 * dc + i]))
    for copy in copies:
        copy.start()
    bf = jnp.bfloat16
    wsc[c1:] = jnp.zeros((LANES - c1, c2), bf)
    w1[:, :, :, c1:, :] = jnp.zeros((3, 3, 3, LANES - c1, c2), bf)
    w2r[:, :, 3] = jnp.zeros((3, 3, rest, c2), bf)
    wdr[:, 3] = jnp.zeros((3, rest, c2), bf)
    for copy in copies:
        copy.wait()


class Steps:
    def __init__(self, frames, rows, cols, c1, c2, w1, w2m, w2r, wsc, g1, g2):
        self.frames, self.rows, self.cols, self.c1, self.c2 = frames, rows, cols, c1, c2
        self.rest = c2 - LANES
        self.R = rows + LOW + HIGH
        self.M1 = up((frames + 1) * self.R + rows + 3, 16)
        self.M2 = up((frames - 1) * self.R + rows + 1, 16)
        self.pitch = rows + 2
        self.rim_rows = list(range(LOW)) + list(range(LOW + rows, LOW + rows + HIGH))
        self.w1, self.w2m, self.w2r, self.wsc = w1, w2m, w2r, wsc
        gap = jnp.zeros((1, LANES - c1), jnp.float32)
        self.gain1 = jnp.concatenate([g1[...], gap], axis=-1)
        self.gain2 = None if g2 is None else g2[...]
        t, h, w = [lax.axis_index(name) for name in AXES]
        starts, top, left = [i == 0 for i in (t, h, w)]
        bottom, right = [i == lax.axis_size(name) - 1 for i, name in ((h, "height"), (w, "width"))]
        p = lax.broadcasted_iota(jnp.int32, (self.M1, 1), 0)
        dead = (p < 2 * self.R) & starts
        for f in range(frames + 2):
            q = p - f * self.R
            dead |= ((q == 0) & top) | (((q == rows + 1) | (q == rows + 2)) & bottom)
        self.live1 = jnp.where(dead, 0.0, 1.0).astype(jnp.float32)
        p = lax.broadcasted_iota(jnp.int32, (self.M2, 1), 0)
        dead = p < 0
        for f in range(frames):
            dead |= (p == f * self.R + rows) & bottom
        self.live2 = jnp.where(dead, 0.0, 1.0).astype(jnp.float32)
        self.keep_left = jnp.where(left, 0.0, 1.0).astype(jnp.float32)
        self.keep_right = jnp.where(right, 0.0, 1.0).astype(jnp.float32)

    def spread(self):
        shape = (EDGE * self.c1, EDGE * LANES)
        source = lax.broadcasted_iota(jnp.int32, shape, 0)
        target = lax.broadcasted_iota(jnp.int32, shape, 1)
        slot, lane = target // LANES, target % LANES
        return jnp.where((source == slot * self.c1 + lane) & (lane < self.c1), 1.0, 0.0).astype(jnp.bfloat16)

    def unpack(self, x, spread, lo, hi):
        wide = jnp.dot(x, spread, preferred_element_type=jnp.float32)
        for k in range(lo, hi):
            v = wide[:, k * LANES : (k + 1) * LANES]
            ms = jnp.sum(v * v, axis=-1, keepdims=True) * (1.0 / self.c1)
            u = v * (0.5 * lax.rsqrt(ms + epsilon)) * self.gain1
            yield v, u + u * jnp.tanh(u)

    def place_own(self, c, v, u, first, raw):
        for f in range(2 * self.frames):
            chunk = slice(f * self.rows, (f + 1) * self.rows)
            at = f * self.R + LOW
            first[c, at : at + self.rows, :] = u[chunk]
            if f >= self.frames:
                at -= self.frames * self.R
                raw[c, at : at + self.rows, :] = v[chunk]

    def place_rim(self, c, u, first):
        n = 2 * self.frames
        for e, row in enumerate(self.rim_rows):
            value = jnp.zeros((n, LANES), jnp.float32) if u is None else u[e * n : (e + 1) * n]
            first[c, pl.ds(row, n, stride=self.R), :] = value

    def place_raw(self, c, v, raw):
        at = LOW * 2 * self.frames + self.frames
        raw[c, pl.ds(LOW + self.rows, self.frames, stride=self.R), :] = v[at : at + self.frames]

    def stack_first(self, c, first, stack, at=None):
        at = c if at is None else at
        for k in range(9):
            off = (k // 3) * self.R + k % 3
            stack[at, :, k * LANES : (k + 1) * LANES] = first[c, off : off + self.M1, :].astype(jnp.bfloat16)

    def conv_first(self, get, wanted):
        lhs = [jnp.concatenate([get(c + dc) for dc in range(3)], axis=-1) for c in wanted]
        return jnp.dot(
            jnp.concatenate(lhs, axis=0),
            self.w1[...].reshape(27 * LANES, self.c2),
            preferred_element_type=jnp.float32,
        )

    def conv_rim(self, get, wanted):
        n = 2 * self.frames
        sums = {}
        for dr in range(3):
            lhs = [jnp.concatenate([get(c + dc, dr) for dc in range(3)], axis=-1) for c in wanted[::2]]
            part = jnp.dot(
                jnp.concatenate(lhs, axis=0),
                self.w1[:, :, dr].reshape(9 * LANES, self.c2),
                preferred_element_type=jnp.float32,
            )
            tall = part.shape[0] // len(wanted)
            for block in range(3):
                row = self.rim_rows[dr + block] - dr
                for i in range(len(wanted)):
                    value = part[i * tall + block * n : i * tall + (block + 1) * n]
                    sums[i, row] = sums[i, row] + value if (i, row) in sums else value
        return sums

    def act_second(self, hid, keep):
        ms = jnp.sum(hid * hid, axis=-1, keepdims=True) * (1.0 / self.c2)
        scale = 0.5 * lax.rsqrt(ms + epsilon) * self.live1
        u = hid * (scale if keep is None else scale * keep) * self.gain2
        return u + u * jnp.tanh(u)

    def halves(self, c, value, low, high):
        count = value.shape[0]
        low[c, 0:count, :] = value[:, :LANES]
        high[c, 0:count, 0 : self.rest] = value[:, LANES:]
        high[c, 0 : count - 1, self.rest : 2 * self.rest] = value[1:, LANES:]

    def stack_second(self, c, low, high, stack):
        for k in range(9):
            off = (k // 3) * self.R + k % 3
            stack[c, :, k * LANES : (k + 1) * LANES] = low[c, off : off + self.M2, :].astype(jnp.bfloat16)
        for k in range(9, 15):
            off = (k - 9) // 2 * self.R + (k - 9) % 2 * 2
            stack[c, :, k * LANES : (k + 1) * LANES] = high[c, off : off + self.M2, :].astype(jnp.bfloat16)

    def conv_second(self, get, get_raw, wanted):
        mains = [[get(m + dc)[:, : 9 * LANES] for dc in range(3)] for m in wanted]
        rests = [[get(m + dc)[:, 9 * LANES :] for dc in range(3)] for m in wanted]
        lhs = [
            jnp.concatenate(main + rest + [get_raw(m + LOW).astype(jnp.bfloat16)], axis=-1)
            for m, main, rest in zip(wanted, mains, rests)
        ]
        rhs = [self.w2m[...].reshape(27 * LANES, self.c2), self.w2r[...].reshape(18 * LANES, self.c2)]
        return jnp.dot(
            jnp.concatenate(lhs, axis=0),
            jnp.concatenate(rhs + [self.wsc[...]], axis=0),
            preferred_element_type=jnp.float32,
        )

    def merged(self, c, value, keep, low, high):
        value = value * (self.live2 if keep is None else self.live2 * keep)
        n = self.rows + 1
        for f in range(self.frames):
            at = f * self.pitch
            chunk = value[f * self.R : f * self.R + n]
            low[c, at : at + n, :] = chunk[:, :LANES]
            high[c, at : at + n, 0 : self.rest] = chunk[:, LANES:]
            high[c, at : at + n - 1, self.rest : 2 * self.rest] = chunk[1:, LANES:]
            gap = jnp.zeros((1, self.rest), jnp.float32)
            high[c, at + n - 1 : at + n, self.rest : 2 * self.rest] = gap

    def down(self, lows, highs, wanted, stack, wdm, wdr, result):
        bf = jnp.bfloat16
        count = stack.shape[1]
        for j in wanted:
            for dc in range(3):
                ref, c = lows(2 * j + dc)
                for dr in range(3):
                    k = dc * 3 + dr
                    stack[j, :, k * LANES : (k + 1) * LANES] = ref[c, pl.ds(dr, count, stride=2), :].astype(bf)
                ref, c = highs(2 * j + dc)
                for half in range(2):
                    k = 9 + 2 * dc + half
                    part = ref[c, pl.ds(2 * half, count, stride=2), :]
                    stack[j, :, k * LANES : (k + 1) * LANES] = part.astype(bf)
        acc = jnp.dot(
            jnp.concatenate([stack[j] for j in wanted], axis=0),
            jnp.concatenate([wdm[...].reshape(9 * LANES, self.c2), wdr[...].reshape(6 * LANES, self.c2)], axis=0),
            preferred_element_type=jnp.float32,
        )
        for i, j in enumerate(wanted):
            result(j, acc[i * count : (i + 1) * count])


def early(dims, own, prev, g1, w1, first, raw, acc_a, acc_b, stack1):
    s = Steps(*dims, w1, None, None, None, g1, None)
    tail = 2 * s.frames * s.R
    first[:, tail:, :] = jnp.zeros((first.shape[0], first.shape[1] - tail, LANES), jnp.float32)
    spread = s.spread()
    for group in range(s.cols // EDGE):
        lanes = slice(group * EDGE * s.c1, (group + 1) * EDGE * s.c1)
        x = jnp.concatenate([prev[:, :, lanes], own[:, :, lanes]], axis=0)
        x = x.reshape(2 * s.frames * s.rows, EDGE * s.c1)
        for k, (v, u) in enumerate(s.unpack(x, spread, 0, EDGE)):
            c = group * EDGE + k
            s.place_own(c, v, u, first, raw)
            s.place_rim(c, None, first)
            s.stack_first(c, first, stack1)
    hidden = list(range(LOW, s.cols))
    step = 14
    for start in range(0, len(hidden), step):
        wanted = hidden[start : start + step]
        acc = s.conv_first(lambda c: stack1[c - LOW], wanted)
        for i, c in enumerate(wanted):
            acc_a[c - LOW, 0 : s.M1, :] = acc[i * s.M1 : (i + 1) * s.M1, :LANES]
            acc_b[c - LOW, 0 : s.M1, 0 : s.rest] = acc[i * s.M1 : (i + 1) * s.M1, LANES:]


def inner(
    dims, rim, w1, w2m, w2r, wsc, g1, g2, _first, _raw, _acc_a, _acc_b,
    first, raw, acc_a, acc_b, stack1, stack2, mer_a, mer_b, sec_a, sec_b, rims, stack_rim,
):
    s = Steps(*dims, w1, w2m, w2r, wsc, g1, g2)
    spread = s.spread()
    n = 2 * s.frames
    tall = rim.shape[0]
    rims[:, tall:, :] = jnp.zeros((s.cols, rims.shape[1] - tall, LANES), jnp.float32)
    edge = [0, 1, s.cols - 2, s.cols - 1]
    for group in range(s.cols // EDGE):
        x = rim[:, group * EDGE * s.c1 : (group + 1) * EDGE * s.c1]
        for k, (v, u) in enumerate(s.unpack(x, spread, 0, EDGE)):
            c = group * EDGE + k
            rims[c, 0:tall, :] = u
            s.place_raw(c, v, raw)
            if c in edge:
                s.place_rim(c, u, first)
    for c in range(s.cols - 1):
        for dr in range(3):
            for dt in range(3):
                rows = slice(dr * n + dt, dr * n + dt + 3 * n)
                part = jnp.concatenate([rims[c, rows, :], rims[c + 1, rows, :]], axis=0)
                stack_rim[c, dr, :, dt * LANES : (dt + 1) * LANES] = part.astype(jnp.bfloat16)
    hidden = list(range(LOW, s.cols))
    step = 6
    for start in range(0, len(hidden), step):
        wanted = hidden[start : start + step]
        gap = jnp.zeros((n, LANES - s.rest), jnp.float32)
        for (i, row), value in s.conv_rim(lambda c, dr: stack_rim[c - LOW, dr], wanted).items():
            c = wanted[i] - LOW
            acc_a[c, pl.ds(row, n, stride=s.R), :] += value[:, :LANES]
            acc_b[c, pl.ds(row, n, stride=s.R), :] += jnp.concatenate([value[:, LANES:], gap], axis=-1)
        for c in wanted:
            hid = jnp.concatenate([acc_a[c - LOW, 0 : s.M1, :], acc_b[c - LOW, 0 : s.M1, : s.rest]], axis=-1)
            s.halves(c - LOW, s.act_second(hid, None), sec_a, sec_b)
            s.stack_second(c - LOW, sec_a, sec_b, stack2)
    for i, c in enumerate(edge):
        s.stack_first(c, first, stack1, i)
    merged = list(range(LOW, s.cols - 2))
    step = 4
    for start in range(0, len(merged), step):
        wanted = merged[start : start + step]
        acc = s.conv_second(
            lambda c: stack2[c - LOW], lambda c: raw[c - LOW, LOW : LOW + s.M2, :], wanted
        )
        for i, c in enumerate(wanted):
            s.merged(c - LOW, acc[i * s.M2 : (i + 1) * s.M2], None, mer_a, mer_b)


def outer(
    dims, got_b, got_a, w1, w2m, w2r, wsc, g1, g2, wdm, wdr, in_raw, in_stack1, in_stack2, in_mer_a, in_mer_b,
    out, first, raw, stack1, sec_a, sec_b, stack2, mer_a, mer_b, stack3,
):
    s = Steps(*dims, w1, w2m, w2r, wsc, g1, g2)
    cols, M1, M2 = s.cols, s.M1, s.M2
    tail = 2 * s.frames * s.R
    first[:, tail:, :] = jnp.zeros((first.shape[0], first.shape[1] - tail, LANES), jnp.float32)
    spread = s.spread()
    left, right = incoming("width", [got_a[...], got_b[...]])
    for x, lo, hi, at in ((left, EDGE - LOW, EDGE, 0), (right, 0, HIGH, LOW)):
        for k, (v, u) in enumerate(s.unpack(x, spread, lo, hi)):
            own_rows = 2 * s.frames * s.rows
            s.place_own(at + k, v[:own_rows], u[:own_rows], first, raw)
            s.place_rim(at + k, u[own_rows:], first)
            s.place_raw(at + k, v[own_rows:], raw)
            s.stack_first(at + k, first, stack1)

    def new_or(own, given, lo, hi):
        return lambda c: given(c - lo) if lo <= c < hi else own(c if c < lo else c - hi + lo)

    def store(j, value):
        n = s.rows // 2
        for f in range(s.frames):
            at = f * s.pitch // 2
            out[f, :, j * s.c2 : (j + 1) * s.c2] = value[at : at + n].astype(jnp.bfloat16)

    lows = new_or(lambda i: (mer_a, i), lambda i: (in_mer_a, i), LOW, cols - 2)
    highs = new_or(lambda i: (mer_b, i), lambda i: (in_mer_b, i), LOW, cols - 2)
    out_cols = cols // 2
    get1 = new_or(lambda i: stack1[i], lambda i: in_stack1[i if i < 2 else i - cols + 4], LOW, LOW + cols)
    get2 = new_or(lambda i: stack2[i], lambda i: in_stack2[i], LOW, cols)
    get_raw = new_or(
        lambda i: raw[i, LOW : LOW + M2, :], lambda i: in_raw[i, LOW : LOW + M2, :], LOW, LOW + cols
    )
    sides = [
        ([0, 1], [s.keep_left, None], [0, 1], [None, None], 0),
        ([cols, cols + 1, cols + 2], [None] + [s.keep_right] * 2, [cols - 2, cols - 1, cols], [None, None, s.keep_right], 2),
    ]
    s.down(lows, highs, list(range(1, out_cols - 2)), stack3, wdm, wdr, store)
    accs = [s.conv_first(get1, side[0]) for side in sides]
    for acc, (wanted, keeps, _, _, at) in zip(accs, sides):
        for i, keep in enumerate(keeps):
            s.halves(at + i, s.act_second(acc[i * M1 : (i + 1) * M1], keep), sec_a, sec_b)
            s.stack_second(at + i, sec_a, sec_b, stack2)
    accs = [s.conv_second(get2, get_raw, side[2]) for side in sides]
    for acc, (_, _, wanted, keeps, at) in zip(accs, sides):
        for i, keep in enumerate(keeps):
            s.merged(at + i, acc[i * M2 : (i + 1) * M2], keep, mer_a, mer_b)
    s.down(lows, highs, [0, out_cols - 2, out_cols - 1], stack3, wdm, wdr, store)


def up(n, k):
    return -(-n // k) * k


def cost(flops):
    return pl.CostEstimate(flops=flops, bytes_accessed=5 * 10**6, transcendentals=10**5)


def local(video_in, gain_first, gain_second, conv_first, conv_second, shortcut, downscale_weight):
    frames, rows, merged_cols = video_in.shape
    c1, c2 = shortcut.shape
    cols = merged_cols // c1
    rest = c2 - LANES
    dims = (frames, rows, cols, c1, c2)
    bf, f32 = jnp.bfloat16, jnp.float32
    vmem = pl.BlockSpec(memory_space=pltpu.VMEM)
    hbm = pl.BlockSpec(memory_space=pltpu.HBM)
    params = pltpu.CompilerParams(vmem_limit_bytes=14 * 1024 * 1024)
    small = pltpu.CompilerParams(vmem_limit_bytes=4 * 1024 * 1024)
    out_cols = cols // 2
    R = rows + LOW + HIGH
    M1 = up((frames + 1) * R + rows + 3, 16)
    M2 = up((frames - 1) * R + rows + 1, 16)
    first_rows = up(max(M1 + 2 * R + 2, (2 * frames + 1) * R), 8)
    acc_rows = up((2 * frames + 1) * R, 8)
    raw_rows = up(max(M2 + LOW, (frames + 1) * R), 8)
    count = up((frames - 1) * (rows + 2) // 2 + rows // 2, 8)
    held = up(2 * count + 1, 8)

    source = [gain_first.reshape(1, c1), gain_second.reshape(1, c2), shortcut]
    source += [conv_first, conv_second, downscale_weight]
    own, g1, g2, wsc, w1, w2m, w2r, wdm, wdr = pl.pallas_call(
        functools.partial(arrange, c1),
        out_shape=[
            pltpu.VMEM(video_in.shape, bf),
            pltpu.VMEM((1, c1), f32),
            pltpu.VMEM((1, c2), f32),
            pltpu.VMEM((LANES, c2), bf),
            pltpu.VMEM((3, 3, 3, LANES, c2), bf),
            pltpu.VMEM((3, 3, 3, LANES, c2), bf),
            pltpu.VMEM((3, 3, 4, rest, c2), bf),
            pltpu.VMEM((3, 3, LANES, c2), bf),
            pltpu.VMEM((3, 4, rest, c2), bf),
        ],
        in_specs=[hbm] * 7,
        out_specs=[vmem] * 9,
        scratch_shapes=[pltpu.SemaphoreType.DMA((19,))],
        compiler_params=small,
        cost_estimate=cost(0),
        name="arrange",
    )(*[pltpu.with_memory_space_constraint(a, pltpu.HBM) for a in [video_in] + source])

    rim_tall = up((LOW + HIGH) * 2 * frames, 16)
    tall = 2 * frames * rows + rim_tall
    got = swap("tm", [video_in] * rounds("tm"))
    *slabs, prev = pl.pallas_call(
        rows_out,
        out_shape=[pltpu.VMEM((2 * frames * HIGH, merged_cols), bf)] * rounds("height")
        + [pltpu.VMEM(video_in.shape, bf)],
        in_specs=[vmem] * (1 + len(got)),
        out_specs=[vmem] * (1 + rounds("height")),
        scratch_shapes=[pltpu.VMEM((2 * frames * HIGH, merged_cols), f32)],
        compiler_params=small,
        cost_estimate=cost(0),
        name="rows_out",
    )(own, *[got[i] for i in ([0, 2, 1] if len(got) == 3 else range(len(got)))])
    got = swap("height", slabs)
    hid_in, mer_in = cols - 2, cols - 4
    worked = [
        pltpu.VMEM((cols, first_rows, LANES), f32),
        pltpu.VMEM((cols, raw_rows, LANES), f32),
        pltpu.VMEM((hid_in, acc_rows, LANES), f32),
        pltpu.VMEM((hid_in, acc_rows, LANES), f32),
    ]
    work = pl.pallas_call(
        functools.partial(early, dims),
        out_shape=worked,
        in_specs=[vmem] * 4,
        out_specs=[vmem] * 4,
        scratch_shapes=[pltpu.VMEM((cols, M1, 9 * LANES), bf)],
        compiler_params=params,
        cost_estimate=cost(10**9),
        name="early",
    )(own, prev, g1, w1)
    rim, *slabs = pl.pallas_call(
        functools.partial(cols_out, EDGE * c1),
        out_shape=[pltpu.VMEM((rim_tall, merged_cols), bf)] + [pltpu.VMEM((tall, EDGE * c1), bf)] * 2,
        in_specs=[vmem] * (2 + len(got)),
        out_specs=[vmem] * 3,
        scratch_shapes=[pltpu.VMEM((merged_cols // LANES, up((2 * frames + 1) * HIGH, 8), LANES), f32)] * 2,
        compiler_params=small,
        cost_estimate=cost(0),
        name="cols_out",
    )(own, prev, *got)
    got_a, got_b = swap("width", slabs)

    _, raw, _, _, *passed = pl.pallas_call(
        functools.partial(inner, dims),
        out_shape=worked
        + [
            pltpu.VMEM((4, M1, 9 * LANES), bf),
            pltpu.VMEM((hid_in, M2, 15 * LANES), bf),
            pltpu.VMEM((mer_in, held, LANES), f32),
            pltpu.VMEM((mer_in, held, LANES), f32),
        ],
        in_specs=[vmem] * 11,
        out_specs=[vmem] * 8,
        scratch_shapes=[
            pltpu.VMEM((hid_in, M1, LANES), f32),
            pltpu.VMEM((hid_in, M1, LANES), f32),
            pltpu.VMEM((cols, rim_tall + 8, LANES), f32),
            pltpu.VMEM((cols - 1, 3, 12 * frames, 3 * LANES), bf),
        ],
        input_output_aliases={7: 0, 8: 1, 9: 2, 10: 3},
        compiler_params=params,
        cost_estimate=cost(4 * 10**9),
        name="inner",
    )(rim, w1, w2m, w2r, wsc, g1, g2, *work)
    edge = LOW + HIGH
    return pl.pallas_call(
        functools.partial(outer, dims),
        out_shape=jax.ShapeDtypeStruct((frames, rows // 2, out_cols * c2), bf),
        in_specs=[vmem] * 15,
        out_specs=vmem,
        scratch_shapes=[
            pltpu.VMEM((edge, first_rows, LANES), f32),
            pltpu.VMEM((edge, raw_rows, LANES), f32),
            pltpu.VMEM((edge, M1, 9 * LANES), bf),
            pltpu.VMEM((edge, M1, LANES), f32),
            pltpu.VMEM((edge, M1, LANES), f32),
            pltpu.VMEM((edge, M2, 15 * LANES), bf),
            pltpu.VMEM((edge, held, LANES), f32),
            pltpu.VMEM((edge, held, LANES), f32),
            pltpu.VMEM((out_cols, count, 15 * LANES), bf),
        ],
        compiler_params=params,
        cost_estimate=cost(2 * 10**9),
        name="outer",
    )(got_b, got_a, w1, w2m, w2r, wsc, g1, g2, wdm, wdr, raw, *passed)


def solution(mesh):
    placed = (P("tm", "height", "width"), P(), P(), P(), P(), P(), P())
    return jax.shard_map(
        local, mesh=mesh, in_specs=placed, out_specs=P("tm", "height", "width"), check_vma=False
    )
```
